32 devices in a mesh: batch: 8 (over z, x), seq: 4 (over y, core).
Axes of the slice: x: 2, y: 2, z: 4, core: 2. Of those that a mesh axis runs over, the one named last changes fastest.
Arguments:
- tokens: bfloat16 [8, 6144, 512], P('batch', 'seq'), may hold values from -6 to 6
- qkv_weight: bfloat16 [3, 512, 512], P(None, 'batch', 'seq'), may hold values from -0.25 to 0.25
- out_proj: bfloat16 [512, 512], P('batch', 'seq'), may hold values from -6 to 6
- in_weight: bfloat16 [512, 2048], P('batch', 'seq'), may hold values from -0.25 to 0.25
- out_weight: bfloat16 [2048, 512], P('seq', 'batch'), may hold values from -0.125 to 0.125
- norm_params: bfloat16 [4, 512], P('seq', 'batch')
- rand_features: bfloat16 [8, 64, 256], replicated, may hold values from -6 to 6
- long_start: int32 [8], P('batch'), may hold values from 256 to 768
- masked_pos: int32 [8, 1536], P('batch', 'seq'), may hold values from 0 to 1535, as said below
- masked_count: int32 [8, 4], P('batch', 'seq'), may hold values from 76 to 384, as said below
- masked_grad: bfloat16 [8, 1536, 512], P('batch', 'seq'), may hold values from -6 to 6
Outputs:
- mixed: bfloat16 [8, 6144, 512], P('batch', 'seq')
- tokens_grad: float32 [8, 6144, 512], P('batch', 'seq')
- qkv_grad: float32 [3, 512, 512], P(None, 'batch', 'seq')
- out_proj_grad: float32 [512, 512], P('batch', 'seq')
- in_grad: float32 [512, 2048], P('batch', 'seq')
- out_grad: float32 [2048, 512], P('seq', 'batch')
- norm_grad: float32 [4, 512], P('seq', 'batch')
The draws below stay inside these ranges and needn't reach their ends.
Inputs may be any that keep to these rules, and one draw needn't show every extreme that they name: `masked_pos`: within each block of 384 slots the positions are distinct. `masked_count`: some block is full in every draw. `long_start`: each group holds one sequence of 5120 tokens starting here, one sequence before it and one after it.
All inputs are finite; a program needn't handle non-finite values.
Results may differ from the reference program's by a relative error of at most 0.03.
Values may be sent and summed in bfloat16 or wider, within the bound.
A program may use at most 192 MiB of HBM per device.

```python
import jax
import jax.numpy as jnp
from jax import lax

D = 512
H = 8
DH = 64
M = 256
FF = 2048
TOK_DEV = 1536
SHORT = 1024
BLOCKS = 4
GROUPS = 8
SEQ_TOK = 6144
MASK_DEV = 384
MASK_LO = 76
SLOTS = 1536
LONG = 5120


def draw_norm_params(key, part):
    key = jax.random.fold_in(key, 37)
    normal_draw = jax.random.normal(key, (4, D), jnp.float32)
    offsets = jnp.array([1.0, 0.0, 1.0, 0.0], jnp.float32)
    spreads = jnp.array([0.25, 0.5, 0.25, 0.5], jnp.float32)
    return (offsets[:, None] + spreads[:, None] * normal_draw).astype(jnp.bfloat16)


def draw_masked_pos(key, part):
    key = jax.random.fold_in(key, 11)
    key_list = jax.random.split(key, GROUPS * BLOCKS)
    picked = jax.vmap(lambda one_key: jax.random.permutation(one_key, TOK_DEV)[:MASK_DEV])(key_list)
    return picked.reshape(GROUPS, BLOCKS * MASK_DEV).astype(jnp.int32)


def draw_masked_count(key, part):
    key = jax.random.fold_in(key, 23)
    draw_key, second = jax.random.split(key)
    counts = jax.random.randint(draw_key, (GROUPS * BLOCKS,), MASK_LO, MASK_DEV + 1)
    chosen = jax.random.randint(second, (), 0, GROUPS * BLOCKS)
    flattened = jnp.where(jnp.arange(GROUPS * BLOCKS) == chosen, MASK_DEV, counts)
    return flattened.reshape(GROUPS, BLOCKS).astype(jnp.int32)


def set_ends(result, own_key, least, top_value):
    shape = result.shape
    index_at = [jax.random.randint(jax.random.fold_in(own_key, axis), (), 0, shape[axis]) for axis in range(len(shape))]
    result = result.at[tuple(index_at)].set(least)
    longest = shape.index(max(shape))
    index_at[longest] = (index_at[longest] + 1) % shape[longest]
    return result.at[tuple(index_at)].set(top_value)


def block_scale(stream_key, dims, cuts, low, largest):
    gain = 1.0
    for axis_at, shards_of in cuts:
        draws = jax.random.uniform(jax.random.fold_in(jax.random.fold_in(stream_key, 6), axis_at), (shards_of,), jnp.float32, low / len(cuts), largest / len(cuts))
        gain = gain * jnp.repeat(jnp.exp(draws), dims[axis_at] // shards_of).reshape((-1,) + (1,) * (len(dims) - 1 - axis_at))
    return gain


def normal_values(key, extent, deviation, bound, pieces=(), held_as=jnp.bfloat16):
    drawn = jax.random.normal(key, extent, jnp.float32) * deviation
    if len(pieces) > 0:
        drawn = block_scale(key, extent, pieces, -0.22, 0.18) * drawn
    return jnp.clip(drawn, min=-bound, max=bound).astype(held_as)


def setup_inputs(seed: int = 0) -> dict:
    arg_keys = jax.random.split(jax.random.key(seed), 12)
    tokens = normal_values(arg_keys[0], (GROUPS, SEQ_TOK, D), 1.0, 6.0, ((0, 8), (1, 4)))
    qkv_weight = normal_values(arg_keys[1], (3, D, D), D ** -0.5, 0.25, ((1, 8), (2, 4)))
    out_proj = normal_values(arg_keys[2], (D, D), (max(1, 3 * D // LONG)) ** -0.5, 6.0, ((0, 8), (1, 4)))
    in_weight = normal_values(arg_keys[3], (D, FF), D ** -0.5, 0.25, ((0, 8), (1, 4)))
    out_weight = normal_values(arg_keys[4], (FF, D), FF ** -0.5, 0.125, ((0, 4), (1, 8)))
    norm_params = draw_norm_params(jax.random.fold_in(arg_keys[11], 71), 0)
    rand_features = normal_values(arg_keys[6], (H, DH, M), 1.0, 6.0)
    long_start = set_ends(jax.random.randint(arg_keys[7], (GROUPS,), SHORT // 4, 3 * SHORT // 4 + 1), jax.random.fold_in(arg_keys[7], 1), SHORT // 4, (3 * SHORT // 4 + 1) - 1).astype(jnp.int32)
    masked_pos = draw_masked_pos(jax.random.fold_in(arg_keys[11], 71), 0)
    masked_count = draw_masked_count(jax.random.fold_in(arg_keys[11], 71), 0)
    masked_grad = normal_values(arg_keys[10], (GROUPS, SLOTS, D), 1.0, 6.0, ((0, 8), (1, 4)))
    return dict(tokens=tokens, qkv_weight=qkv_weight, out_proj=out_proj, in_weight=in_weight, out_weight=out_weight, norm_params=norm_params, rand_features=rand_features, long_start=long_start, masked_pos=masked_pos, masked_count=masked_count, masked_grad=masked_grad)


EPS = 1e-05
FULL_PRECISION = lax.Precision.HIGHEST

@jax.custom_vjp
def low(v):
    return lax.optimization_barrier(v.astype(jnp.bfloat16)).astype(jnp.float32)

@jax.custom_vjp
def low_back(v):
    return v

def low_keep(v):
    return (low(v), None)

def low_pass(kept, grad):
    return (grad,)

def back_keep(v):
    return (v, None)

def back_low(kept, grad):
    return (low(grad),)
low.defvjp(low_keep, low_pass)
low_back.defvjp(back_keep, back_low)

def layer_norm_parts(values, gain_row, shift_row):
    row_mean = lax.optimization_barrier(jnp.mean(values, axis=-1, keepdims=True))
    centred = values - row_mean
    row_var = lax.optimization_barrier(jnp.mean(centred * centred, axis=-1, keepdims=True))
    inverse = lax.rsqrt(row_var + EPS)
    unit_rows = centred * inverse
    return (unit_rows * gain_row + shift_row, unit_rows, inverse)

def positive_features(values, feature_dirs):
    feat_scale = DH ** (-0.25)
    projected = low_back(feat_scale * jnp.einsum('rhd,hdm->rhm', values, feature_dirs, precision=FULL_PRECISION))
    sq_norm = lax.optimization_barrier(jnp.sum(values * values, axis=-1, keepdims=True))
    return jnp.exp(projected - 0.5 * feat_scale * feat_scale * sq_norm) * M ** (-0.5)

def forward(tokens_wide, qkv_wide, out_wide, in_wide, down_wide, norm_wide, feature_dirs, long_from):
    row_count = tokens_wide.shape[0]
    position = jnp.arange(row_count, dtype=jnp.int32)
    segment = (position >= long_from).astype(jnp.int32) + (position >= long_from + LONG).astype(jnp.int32)
    segment_member = (segment[:, None] == jnp.arange(3, dtype=jnp.int32)[None, :]).astype(jnp.float32)
    normed = low(layer_norm_parts(tokens_wide, norm_wide[0], norm_wide[1])[0])

    def project(weight_mat):
        return low(low_back(jnp.dot(normed, weight_mat, precision=FULL_PRECISION))).reshape(row_count, H, DH)
    query = project(qkv_wide[0])
    key_vecs = project(qkv_wide[1])
    value_vectors = project(qkv_wide[2])
    query_feature_map = low(positive_features(query, feature_dirs))
    key_feature_map = low(positive_features(key_vecs, feature_dirs))
    state_summary = low(low_back(jnp.einsum('thm,ts,thd->shmd', key_feature_map, segment_member, value_vectors, precision=FULL_PRECISION)))
    total = low(jnp.einsum('thm,ts->shm', key_feature_map, segment_member, precision=FULL_PRECISION))
    numerator = jnp.zeros((row_count, H, DH), jnp.float32)
    denom = jnp.zeros((row_count, H), jnp.float32)
    for segment_label in range(3):
        numerator = numerator + segment_member[:, segment_label, None, None] * jnp.einsum('pox,oxa->poa', query_feature_map, state_summary[segment_label], precision=FULL_PRECISION)
        denom = denom + segment_member[:, segment_label, None] * jnp.einsum('thm,hm->th', query_feature_map, total[segment_label], precision=FULL_PRECISION)
    numerator = low_back(numerator)
    denom = low_back(denom)
    heads_out = low((numerator / denom[:, :, None]).reshape(row_count, D))
    middle = tokens_wide + low_back(jnp.dot(heads_out, out_wide, precision=FULL_PRECISION))
    normed_two = low(layer_norm_parts(middle, norm_wide[2], norm_wide[3])[0])
    upper = low_back(jnp.dot(normed_two, in_wide, precision=FULL_PRECISION))
    activated = low(jax.nn.gelu(upper, approximate=False))
    return middle + low_back(jnp.dot(activated, down_wide, precision=FULL_PRECISION))

def reference(tokens, qkv_weight, out_proj, in_weight, out_weight, norm_params, rand_features, long_start, masked_pos, masked_count, masked_grad):
    weights = (qkv_weight.astype(jnp.float32), out_proj.astype(jnp.float32), in_weight.astype(jnp.float32), out_weight.astype(jnp.float32), norm_params.astype(jnp.float32))
    feature_dirs = rand_features.astype(jnp.float32)
    slot_ids = jnp.arange(SLOTS, dtype=jnp.int32)
    block_of = (slot_ids // MASK_DEV).astype(jnp.int32)

    def one_group(grad_sum, inputs):
        group_rows, long_from, group_pos, count_row, group_cot = inputs
        target = (group_pos + block_of * TOK_DEV).astype(jnp.int32)
        in_use = (slot_ids % MASK_DEV < count_row[block_of]).astype(jnp.float32)
        dense_cot = jnp.zeros((SEQ_TOK, D), jnp.float32).at[target].add(group_cot.astype(jnp.float32) * in_use[:, None])

        def run(token_rows, *weight_list):
            return forward(token_rows, *weight_list, feature_dirs, long_from)
        group_out, pullback = jax.vjp(run, group_rows.astype(jnp.float32), *weights)
        pulled = pullback(dense_cot)
        grad_sum = tuple((acc + new for acc, new in zip(grad_sum, pulled[1:])))
        return (grad_sum, (group_out.astype(jnp.bfloat16), pulled[0]))
    zero_grads = tuple((jnp.zeros(w_item.shape, jnp.float32) for w_item in weights))
    grad_sum, (mixed_rows, token_grads) = lax.scan(one_group, zero_grads, (tokens, long_start, masked_pos, masked_count, masked_grad))
    return (mixed_rows, token_grads, grad_sum[0], grad_sum[1], grad_sum[2], grad_sum[3], grad_sum[4])
```

```python
import functools

import jax
import jax.numpy as jnp
from jax import lax
from jax.experimental import pallas as pl
from jax.experimental.pallas import tpu as pltpu
from jax.sharding import PartitionSpec as P

SHORT = 1024


EPS = 1e-05


def layer_norm_parts(values, gain_row, shift_row):
    row_mean = jnp.mean(values, axis=-1, keepdims=True)
    centred = values - row_mean
    row_var = jnp.mean(centred * centred, axis=-1, keepdims=True)
    inverse = lax.rsqrt(row_var + EPS)
    unit_rows = centred * inverse
    return (unit_rows * gain_row + shift_row, unit_rows, inverse)


def layer_norm_back(incoming, unit_rows, inverse, gain_row):
    scaled = incoming * gain_row
    inner = (
        scaled
        - jnp.mean(scaled, axis=-1, keepdims=True)
        - unit_rows * jnp.mean(scaled * unit_rows, axis=-1, keepdims=True)
    )
    return (inner * inverse, jnp.sum(incoming * unit_rows, axis=0), jnp.sum(incoming, axis=0))


def exact_gelu(values):
    return jax.nn.gelu(values, approximate=False)


def positive_raw(values, feature_dirs):
    feat_scale = values.shape[-1] ** (-0.25)
    projected = feat_scale * jnp.einsum(
        "rhd,hdm->rhm", values, feature_dirs, preferred_element_type=jnp.float32
    )
    values_wide = values.astype(jnp.float32)
    sq_norm = jnp.sum(values_wide * values_wide, axis=-1, keepdims=True)
    return jnp.exp(projected - 0.5 * feat_scale * feat_scale * sq_norm) * feature_dirs.shape[
        -1
    ] ** (-0.5)


def positive_back(feat_grad, raw_feat, values, feature_dirs):
    feat_scale = values.shape[-1] ** (-0.25)
    exponent_grad = feat_grad * raw_feat
    direct = feat_scale * jnp.einsum(
        "rhm,hdm->rhd",
        exponent_grad.astype(jnp.bfloat16),
        feature_dirs,
        preferred_element_type=jnp.float32,
    )
    values_wide = values.astype(jnp.float32)
    norm_part = (
        feat_scale * feat_scale * values_wide * jnp.sum(exponent_grad, axis=-1, keepdims=True)
    )
    return (direct - norm_part).astype(jnp.bfloat16)


def place_two(first_sel, second_sel, first_val, second_val):
    shape_tail = (1,) * first_val.ndim
    return (
        first_sel.reshape((3,) + shape_tail) * first_val[None]
        + second_sel.reshape((3,) + shape_tail) * second_val[None]
    )


def pick_one(stacked, which):
    return lax.dynamic_index_in_dim(stacked, which, 0, keepdims=False)


def on_device(
    tokens,
    qkv_weight,
    out_proj,
    in_weight,
    out_weight,
    norm_params,
    rand_features,
    long_start,
    masked_pos,
    masked_count,
    masked_grad,
):
    low_type = jnp.bfloat16
    wider_number_type = jnp.float32
    part_qkv, part_out, part_in, part_down, part_norm = (
        lax.all_gather(qkv_weight, "seq", axis=2, tiled=True),
        lax.all_gather(out_proj, "seq", axis=1, tiled=True),
        lax.all_gather(in_weight, "seq", axis=1, tiled=True),
        lax.all_gather(out_weight, "seq", axis=0, tiled=True),
        lax.all_gather(norm_params, "seq", axis=0, tiled=True),
    )
    w_qkv, w_out, w_in, w_down, norm_low = (
        lax.all_gather(part_qkv, "batch", axis=1, tiled=True),
        lax.all_gather(part_out, "batch", axis=0, tiled=True),
        lax.all_gather(part_in, "batch", axis=0, tiled=True),
        lax.all_gather(part_down, "batch", axis=1, tiled=True),
        lax.all_gather(part_norm, "batch", axis=1, tiled=True),
    )
    norm_wide = norm_low.astype(wider_number_type)
    row_count = tokens.shape[1]
    model_width = tokens.shape[2]
    head_count = rand_features.shape[0]
    head_size = rand_features.shape[1]
    seq_index = lax.axis_index("seq")
    seq_last = lax.axis_size("seq") - 1
    position = seq_index * row_count + jnp.arange(row_count, dtype=jnp.int32)
    long_from = long_start[0]
    long_span = lax.axis_size("seq") * row_count - SHORT
    segment = (position >= long_from).astype(jnp.int32) + (
        position >= long_from + long_span
    ).astype(jnp.int32)
    seg_lower = jnp.where(seq_index == 0, 0, 1).astype(jnp.int32)
    seg_upper = jnp.where(seq_index == seq_last, 2, 1).astype(jnp.int32)
    member_upper = ((segment == seg_upper) & (seg_upper != seg_lower)).astype(wider_number_type)
    member_lower = 1.0 - member_upper
    sel_lower = (jnp.arange(3, dtype=jnp.int32) == seg_lower).astype(wider_number_type)
    sel_upper = (jnp.arange(3, dtype=jnp.int32) == seg_upper).astype(wider_number_type) * (
        seg_upper != seg_lower
    ).astype(wider_number_type)
    tokens_wide = tokens[0].astype(wider_number_type)
    normed_wide, unit_one, inverse_one = layer_norm_parts(tokens_wide, norm_wide[0], norm_wide[1])
    normed = normed_wide.astype(low_type)
    query = (
        jnp.dot(normed, w_qkv[0], preferred_element_type=wider_number_type)
        .astype(low_type)
        .reshape(row_count, head_count, head_size)
    )
    key_vecs = (
        jnp.dot(normed, w_qkv[1], preferred_element_type=wider_number_type)
        .astype(low_type)
        .reshape(row_count, head_count, head_size)
    )
    value_vectors = (
        jnp.dot(normed, w_qkv[2], preferred_element_type=wider_number_type)
        .astype(low_type)
        .reshape(row_count, head_count, head_size)
    )
    key_raw = positive_raw(key_vecs, rand_features)
    key_feature_map = key_raw.astype(low_type)
    query_feature_map = positive_raw(query, rand_features).astype(low_type)
    key_bottom_rows = key_feature_map * member_lower.astype(low_type)[:, None, None]
    key_top_rows = key_feature_map * member_upper.astype(low_type)[:, None, None]
    summary_lower = jnp.einsum(
        "jkn,jkp->knp", key_bottom_rows, value_vectors, preferred_element_type=wider_number_type
    )
    summary_upper = jnp.einsum(
        "jkn,jkp->knp", key_top_rows, value_vectors, preferred_element_type=wider_number_type
    )
    total_lower = jnp.einsum(
        "thm,t->hm",
        key_feature_map,
        member_lower.astype(low_type),
        preferred_element_type=wider_number_type,
    )
    total_upper = jnp.einsum(
        "thm,t->hm",
        key_feature_map,
        member_upper.astype(low_type),
        preferred_element_type=wider_number_type,
    )
    summary_part = place_two(sel_lower, sel_upper, summary_lower, summary_upper)
    total_part = place_two(sel_lower, sel_upper, total_lower, total_upper)
    state_summary, total = lax.psum((summary_part, total_part), "seq")
    summary_low = state_summary.astype(low_type)
    total_low = total.astype(low_type)
    sum_bottom_half = pick_one(summary_low, seg_lower)
    sum_top_half = pick_one(summary_low, seg_upper)
    tot_lo = pick_one(total_low, seg_lower)
    tot_hi = pick_one(total_low, seg_upper)
    numerator = member_lower[:, None, None] * jnp.einsum(
        "pox,oxa->poa", query_feature_map, sum_bottom_half, preferred_element_type=wider_number_type
    )
    numerator = numerator + member_upper[:, None, None] * jnp.einsum(
        "pox,oxa->poa", query_feature_map, sum_top_half, preferred_element_type=wider_number_type
    )
    denom = member_lower[:, None] * jnp.einsum(
        "thm,hm->th", query_feature_map, tot_lo, preferred_element_type=wider_number_type
    )
    denom = denom + member_upper[:, None] * jnp.einsum(
        "thm,hm->th", query_feature_map, tot_hi, preferred_element_type=wider_number_type
    )
    heads_out = (numerator / denom[:, :, None]).reshape(row_count, model_width).astype(low_type)
    middle = tokens_wide + jnp.dot(heads_out, w_out, preferred_element_type=wider_number_type)
    normed_two = layer_norm_parts(middle, norm_wide[2], norm_wide[3])[0].astype(low_type)
    upper = jnp.dot(normed_two, w_in, preferred_element_type=wider_number_type)
    activated = exact_gelu(upper).astype(low_type)
    result = (middle + jnp.dot(activated, w_down, preferred_element_type=wider_number_type)).astype(
        low_type
    )
    back_qkv, back_out, back_in, back_down = (w_qkv, w_out, w_in, w_down)
    picked = masked_pos[0]
    in_use = (jnp.arange(picked.shape[0], dtype=jnp.int32) < masked_count[0, 0]).astype(
        wider_number_type
    )
    cot_rows = masked_grad[0].astype(wider_number_type) * in_use[:, None]
    cot_low = cot_rows.astype(low_type)
    middle_rows = middle[picked]
    normed_rows_wide, unit_two, inverse_two = layer_norm_parts(
        middle_rows, norm_wide[2], norm_wide[3]
    )
    normed_rows = normed_rows_wide.astype(low_type)
    upper_rows = jnp.dot(normed_rows, back_in, preferred_element_type=wider_number_type)
    act_rows = exact_gelu(upper_rows).astype(low_type)
    act_grad = jnp.dot(cot_low, back_down.T, preferred_element_type=wider_number_type)
    upper_grad = jax.vjp(exact_gelu, upper_rows)[1](act_grad)[0].astype(low_type)
    grad_in = jnp.einsum(
        "rd,rf->df", normed_rows, upper_grad, preferred_element_type=wider_number_type
    )
    grad_down = jnp.einsum("rf,rd->fd", act_rows, cot_low, preferred_element_type=wider_number_type)
    normed_grad_two = jnp.dot(upper_grad, back_in.T, preferred_element_type=wider_number_type)
    middle_ln, gain_two_grad, bias_two_grad = layer_norm_back(
        normed_grad_two, unit_two, inverse_two, norm_wide[2]
    )
    middle_grad = cot_rows + middle_ln
    attn_grad = middle_grad.astype(low_type)
    grad_out = jnp.einsum(
        "rd,re->de", heads_out[picked], attn_grad, preferred_element_type=wider_number_type
    )
    heads_grad = jnp.dot(attn_grad, back_out.T, preferred_element_type=wider_number_type).reshape(
        -1, head_count, head_size
    )
    query_rows = query[picked]
    query_raw_rows = positive_raw(query_rows, rand_features)
    query_feat_rows = query_feature_map[picked]
    lower_rows = member_lower[picked]
    upper_rows_mask = member_upper[picked]
    numer_rows = numerator[picked]
    denom_rows = denom[picked]
    numerator_gradient = (heads_grad / denom_rows[:, :, None]).astype(low_type)
    denom_grad = (-jnp.sum(heads_grad * numer_rows, axis=-1) / (denom_rows * denom_rows)).astype(
        low_type
    )
    lower_rows_low = lower_rows.astype(low_type)
    upper_rows_low = upper_rows_mask.astype(low_type)
    sgrad_lower = jnp.einsum(
        "wpb,wpq->pbq",
        query_feat_rows,
        numerator_gradient * lower_rows_low[:, None, None],
        preferred_element_type=wider_number_type,
    )
    sgrad_upper = jnp.einsum(
        "wpb,wpq->pbq",
        query_feat_rows,
        numerator_gradient * upper_rows_low[:, None, None],
        preferred_element_type=wider_number_type,
    )
    tgrad_lower = jnp.einsum(
        "rhm,rh->hm",
        query_feat_rows,
        denom_grad * lower_rows_low[:, None],
        preferred_element_type=wider_number_type,
    )
    tgrad_upper = jnp.einsum(
        "rhm,rh->hm",
        query_feat_rows,
        denom_grad * upper_rows_low[:, None],
        preferred_element_type=wider_number_type,
    )
    summary_grad_part = place_two(sel_lower, sel_upper, sgrad_lower, sgrad_upper)
    total_grad_part = place_two(sel_lower, sel_upper, tgrad_lower, tgrad_upper)
    summary_grad, total_grad = (
        lax.psum(summary_grad_part.astype(jnp.bfloat16), "seq").astype(jnp.float32),
        lax.psum(total_grad_part.astype(jnp.bfloat16), "seq").astype(jnp.float32),
    )
    summary_grad_low = summary_grad.astype(low_type)
    segment_grad_bottom = pick_one(summary_grad_low, seg_lower)
    segment_grad_top = pick_one(summary_grad_low, seg_upper)
    tg_lo = pick_one(total_grad, seg_lower)
    tg_hi = pick_one(total_grad, seg_upper)
    denom_grad_wide = denom_grad.astype(wider_number_type)
    query_lower = (
        jnp.einsum(
            "sci,cni->scn",
            numerator_gradient,
            sum_bottom_half,
            preferred_element_type=wider_number_type,
        )
        + denom_grad_wide[:, :, None] * tot_lo.astype(wider_number_type)[None]
    )
    query_upper = (
        jnp.einsum(
            "sci,cni->scn",
            numerator_gradient,
            sum_top_half,
            preferred_element_type=wider_number_type,
        )
        + denom_grad_wide[:, :, None] * tot_hi.astype(wider_number_type)[None]
    )
    query_feat_grad = (
        lower_rows[:, None, None] * query_lower + upper_rows_mask[:, None, None] * query_upper
    )
    key_lower_grad = (
        jnp.einsum(
            "zqy,qiy->zqi",
            value_vectors,
            segment_grad_bottom,
            preferred_element_type=wider_number_type,
        )
        + tg_lo[None]
    )
    key_upper_grad = (
        jnp.einsum(
            "zqy,qiy->zqi",
            value_vectors,
            segment_grad_top,
            preferred_element_type=wider_number_type,
        )
        + tg_hi[None]
    )
    key_feat_grad = (
        member_lower[:, None, None] * key_lower_grad + member_upper[:, None, None] * key_upper_grad
    )
    value_grad = member_lower[:, None, None] * jnp.einsum(
        "pox,oxa->poa",
        key_feature_map,
        segment_grad_bottom,
        preferred_element_type=wider_number_type,
    )
    value_grad = value_grad + member_upper[:, None, None] * jnp.einsum(
        "pox,oxa->poa", key_feature_map, segment_grad_top, preferred_element_type=wider_number_type
    )
    query_grad = positive_back(query_feat_grad, query_raw_rows, query_rows, rand_features).reshape(
        -1, model_width
    )
    key_grad = positive_back(key_feat_grad, key_raw, key_vecs, rand_features).reshape(
        row_count, model_width
    )
    value_low = value_grad.astype(low_type).reshape(row_count, model_width)
    grad_query_w = jnp.einsum(
        "rd,re->de", normed[picked], query_grad, preferred_element_type=wider_number_type
    )
    grad_key_w = jnp.einsum("td,te->de", normed, key_grad, preferred_element_type=wider_number_type)
    grad_value_w = jnp.einsum(
        "td,te->de", normed, value_low, preferred_element_type=wider_number_type
    )
    query_back = jnp.dot(query_grad, back_qkv[0].T, preferred_element_type=wider_number_type)
    normed_grad_one = jnp.dot(
        key_grad, back_qkv[1].T, preferred_element_type=wider_number_type
    ) + jnp.dot(value_low, back_qkv[2].T, preferred_element_type=wider_number_type)
    normed_grad_one = normed_grad_one.at[picked].add(query_back)
    token_ln, gain_one_grad, bias_one_grad = layer_norm_back(
        normed_grad_one, unit_one, inverse_one, norm_wide[0]
    )
    tokens_grad = token_ln.at[picked].add(middle_grad)
    grad_qkv = jnp.stack([grad_query_w, grad_key_w, grad_value_w])
    grad_norm = jnp.stack([gain_one_grad, bias_one_grad, gain_two_grad, bias_two_grad])
    first_qkv, first_out, first_in, first_down, first_norm = (
        lax.psum_scatter(grad_qkv, "batch", scatter_dimension=1, tiled=True),
        lax.psum_scatter(grad_out, "batch", scatter_dimension=0, tiled=True),
        lax.psum_scatter(grad_in, "batch", scatter_dimension=0, tiled=True),
        lax.psum_scatter(grad_down, "batch", scatter_dimension=1, tiled=True),
        lax.psum_scatter(grad_norm, "batch", scatter_dimension=1, tiled=True),
    )
    owned = (
        lax.psum_scatter(
            first_qkv.astype(jnp.bfloat16), "seq", scatter_dimension=2, tiled=True
        ).astype(jnp.float32),
        lax.psum_scatter(
            first_out.astype(jnp.bfloat16), "seq", scatter_dimension=1, tiled=True
        ).astype(jnp.float32),
        lax.psum_scatter(
            first_in.astype(jnp.bfloat16), "seq", scatter_dimension=1, tiled=True
        ).astype(jnp.float32),
        lax.psum_scatter(
            first_down.astype(jnp.bfloat16), "seq", scatter_dimension=0, tiled=True
        ).astype(jnp.float32),
        lax.psum_scatter(
            first_norm.astype(jnp.bfloat16), "seq", scatter_dimension=0, tiled=True
        ).astype(jnp.float32),
    )
    return (result[None], tokens_grad[None], owned[0], owned[1], owned[2], owned[3], owned[4])


MESH = pl.DeviceIdType.MESH
LOW = jnp.bfloat16
WIDE = jnp.float32
LOG2E = 1.4426950408889634
ROOT_HALF = 0.7071067811865476
PDF_SCALE = 0.3989422804014327
PAD = 16


def dot_over(a, b, ca, cb):
    return lax.dot_general(a, b, (((ca,), (cb,)), ((), ())), preferred_element_type=WIDE)


def nn(a, b):
    return dot_over(a, b, 1, 0)


def nt(a, b):
    return dot_over(a, b, 1, 1)


def turn(a):
    if a.dtype == LOW:
        return a.astype(WIDE).T.astype(LOW)
    return a.T


def flat(a):
    return a.reshape(-1, a.shape[-1])


def unit_norm(x):
    cen = x - jnp.mean(x, axis=-1, keepdims=True)
    inv = lax.rsqrt(jnp.mean(cen * cen, axis=-1, keepdims=True) + EPS)
    return cen * inv, inv


def norm_back(incoming, unit, inv, gain):
    e = incoming * gain
    mean_e = jnp.mean(e, axis=-1, keepdims=True)
    mean_eu = jnp.mean(e * unit, axis=-1, keepdims=True)
    return inv * (e - mean_e - unit * mean_eu)


def features(proj, u_low, scale, feat):
    wide = u_low.astype(WIDE)
    sq = jnp.sum(wide * wide, axis=0, keepdims=True)
    shift = (0.5 * scale * scale * LOG2E) * sq
    half_log = 0.5 * (feat.bit_length() - 1)
    return jnp.exp2((scale * LOG2E) * proj - (shift + half_log))


class Wires:
    def __init__(self, send_sems, recv_sems):
        self.send_sems, self.recv_sems, self.used, self.sent = send_sems, recv_sems, 0, []

    def send(self, src, dst, dev):
        c = pltpu.make_async_remote_copy(
            src_ref=src,
            dst_ref=dst,
            send_sem=self.send_sems.at[self.used],
            recv_sem=self.recv_sems.at[self.used],
            device_id=dev,
            device_id_type=MESH,
        )
        self.used += 1
        c.start()
        self.sent.append(c)
        return c

    def left(self, copies):
        for c in copies:
            c.wait_send()
            self.sent = [o for o in self.sent if o is not c]

    def drain(self):
        self.left(list(self.sent))


def arrived(copies):
    for c in copies:
        c.wait_recv()


def layer_kernel(
    nz,
    ns,
    tok,
    wqkv_in,
    wo_in,
    win_in,
    wdn_in,
    nrm_in,
    rf,
    ls,
    pos,
    cnt,
    mg,
    mixed_out,
    tgrad_out,
    gqkv,
    gop,
    gin,
    gdn,
    gnorm,
    w0,
    w1,
    w2,
    nb,
    wkvt,
    wqt,
    wo,
    xnt,
    kvt,
    vs,
    kft,
    pm,
    pt,
    posc,
    rft,
    sumf,
    loc,
    ar_a,
    ar_r1,
    ar_r2,
    ar_f,
    dsumt,
    qrt,
    qfr,
    num_r,
    den_r,
    dn_st,
    hot,
    hort,
    dmid_low,
    xnrt,
    dqt,
    dhd,
    dxqt,
    gkv,
    gqo,
    g1,
    g2,
    rc_kv,
    rc_qo,
    rc1,
    rc2,
    ra_kv,
    ra_qo,
    ra1,
    ra2,
    rb_kv,
    rb_qo,
    rb1,
    rb2,
    rz_kv,
    rz_qo,
    rz1,
    rz2,
    ng_a,
    ng_r,
    mixed_v,
    tgrad_v,
    send_sems,
    recv_sems,
    out_sems,
):
    rows, width = tok.shape
    slots = mg.shape[0]
    heads, size, feat = rf.shape
    scale = size**-0.25
    bd = w0.shape[3]
    sw = wqkv_in.shape[2]
    fw = w1.shape[4]
    tile = 256
    wide_tile = 512
    b = lax.axis_index("batch")
    s = lax.axis_index("seq")
    x = lax.rem(b, 2)
    z = b // 2
    c = lax.rem(s, 2)
    y = s // 2
    to_core = (b, s + 1 - 2 * c)
    to_y = (b, s + 2 - 4 * y)
    to_x = (b + 1 - 2 * x, s)
    to_z = [(lax.rem(z + k, nz) * 2 + x, s) for k in range(1, nz)]
    s_core = s + 1 - 2 * c
    s_y = s + 2 - 4 * y
    wires = Wires(send_sems, recv_sems)

    w0[s, z, x, :, 0:sw] = wqkv_in[1]
    w0[s, z, x, :, sw : 2 * sw] = wqkv_in[2]
    w0[s, z, x, :, 2 * sw : 3 * sw] = wqkv_in[0]
    w0[s, z, x, :, 3 * sw : 4 * sw] = wo_in[...]
    w1[s, z, x] = win_in[...]
    w2[s, z, x] = turn(wdn_in[...])
    place = (
        lax.broadcasted_iota(jnp.int32, (bd, 2 * bd), 1)
        == lax.broadcasted_iota(jnp.int32, (bd, 2 * bd), 0) + bd * x
    )
    nb[s, z, x] = nn(
        jnp.broadcast_to(nrm_in[...], (PAD, bd)), jnp.where(place, 1.0, 0.0).astype(LOW)
    ).astype(LOW)

    barrier = pltpu.get_barrier_semaphore()
    partners = [to_core, to_y, to_x] + to_z
    for dev in partners:
        pl.semaphore_signal(barrier, inc=1, device_id=dev, device_id_type=MESH)
    pl.semaphore_wait(barrier, len(partners))

    def spread_z(ref):
        return [wires.send(ref.at[s, z, x], ref.at[s, z, x], dev) for dev in to_z]

    def spread_z_half(ref, lo, hi):
        at = ref.at[s, z, x, :, lo:hi]
        return [wires.send(at, at, dev) for dev in to_z]

    n_z = spread_z(nb)
    kv_z = spread_z_half(w0, 0, 2 * sw)

    seq_pos = s * rows
    long_from = ls[0, 0]
    long_to = long_from + ns * rows - SHORT

    def shared_mask(position):
        at = position + seq_pos
        return jnp.where((at >= long_from) & (at < long_to), 1.0, 0.0)

    pos_row = pos[...]
    posc[...] = jnp.broadcast_to(pos_row.astype(WIDE), (128, slots)).T
    sh_r = shared_mask(pos_row)

    def select_tile(t, carry):
        at = pl.multiple_of(t * tile, tile)
        row_id = lax.broadcasted_iota(jnp.int32, (tile, slots), 0) + at
        pt[pl.ds(at, tile), :] = jnp.where(row_id == pos_row, 1.0, 0.0).astype(LOW)
        for j in range(tile // 128):
            lane = lax.broadcasted_iota(jnp.int32, (slots, 128), 1) + (at + 128 * j)
            pm[:, pl.ds(at + 128 * j, 128)] = jnp.where(
                lane.astype(WIDE) == posc[...], 1.0, 0.0
            ).astype(LOW)
        lane = lax.broadcasted_iota(jnp.int32, (1, tile), 1) + at
        sh = shared_mask(lane)
        row = lax.broadcasted_iota(jnp.int32, (PAD, tile), 0)
        ones = jnp.where(row == 0, sh, jnp.where(row == 1, 1.0 - sh, 0.0)).astype(LOW)
        for h in range(heads):
            vs[h, 2 * size : 2 * size + PAD, pl.ds(at, tile)] = ones
        return carry

    lax.fori_loop(0, rows // tile, select_tile, 0)
    for h in range(heads):
        rft[h] = turn(rf[h])

    arrived(n_z)
    at = nb.at[s, :, x]
    n_x = [wires.send(at, at, to_x)]
    toks_r = nn(pm[...], tok[...])
    arrived(n_x)
    at = nb.at[s]
    n_y = [wires.send(at, at, to_y)]
    unit_r, _ = unit_norm(toks_r)
    arrived(n_y)
    n_c = []
    for side in (s, s_y):
        at = nb.at[side]
        n_c.append(wires.send(at, at, to_core))
    arrived(kv_z)
    at = w0.at[s, :, x, :, 0 : 2 * sw]
    kv_x = [wires.send(at, at, to_x)]
    qo_z = spread_z_half(w0, 2 * sw, 4 * sw)
    arrived(n_c)

    def norm_row(i):
        return jnp.concatenate(
            [
                (nb[i, j, 0, 0:1, :] + nb[i, j, 1, 0:1, :]).astype(WIDE)
                for j in range(nz)
            ],
            axis=1,
        )

    gain1, bias1, gain2, bias2 = [norm_row(i) for i in range(4)]
    xn_r = (unit_r * gain1 + bias1).astype(LOW)
    xnrt[...] = turn(xn_r)

    def norm_tile(t, carry):
        at = pl.multiple_of(t * tile, tile)
        unit, _ = unit_norm(tok[pl.ds(at, tile), :].astype(WIDE))
        xnt[:, pl.ds(at, tile)] = turn((unit * gain1 + bias1).astype(LOW))
        return carry

    lax.fori_loop(0, rows // tile, norm_tile, 0)

    arrived(kv_x)
    at = w0.at[s, :, :, :, 0 : 2 * sw]
    kv_y = [wires.send(at, at, to_y)]
    kv_c = [wires.send(at, at, to_core)]
    w1_z = spread_z(w1)

    def kv_block(sd):
        wkvt[sd] = turn(flat(w0[sd, :, :, :, 0 : 2 * sw]))

        def step(t, carry):
            at = pl.multiple_of(t * wide_tile, wide_tile)
            cols = pl.ds(at, wide_tile)
            r = nn(wkvt[sd], xnt[:, cols]).astype(LOW)
            kvt[sd, :, cols] = r
            lane = lax.broadcasted_iota(jnp.int32, (1, wide_tile), 1) + at
            sh = shared_mask(lane).astype(LOW)
            for i in range(2):
                h = 2 * sd + i
                k_h = r[size * i : size * (i + 1)]
                v_h = r[sw + size * i : sw + size * (i + 1)]
                kft[h, :, cols] = features(nn(rft[h], k_h), k_h, scale, feat).astype(LOW)
                vs[h, 0:size, cols] = v_h * sh
                vs[h, size : 2 * size, cols] = v_h * (1.0 - sh)
            return carry

        lax.fori_loop(0, rows // wide_tile, step, 0)
        for i in range(2):
            h = 2 * sd + i
            part = nt(vs[h], kft[h]).astype(LOW)
            ar_a[sd, i, 0:size, :] = part[0:size]
            ar_a[sd, i, size : size + PAD, :] = part[2 * size :]
            loc[h] = part[size:]

    arrived(kv_c)

    def kv_first(j, carry):
        kv_block(s + j * (s_core - s))
        return carry

    lax.fori_loop(0, 2, kv_first, 0)

    arrived(qo_z)
    at = w0.at[s, :, x, :, 2 * sw : 4 * sw]
    qo_x = [wires.send(at, at, to_x)]
    arrived(kv_y)
    at = w0.at[s_y, :, :, :, 0 : 2 * sw]
    kv_c2 = [wires.send(at, at, to_core)]
    arrived(w1_z)
    w2_z = spread_z(w2)
    at = w1.at[s, :, x]
    w1_x = [wires.send(at, at, to_x)]
    arrived(kv_c2)

    def kv_second(j, carry):
        base = s_y
        kv_block(base + j * (s_core - s))
        return carry

    lax.fori_loop(0, 2, kv_second, 0)

    def reduce_first(buf, r1):
        return [
            wires.send(buf.at[2 * yy + 1 - c], r1.at[yy], to_core) for yy in range(2)
        ]

    def reduce_second(buf, r1, r2, f, copies):
        arrived(copies)
        wires.left(copies)
        for yy in range(2):
            mine = 2 * yy + c
            buf[mine] = (buf[mine].astype(WIDE) + r1[yy].astype(WIDE)).astype(LOW)
        return [wires.send(buf.at[2 * yy + c], r2.at[yy], to_y) for yy in range(2)]

    def reduce_third(buf, r1, r2, f, copies):
        arrived(copies)
        wires.left(copies)
        for yy in range(2):
            mine = 2 * yy + c
            f[mine] = (buf[mine].astype(WIDE) + r2[yy].astype(WIDE)).astype(LOW)
        return [wires.send(f.at[2 * yy + c], f.at[2 * yy + c], to_core) for yy in range(2)]

    ar1 = reduce_first(ar_a, ar_r1.at[0])
    arrived(qo_x)
    at = w0.at[s, :, :, :, 2 * sw : 4 * sw]
    qo_c = [wires.send(at, at, to_core)]
    qo_y = [wires.send(at, at, to_y)]
    ar1 = reduce_second(ar_a, ar_r1.at[0], ar_r2.at[0], ar_f.at[0], ar1)
    arrived(w1_x)
    at = w1.at[s]
    w1_y = [wires.send(at, at, to_y)]
    w1_c = [wires.send(at, at, to_core)]
    arrived(w2_z)
    at = w2.at[s, :, x]
    w2_x = [wires.send(at, at, to_x)]
    arrived(qo_y)
    at = w0.at[s_y, :, :, :, 2 * sw : 4 * sw]
    qo_c2 = [wires.send(at, at, to_core)]
    ar1 = reduce_third(ar_a, ar_r1.at[0], ar_r2.at[0], ar_f.at[0], ar1)
    arrived(qo_c)
    arrived(qo_c2)
    for i in range(ns):
        wqt[sw * i : sw * (i + 1), :] = turn(flat(w0[i, :, :, :, 2 * sw : 3 * sw]))
        wo[:, sw * i : sw * (i + 1)] = flat(w0[i, :, :, :, 3 * sw : 4 * sw])

    qr = nn(wqt[...], xnrt[...]).astype(LOW)
    for h in range(heads):
        q_h = qr[size * h : size * (h + 1)]
        qrt[h] = q_h
        qfr[h] = features(nn(rft[h], q_h), q_h, scale, feat).astype(LOW)

    arrived(ar1)
    for h in range(heads):
        sumf[h, 0:size, :] = ar_f[0, h // 2, h % 2, 0:size, :]
        sumf[h, size : 2 * size, :] = loc[h, 0:size, :]
        first = lax.broadcasted_iota(jnp.int32, (PAD, feat), 0) == 0
        sumf[h, 2 * size : 2 * size + PAD, :] = jnp.where(
            first,
            ar_f[0, h // 2, h % 2, size : size + PAD, :].astype(WIDE),
            loc[h, size : size + PAD, :].astype(WIDE),
        ).astype(LOW)

    def split_ratio(nd, sh):
        pick = jnp.broadcast_to(sh, (size, sh.shape[1])) > 0.5
        num = jnp.where(pick, nd[0:size], nd[size : 2 * size])
        den = jnp.where(sh > 0.5, nd[2 * size : 2 * size + 1], nd[2 * size + 1 : 2 * size + 2])
        return num, den

    for h in range(heads):
        num, den = split_ratio(nn(sumf[h], qfr[h]), sh_r)
        num_r[h] = num
        den_r[h] = jnp.broadcast_to(den, (8, slots))
        hort[size * h : size * (h + 1), :] = (num * (1.0 / den)).astype(LOW)

    middle_r = toks_r + nn(turn(hort[...]), wo[...])
    unit2, inv2 = unit_norm(middle_r)
    xn2_r = (unit2 * gain2 + bias2).astype(LOW)
    xn2_rt = turn(xn2_r)
    slot_id = lax.broadcasted_iota(jnp.int32, (slots, 1), 0)
    cot = mg[...].astype(WIDE) * jnp.where(slot_id < cnt[0, 0], 1.0, 0.0)
    cot_low = cot.astype(LOW)
    cot_t = turn(cot_low)

    arrived(w2_x)
    at = w2.at[s]
    w2_y = [wires.send(at, at, to_y)]
    w2_c = [wires.send(at, at, to_core)]
    arrived(w1_y)
    at = w1.at[s_y]
    w1_c2 = [wires.send(at, at, to_core)]
    arrived(w2_y)
    at = w2.at[s_y]
    w2_c2 = [wires.send(at, at, to_core)]
    arrived(w1_c)
    arrived(w2_c)
    arrived(w1_c2)
    arrived(w2_c2)

    dn2 = jnp.zeros((slots, width), WIDE)
    for i in range(ns):
        win = flat(w1[i])
        upper = nn(xn2_r, win)
        cdf = 0.5 + 0.5 * lax.erf(upper * ROOT_HALF)
        act = (upper * cdf).astype(LOW)
        slope = cdf + upper * (PDF_SCALE * jnp.exp(-0.5 * upper * upper))
        du = (nn(cot_low, flat(w2[i])) * slope).astype(LOW)
        g1[i] = nn(xn2_rt, du).astype(LOW).reshape(g1.shape[1:])
        g2[i] = nn(cot_t, act).astype(LOW).reshape(g2.shape[1:])
        dn2 = dn2 + nt(du, win)

    def scatter_first(g, rc):
        return [wires.send(g.at[2 * yy + 1 - c], rc.at[yy], to_core) for yy in range(2)]

    def scatter_add_core(g, rc, copies):
        arrived(copies)
        for yy in range(2):
            def step(j, carry):
                g[2 * yy + c, j] = (g[2 * yy + c, j].astype(WIDE) + rc[yy, j].astype(WIDE)).astype(LOW)
                return carry
            lax.fori_loop(0, nz, step, 0)

    def scatter_y(g, ra):
        return [wires.send(g.at[2 * (1 - y) + c], ra, to_y)]

    def scatter_y_add(g, ra, copies):
        arrived(copies)
        def step(j, carry):
            g[s, j] = (g[s, j].astype(WIDE) + ra[j].astype(WIDE)).astype(LOW)
            return carry
        lax.fori_loop(0, nz, step, 0)

    def scatter_x(g, rb):
        return [wires.send(g.at[s, :, 1 - x], rb, to_x)]

    def scatter_x_add(g, rb, copies):
        arrived(copies)
        g[s, :, x] = (g[s, :, x].astype(WIDE) + rb[...].astype(WIDE)).astype(LOW)

    def scatter_z(g, rz):
        return [
            wires.send(g.at[s, lax.rem(z + k, nz), x], rz.at[k - 1], to_z[k - 1])
            for k in range(1, nz)
        ]

    def scatter_done(g, rz, copies):
        arrived(copies)
        total = g[s, z, x].astype(WIDE)
        for k in range(nz - 1):
            total = total + rz[k].astype(WIDE)
        return total

    s1 = scatter_first(g1, rc1)
    s2 = scatter_first(g2, rc2)

    norm_g2 = jnp.sum(dn2 * unit2, axis=0, keepdims=True)
    norm_g3 = jnp.sum(dn2, axis=0, keepdims=True)
    dm = cot + norm_back(dn2, unit2, inv2, gain2)
    d_att = dm.astype(LOW)
    dmid_low[...] = d_att
    for i in range(ns):
        part = nn(hort[...], d_att[:, sw * i : sw * (i + 1)]).astype(LOW)
        gqo[i, :, :, :, sw : 2 * sw] = part.reshape(gqo.shape[1:4] + (sw,))
    dhd[...] = nt(wo[...], d_att)
    for h in range(heads):
        dh = dhd[size * h : size * (h + 1), :]
        rden = 1.0 / den_r[h, 0:1, :]
        d_num = (dh * rden).astype(LOW)
        d_den = (-jnp.sum(dh * num_r[h], axis=0, keepdims=True) * (rden * rden)).astype(LOW)
        shl = sh_r.astype(LOW)
        dn_st[h, 0:size, :] = d_num * shl
        dn_st[h, size : 2 * size, :] = d_num * (1.0 - shl)
        row = lax.broadcasted_iota(jnp.int32, (PAD, slots), 0)
        dd = jnp.broadcast_to(d_den.astype(WIDE), (PAD, slots))
        dn_st[h, 2 * size : 2 * size + PAD, :] = jnp.where(
            row == 0, dd * sh_r, jnp.where(row == 1, dd * (1.0 - sh_r), 0.0)
        ).astype(LOW)
        part = nt(dn_st[h], qfr[h]).astype(LOW)
        ar_a[h // 2, h % 2, 0:size, :] = part[0:size]
        ar_a[h // 2, h % 2, size : size + PAD, :] = part[2 * size :]
        loc[h] = part[size:]
    ar2 = reduce_first(ar_a, ar_r1.at[1])
    scatter_add_core(g1, rc1, s1)
    s1 = scatter_y(g1, ra1)
    scatter_add_core(g2, rc2, s2)
    s2 = [wires.send(g2.at[2 * yy + c, :, 1 - x], rb2.at[yy], to_x) for yy in range(2)]
    ar2 = reduce_second(ar_a, ar_r1.at[1], ar_r2.at[1], ar_f.at[1], ar2)

    for h in range(heads):
        d_qf = nn(turn(sumf[h]), dn_st[h])
        w = d_qf * qfr[h].astype(WIDE)
        ws = jnp.sum(w, axis=0, keepdims=True)
        q_h = qrt[h].astype(WIDE)
        dqt[size * h : size * (h + 1), :] = (
            scale * nn(rf[h], w.astype(LOW)) - (scale * scale) * q_h * ws
        ).astype(LOW)
    for i in range(ns):
        part = nt(xnrt[...], dqt[sw * i : sw * (i + 1), :]).astype(LOW)
        gqo[i, :, :, :, 0:sw] = part.reshape(gqo.shape[1:4] + (sw,))
    s0 = scatter_first(gqo, rc_qo)
    acc = jnp.zeros((width, slots), WIDE)
    for i in range(ns):
        acc = acc + nn(flat(w0[i, :, :, :, 2 * sw : 3 * sw]), dqt[sw * i : sw * (i + 1), :])
    dxqt[...] = acc.astype(LOW)
    ar2 = reduce_third(ar_a, ar_r1.at[1], ar_r2.at[1], ar_f.at[1], ar2)

    def dense_tile(t):
        at = pl.multiple_of(t * tile, tile)
        cols = pl.ds(at, tile)
        q = nn(wqt[...], xnt[:, cols]).astype(LOW)
        lane = lax.broadcasted_iota(jnp.int32, (1, tile), 1) + at
        sh = shared_mask(lane)
        for h in range(heads):
            q_h = q[size * h : size * (h + 1)]
            qf = features(nn(rft[h], q_h), q_h, scale, feat).astype(LOW)
            num, den = split_ratio(nn(sumf[h], qf), sh)
            hot[size * h : size * (h + 1), :] = (num * (1.0 / den)).astype(LOW)
        mid = tok[cols, :].astype(WIDE) + nn(turn(hot[...]), wo[...])
        unit, _ = unit_norm(mid)
        xn2 = (unit * gain2 + bias2).astype(LOW)
        total = mid
        for i in range(ns):
            up = nn(xn2, flat(w1[i]))
            act = (up * (0.5 + 0.5 * lax.erf(up * ROOT_HALF))).astype(LOW)
            total = total + nt(act, flat(w2[i]))
        mixed_v[cols, :] = total.astype(LOW)

    def dense_loop(lo, hi):
        def step(t, carry):
            dense_tile(t)
            return carry

        lax.fori_loop(lo, hi, step, 0)

    dense_loop(0, 2)

    arrived(ar2)
    for h in range(heads):
        first = lax.broadcasted_iota(jnp.int32, (PAD, feat), 0) == 0
        tail = jnp.where(
            first,
            ar_f[1, h // 2, h % 2, size : size + PAD, :].astype(WIDE),
            loc[h, size : size + PAD, :].astype(WIDE),
        ).astype(LOW)
        stack = jnp.concatenate([ar_f[1, h // 2, h % 2, 0:size, :], loc[h, 0:size, :], tail], axis=0)
        ar_a[h // 2, h % 2, 0:size, :] = stack[0:size]
        dsumt[h] = turn(stack)

    scatter_y_add(g1, ra1, s1)
    s1 = scatter_x(g1, rb1)
    arrived(s2)
    for yy in range(2):
        g2[2 * yy + c, :, x] = (g2[2 * yy + c, :, x].astype(WIDE) + rb2[yy].astype(WIDE)).astype(LOW)
    s2 = [wires.send(g2.at[2 * (1 - y) + c, :, x], ra2, to_y)]

    def key_block(sd, carry):
        def step(t, carry2):
            at = pl.multiple_of(t * wide_tile, wide_tile)
            cols = pl.ds(at, wide_tile)
            lane = lax.broadcasted_iota(jnp.int32, (1, wide_tile), 1) + at
            sh = shared_mask(lane)
            pick = jnp.broadcast_to(sh, (size, wide_tile)) > 0.5
            for i in range(2):
                h = 2 * sd + i
                kf = kft[h, :, cols]
                w = nn(dsumt[h], vs[h, :, cols]) * kf.astype(WIDE)
                ws = jnp.sum(w, axis=0, keepdims=True)
                k_h = kvt[sd, size * i : size * (i + 1), cols].astype(WIDE)
                dk = scale * nn(rf[h], w.astype(LOW)) - (scale * scale) * k_h * ws
                dva = nn(ar_a[sd, i, 0:size, :], kf)
                dvb = nn(loc[h, 0:size, :], kf)
                kvt[sd, size * i : size * (i + 1), cols] = dk.astype(LOW)
                kvt[sd, sw + size * i : sw + size * (i + 1), cols] = jnp.where(pick, dva, dvb).astype(LOW)
            return carry2

        lax.fori_loop(0, rows // wide_tile, step, 0)
        gkv[sd] = nt(xnt[...], kvt[sd]).astype(LOW).reshape(gkv.shape[1:])
        return carry

    lax.fori_loop(0, ns, key_block, 0)
    s3 = scatter_first(gkv, rc_kv)
    scatter_add_core(gqo, rc_qo, s0)
    s0 = scatter_y(gqo, ra_qo)
    scatter_x_add(g1, rb1, s1)
    s1 = scatter_z(g1, rz1)
    arrived(s2)
    g2[s, :, x] = (g2[s, :, x].astype(WIDE) + ra2[...].astype(WIDE)).astype(LOW)
    s2 = scatter_z(g2, rz2)
    scatter_add_core(gkv, rc_kv, s3)
    s3 = scatter_y(gkv, ra_kv)

    ng_a[...] = jnp.zeros(ng_a.shape, WIDE)

    def token_tile(t, carry):
        at = pl.multiple_of(t * tile, tile)
        cols = pl.ds(at, tile)
        dxt = nn(dxqt[...], pm[:, cols])
        for i in range(ns):
            dxt = dxt + nn(flat(w0[i, :, :, :, 0 : 2 * sw]), kvt[i, :, cols])
        dx = dxt.T
        unit, inv = unit_norm(tok[cols, :].astype(WIDE))
        tgrad_v[cols, :] = norm_back(dx, unit, inv, gain1) + nn(pt[cols, :], dmid_low[...])
        ng_a[0:1, :] += jnp.sum(dx * unit, axis=0, keepdims=True)
        ng_a[1:2, :] += jnp.sum(dx, axis=0, keepdims=True)
        return carry

    lax.fori_loop(0, rows // tile, token_tile, 0)
    out_t = pltpu.make_async_copy(tgrad_v, tgrad_out, out_sems.at[0])
    out_t.start()
    ng_a[2:3, :] = norm_g2
    ng_a[3:4, :] = norm_g3

    n_g = [wires.send(ng_a, ng_r.at[0], to_core)]
    scatter_y_add(gqo, ra_qo, s0)
    s0 = scatter_x(gqo, rb_qo)
    scatter_y_add(gkv, ra_kv, s3)
    s3 = scatter_x(gkv, rb_kv)
    arrived(n_g)
    wires.left(n_g)
    ng_a[...] += ng_r[0]
    n_g = [wires.send(ng_a, ng_r.at[1], to_y)]
    dense_loop(2, 4)
    arrived(n_g)
    wires.left(n_g)
    ng_a[...] += ng_r[1]
    n_g = [wires.send(ng_a, ng_r.at[2], to_x)]
    scatter_x_add(gqo, rb_qo, s0)
    s0 = scatter_z(gqo, rz_qo)
    scatter_x_add(gkv, rb_kv, s3)
    s3 = scatter_z(gkv, rz_kv)
    arrived(n_g)
    wires.left(n_g)
    ng_a[...] += ng_r[2]
    n_g = [wires.send(ng_a, ng_r.at[2 + k], to_z[k - 1]) for k in range(1, nz)]
    dense_loop(4, rows // tile)
    out_m = pltpu.make_async_copy(mixed_v, mixed_out, out_sems.at[1])
    out_m.start()

    gin[...] = scatter_done(g1, rz1, s1)
    gdn[...] = scatter_done(g2, rz2, s2).T
    qo = scatter_done(gqo, rz_qo, s0)
    kv = scatter_done(gkv, rz_kv, s3)
    gqkv[0] = qo[:, 0:sw]
    gqkv[1] = kv[:, 0:sw]
    gqkv[2] = kv[:, sw : 2 * sw]
    gop[...] = qo[:, sw : 2 * sw]
    arrived(n_g)
    total = ng_a[...]
    for k in range(1, nz):
        total = total + ng_r[2 + k]
    row = lax.broadcasted_iota(jnp.int32, total.shape, 0)
    mine = jnp.sum(jnp.where(row == s, total, 0.0), axis=0, keepdims=True)
    mine = jnp.broadcast_to(mine, total.shape)
    gnorm[...] = pltpu.roll(mine, lax.rem(width - bd * b, width), 1)[0:1, 0:bd]
    wires.drain()
    out_t.wait()
    out_m.wait()


def fits(mesh, args):
    tokens, qkv_weight, _, in_weight, _, _, rand_features = args[:7]
    nbat, ns = mesh.shape["batch"], mesh.shape["seq"]
    bd, sw = qkv_weight.shape[1], qkv_weight.shape[2]
    rows, width = tokens.shape[1], tokens.shape[2]
    heads, size, feat = rand_features.shape
    return (
        ns == 4
        and nbat == 8
        and tokens.shape[0] == 1
        and bd % 64 == 0
        and sw == 2 * size
        and in_weight.shape[1] == 4 * sw
        and heads == 2 * ns
        and rows % 512 == 0
        and feat == 256
    )


def fused_layer(
    nbat,
    ns,
    tokens,
    qkv_weight,
    out_proj,
    in_weight,
    out_weight,
    norm_params,
    rand_features,
    long_start,
    masked_pos,
    masked_count,
    masked_grad,
):
    nz = nbat // 2
    rows, width = tokens.shape[1], tokens.shape[2]
    slots = masked_grad.shape[1]
    heads, size, feat = rand_features.shape
    bd, sw = qkv_weight.shape[1], qkv_weight.shape[2]
    fw = in_weight.shape[1]
    stack = 2 * size + PAD
    low = lambda *shape: pltpu.VMEM(shape, LOW)
    wide = lambda *shape: pltpu.VMEM(shape, WIDE)
    vmem = pl.BlockSpec(memory_space=pltpu.VMEM)
    smem = pl.BlockSpec(memory_space=pltpu.SMEM)
    anywhere = pl.BlockSpec(memory_space=pl.ANY)
    tall = (nz, 2, bd)
    scratch = [
        low(ns, *tall, 4 * sw),
        low(ns, *tall, fw),
        low(ns, *tall, fw),
        low(ns, nz, 2, PAD, 2 * bd),
        low(ns, 2 * sw, width),
        low(width, width),
        low(width, width),
        low(width, rows),
        low(ns, 2 * sw, rows),
        low(heads, stack, rows),
        low(heads, feat, rows),
        low(slots, rows),
        low(rows, slots),
        wide(slots, 128),
        low(heads, feat, size),
        low(heads, stack, feat),
        low(heads, size + PAD, feat),
        low(ns, 2, size + PAD, feat),
        low(2, 2, 2, size + PAD, feat),
        low(2, 2, 2, size + PAD, feat),
        low(2, ns, 2, size + PAD, feat),
        low(heads, feat, stack),
        low(heads, size, slots),
        low(heads, feat, slots),
        wide(heads, size, slots),
        wide(heads, 8, slots),
        low(heads, stack, slots),
        low(width, 256),
        low(width, slots),
        low(slots, width),
        low(width, slots),
        low(width, slots),
        wide(width, slots),
        low(width, slots),
        low(ns, *tall, 2 * sw),
        low(ns, *tall, 2 * sw),
        low(ns, *tall, fw),
        low(ns, *tall, fw),
        low(2, *tall, 2 * sw),
        low(2, *tall, 2 * sw),
        low(2, *tall, fw),
        low(2, *tall, fw),
        low(*tall, 2 * sw),
        low(*tall, 2 * sw),
        low(*tall, fw),
        low(nz, bd, fw),
        low(nz, bd, 2 * sw),
        low(nz, bd, 2 * sw),
        low(nz, bd, fw),
        low(2, nz, bd, fw),
        low(nz - 1, bd, 2 * sw),
        low(nz - 1, bd, 2 * sw),
        low(nz - 1, bd, fw),
        low(nz - 1, bd, fw),
        wide(8, width),
        wide(2 + nz, 8, width),
        low(rows, width),
        wide(rows, width),
        pltpu.SemaphoreType.DMA((96,)),
        pltpu.SemaphoreType.DMA((96,)),
        pltpu.SemaphoreType.DMA((2,)),
    ]
    f32 = lambda *shape: jax.ShapeDtypeStruct(shape, WIDE)
    outs = pl.pallas_call(
        functools.partial(layer_kernel, nz, ns),
        out_shape=(
            jax.ShapeDtypeStruct((rows, width), LOW),
            f32(rows, width),
            f32(3, bd, sw),
            f32(bd, sw),
            f32(bd, fw),
            f32(fw, bd),
            f32(1, bd),
        ),
        in_specs=[vmem] * 7 + [smem, vmem, smem, vmem],
        out_specs=(anywhere, anywhere, vmem, vmem, vmem, vmem, vmem),
        scratch_shapes=scratch,
        compiler_params=pltpu.CompilerParams(
            collective_id=0, has_side_effects=True, vmem_limit_bytes=62 * 2**20
        ),
        name="layer",
    )(
        tokens.reshape(rows, width),
        qkv_weight,
        out_proj,
        in_weight,
        out_weight,
        norm_params,
        rand_features,
        long_start.reshape(1, 1),
        masked_pos,
        masked_count,
        masked_grad.reshape(slots, width),
    )
    return (outs[0][None], outs[1][None]) + outs[2:]


def solution(mesh):
    def body(*args):
        if fits(mesh, args):
            return fused_layer(mesh.shape["batch"], mesh.shape["seq"], *args)
        return on_device(*args)

    placed = (
        P("batch", "seq", None),
        P(None, "batch", "seq"),
        P("batch", "seq"),
        P("batch", "seq"),
        P("seq", "batch"),
        P("seq", "batch"),
        P(),
        P("batch"),
        P("batch", "seq"),
        P("batch", "seq"),
        P("batch", "seq", None),
    )
    return jax.shard_map(
        body,
        mesh=mesh,
        in_specs=placed,
        out_specs=(
            P("batch", "seq", None),
            P("batch", "seq", None),
            P(None, "batch", "seq"),
            P("batch", "seq"),
            P("batch", "seq"),
            P("seq", "batch"),
            P("seq", "batch"),
        ),
        check_vma=False,
    )
```

```python
import functools

import jax
import jax.numpy as jnp
from jax import lax
from jax.experimental import pallas as pl
from jax.experimental.pallas import tpu as pltpu
from jax.sharding import PartitionSpec as P

SHORT = 1024


EPS = 1e-05


def layer_norm_parts(values, gain_row, shift_row):
    row_mean = jnp.mean(values, axis=-1, keepdims=True)
    centred = values - row_mean
    row_var = jnp.mean(centred * centred, axis=-1, keepdims=True)
    inverse = lax.rsqrt(row_var + EPS)
    unit_rows = centred * inverse
    return (unit_rows * gain_row + shift_row, unit_rows, inverse)


def layer_norm_back(incoming, unit_rows, inverse, gain_row):
    scaled = incoming * gain_row
    inner = (
        scaled
        - jnp.mean(scaled, axis=-1, keepdims=True)
        - unit_rows * jnp.mean(scaled * unit_rows, axis=-1, keepdims=True)
    )
    return (inner * inverse, jnp.sum(incoming * unit_rows, axis=0), jnp.sum(incoming, axis=0))


def exact_gelu(values):
    return jax.nn.gelu(values, approximate=False)


def positive_raw(values, feature_dirs):
    feat_scale = values.shape[-1] ** (-0.25)
    projected = feat_scale * jnp.einsum(
        "rhd,hdm->rhm", values, feature_dirs, preferred_element_type=jnp.float32
    )
    values_wide = values.astype(jnp.float32)
    sq_norm = jnp.sum(values_wide * values_wide, axis=-1, keepdims=True)
    return jnp.exp(projected - 0.5 * feat_scale * feat_scale * sq_norm) * feature_dirs.shape[
        -1
    ] ** (-0.5)


def positive_back(feat_grad, raw_feat, values, feature_dirs):
    feat_scale = values.shape[-1] ** (-0.25)
    exponent_grad = feat_grad * raw_feat
    direct = feat_scale * jnp.einsum(
        "rhm,hdm->rhd",
        exponent_grad.astype(jnp.bfloat16),
        feature_dirs,
        preferred_element_type=jnp.float32,
    )
    values_wide = values.astype(jnp.float32)
    norm_part = (
        feat_scale * feat_scale * values_wide * jnp.sum(exponent_grad, axis=-1, keepdims=True)
    )
    return (direct - norm_part).astype(jnp.bfloat16)


def place_two(first_sel, second_sel, first_val, second_val):
    shape_tail = (1,) * first_val.ndim
    return (
        first_sel.reshape((3,) + shape_tail) * first_val[None]
        + second_sel.reshape((3,) + shape_tail) * second_val[None]
    )


def pick_one(stacked, which):
    return lax.dynamic_index_in_dim(stacked, which, 0, keepdims=False)


def on_device(
    tokens,
    qkv_weight,
    out_proj,
    in_weight,
    out_weight,
    norm_params,
    rand_features,
    long_start,
    masked_pos,
    masked_count,
    masked_grad,
):
    low_type = jnp.bfloat16
    wider_number_type = jnp.float32
    part_qkv, part_out, part_in, part_down, part_norm = (
        lax.all_gather(qkv_weight, "seq", axis=2, tiled=True),
        lax.all_gather(out_proj, "seq", axis=1, tiled=True),
        lax.all_gather(in_weight, "seq", axis=1, tiled=True),
        lax.all_gather(out_weight, "seq", axis=0, tiled=True),
        lax.all_gather(norm_params, "seq", axis=0, tiled=True),
    )
    w_qkv, w_out, w_in, w_down, norm_low = (
        lax.all_gather(part_qkv, "batch", axis=1, tiled=True),
        lax.all_gather(part_out, "batch", axis=0, tiled=True),
        lax.all_gather(part_in, "batch", axis=0, tiled=True),
        lax.all_gather(part_down, "batch", axis=1, tiled=True),
        lax.all_gather(part_norm, "batch", axis=1, tiled=True),
    )
    norm_wide = norm_low.astype(wider_number_type)
    row_count = tokens.shape[1]
    model_width = tokens.shape[2]
    head_count = rand_features.shape[0]
    head_size = rand_features.shape[1]
    seq_index = lax.axis_index("seq")
    seq_last = lax.axis_size("seq") - 1
    position = seq_index * row_count + jnp.arange(row_count, dtype=jnp.int32)
    long_from = long_start[0]
    long_span = lax.axis_size("seq") * row_count - SHORT
    segment = (position >= long_from).astype(jnp.int32) + (
        position >= long_from + long_span
    ).astype(jnp.int32)
    seg_lower = jnp.where(seq_index == 0, 0, 1).astype(jnp.int32)
    seg_upper = jnp.where(seq_index == seq_last, 2, 1).astype(jnp.int32)
    member_upper = ((segment == seg_upper) & (seg_upper != seg_lower)).astype(wider_number_type)
    member_lower = 1.0 - member_upper
    sel_lower = (jnp.arange(3, dtype=jnp.int32) == seg_lower).astype(wider_number_type)
    sel_upper = (jnp.arange(3, dtype=jnp.int32) == seg_upper).astype(wider_number_type) * (
        seg_upper != seg_lower
    ).astype(wider_number_type)
    tokens_wide = tokens[0].astype(wider_number_type)
    normed_wide, unit_one, inverse_one = layer_norm_parts(tokens_wide, norm_wide[0], norm_wide[1])
    normed = normed_wide.astype(low_type)
    query = (
        jnp.dot(normed, w_qkv[0], preferred_element_type=wider_number_type)
        .astype(low_type)
        .reshape(row_count, head_count, head_size)
    )
    key_vecs = (
        jnp.dot(normed, w_qkv[1], preferred_element_type=wider_number_type)
        .astype(low_type)
        .reshape(row_count, head_count, head_size)
    )
    value_vectors = (
        jnp.dot(normed, w_qkv[2], preferred_element_type=wider_number_type)
        .astype(low_type)
        .reshape(row_count, head_count, head_size)
    )
    key_raw = positive_raw(key_vecs, rand_features)
    key_feature_map = key_raw.astype(low_type)
    query_feature_map = positive_raw(query, rand_features).astype(low_type)
    key_bottom_rows = key_feature_map * member_lower.astype(low_type)[:, None, None]
    key_top_rows = key_feature_map * member_upper.astype(low_type)[:, None, None]
    summary_lower = jnp.einsum(
        "jkn,jkp->knp", key_bottom_rows, value_vectors, preferred_element_type=wider_number_type
    )
    summary_upper = jnp.einsum(
        "jkn,jkp->knp", key_top_rows, value_vectors, preferred_element_type=wider_number_type
    )
    total_lower = jnp.einsum(
        "thm,t->hm",
        key_feature_map,
        member_lower.astype(low_type),
        preferred_element_type=wider_number_type,
    )
    total_upper = jnp.einsum(
        "thm,t->hm",
        key_feature_map,
        member_upper.astype(low_type),
        preferred_element_type=wider_number_type,
    )
    summary_part = place_two(sel_lower, sel_upper, summary_lower, summary_upper)
    total_part = place_two(sel_lower, sel_upper, total_lower, total_upper)
    state_summary, total = lax.psum((summary_part, total_part), "seq")
    summary_low = state_summary.astype(low_type)
    total_low = total.astype(low_type)
    sum_bottom_half = pick_one(summary_low, seg_lower)
    sum_top_half = pick_one(summary_low, seg_upper)
    tot_lo = pick_one(total_low, seg_lower)
    tot_hi = pick_one(total_low, seg_upper)
    numerator = member_lower[:, None, None] * jnp.einsum(
        "pox,oxa->poa", query_feature_map, sum_bottom_half, preferred_element_type=wider_number_type
    )
    numerator = numerator + member_upper[:, None, None] * jnp.einsum(
        "pox,oxa->poa", query_feature_map, sum_top_half, preferred_element_type=wider_number_type
    )
    denom = member_lower[:, None] * jnp.einsum(
        "thm,hm->th", query_feature_map, tot_lo, preferred_element_type=wider_number_type
    )
    denom = denom + member_upper[:, None] * jnp.einsum(
        "thm,hm->th", query_feature_map, tot_hi, preferred_element_type=wider_number_type
    )
    heads_out = (numerator / denom[:, :, None]).reshape(row_count, model_width).astype(low_type)
    middle = tokens_wide + jnp.dot(heads_out, w_out, preferred_element_type=wider_number_type)
    normed_two = layer_norm_parts(middle, norm_wide[2], norm_wide[3])[0].astype(low_type)
    upper = jnp.dot(normed_two, w_in, preferred_element_type=wider_number_type)
    activated = exact_gelu(upper).astype(low_type)
    result = (middle + jnp.dot(activated, w_down, preferred_element_type=wider_number_type)).astype(
        low_type
    )
    back_qkv, back_out, back_in, back_down = (w_qkv, w_out, w_in, w_down)
    picked = masked_pos[0]
    in_use = (jnp.arange(picked.shape[0], dtype=jnp.int32) < masked_count[0, 0]).astype(
        wider_number_type
    )
    cot_rows = masked_grad[0].astype(wider_number_type) * in_use[:, None]
    cot_low = cot_rows.astype(low_type)
    middle_rows = middle[picked]
    normed_rows_wide, unit_two, inverse_two = layer_norm_parts(
        middle_rows, norm_wide[2], norm_wide[3]
    )
    normed_rows = normed_rows_wide.astype(low_type)
    upper_rows = jnp.dot(normed_rows, back_in, preferred_element_type=wider_number_type)
    act_rows = exact_gelu(upper_rows).astype(low_type)
    act_grad = jnp.dot(cot_low, back_down.T, preferred_element_type=wider_number_type)
    upper_grad = jax.vjp(exact_gelu, upper_rows)[1](act_grad)[0].astype(low_type)
    grad_in = jnp.einsum(
        "rd,rf->df", normed_rows, upper_grad, preferred_element_type=wider_number_type
    )
    grad_down = jnp.einsum("rf,rd->fd", act_rows, cot_low, preferred_element_type=wider_number_type)
    normed_grad_two = jnp.dot(upper_grad, back_in.T, preferred_element_type=wider_number_type)
    middle_ln, gain_two_grad, bias_two_grad = layer_norm_back(
        normed_grad_two, unit_two, inverse_two, norm_wide[2]
    )
    middle_grad = cot_rows + middle_ln
    attn_grad = middle_grad.astype(low_type)
    grad_out = jnp.einsum(
        "rd,re->de", heads_out[picked], attn_grad, preferred_element_type=wider_number_type
    )
    heads_grad = jnp.dot(attn_grad, back_out.T, preferred_element_type=wider_number_type).reshape(
        -1, head_count, head_size
    )
    query_rows = query[picked]
    query_raw_rows = positive_raw(query_rows, rand_features)
    query_feat_rows = query_feature_map[picked]
    lower_rows = member_lower[picked]
    upper_rows_mask = member_upper[picked]
    numer_rows = numerator[picked]
    denom_rows = denom[picked]
    numerator_gradient = (heads_grad / denom_rows[:, :, None]).astype(low_type)
    denom_grad = (-jnp.sum(heads_grad * numer_rows, axis=-1) / (denom_rows * denom_rows)).astype(
        low_type
    )
    lower_rows_low = lower_rows.astype(low_type)
    upper_rows_low = upper_rows_mask.astype(low_type)
    sgrad_lower = jnp.einsum(
        "wpb,wpq->pbq",
        query_feat_rows,
        numerator_gradient * lower_rows_low[:, None, None],
        preferred_element_type=wider_number_type,
    )
    sgrad_upper = jnp.einsum(
        "wpb,wpq->pbq",
        query_feat_rows,
        numerator_gradient * upper_rows_low[:, None, None],
        preferred_element_type=wider_number_type,
    )
    tgrad_lower = jnp.einsum(
        "rhm,rh->hm",
        query_feat_rows,
        denom_grad * lower_rows_low[:, None],
        preferred_element_type=wider_number_type,
    )
    tgrad_upper = jnp.einsum(
        "rhm,rh->hm",
        query_feat_rows,
        denom_grad * upper_rows_low[:, None],
        preferred_element_type=wider_number_type,
    )
    summary_grad_part = place_two(sel_lower, sel_upper, sgrad_lower, sgrad_upper)
    total_grad_part = place_two(sel_lower, sel_upper, tgrad_lower, tgrad_upper)
    summary_grad, total_grad = (
        lax.psum(summary_grad_part.astype(jnp.bfloat16), "seq").astype(jnp.float32),
        lax.psum(total_grad_part.astype(jnp.bfloat16), "seq").astype(jnp.float32),
    )
    summary_grad_low = summary_grad.astype(low_type)
    segment_grad_bottom = pick_one(summary_grad_low, seg_lower)
    segment_grad_top = pick_one(summary_grad_low, seg_upper)
    tg_lo = pick_one(total_grad, seg_lower)
    tg_hi = pick_one(total_grad, seg_upper)
    denom_grad_wide = denom_grad.astype(wider_number_type)
    query_lower = (
        jnp.einsum(
            "sci,cni->scn",
            numerator_gradient,
            sum_bottom_half,
            preferred_element_type=wider_number_type,
        )
        + denom_grad_wide[:, :, None] * tot_lo.astype(wider_number_type)[None]
    )
    query_upper = (
        jnp.einsum(
            "sci,cni->scn",
            numerator_gradient,
            sum_top_half,
            preferred_element_type=wider_number_type,
        )
        + denom_grad_wide[:, :, None] * tot_hi.astype(wider_number_type)[None]
    )
    query_feat_grad = (
        lower_rows[:, None, None] * query_lower + upper_rows_mask[:, None, None] * query_upper
    )
    key_lower_grad = (
        jnp.einsum(
            "zqy,qiy->zqi",
            value_vectors,
            segment_grad_bottom,
            preferred_element_type=wider_number_type,
        )
        + tg_lo[None]
    )
    key_upper_grad = (
        jnp.einsum(
            "zqy,qiy->zqi",
            value_vectors,
            segment_grad_top,
            preferred_element_type=wider_number_type,
        )
        + tg_hi[None]
    )
    key_feat_grad = (
        member_lower[:, None, None] * key_lower_grad + member_upper[:, None, None] * key_upper_grad
    )
    value_grad = member_lower[:, None, None] * jnp.einsum(
        "pox,oxa->poa",
        key_feature_map,
        segment_grad_bottom,
        preferred_element_type=wider_number_type,
    )
    value_grad = value_grad + member_upper[:, None, None] * jnp.einsum(
        "pox,oxa->poa", key_feature_map, segment_grad_top, preferred_element_type=wider_number_type
    )
    query_grad = positive_back(query_feat_grad, query_raw_rows, query_rows, rand_features).reshape(
        -1, model_width
    )
    key_grad = positive_back(key_feat_grad, key_raw, key_vecs, rand_features).reshape(
        row_count, model_width
    )
    value_low = value_grad.astype(low_type).reshape(row_count, model_width)
    grad_query_w = jnp.einsum(
        "rd,re->de", normed[picked], query_grad, preferred_element_type=wider_number_type
    )
    grad_key_w = jnp.einsum("td,te->de", normed, key_grad, preferred_element_type=wider_number_type)
    grad_value_w = jnp.einsum(
        "td,te->de", normed, value_low, preferred_element_type=wider_number_type
    )
    query_back = jnp.dot(query_grad, back_qkv[0].T, preferred_element_type=wider_number_type)
    normed_grad_one = jnp.dot(
        key_grad, back_qkv[1].T, preferred_element_type=wider_number_type
    ) + jnp.dot(value_low, back_qkv[2].T, preferred_element_type=wider_number_type)
    normed_grad_one = normed_grad_one.at[picked].add(query_back)
    token_ln, gain_one_grad, bias_one_grad = layer_norm_back(
        normed_grad_one, unit_one, inverse_one, norm_wide[0]
    )
    tokens_grad = token_ln.at[picked].add(middle_grad)
    grad_qkv = jnp.stack([grad_query_w, grad_key_w, grad_value_w])
    grad_norm = jnp.stack([gain_one_grad, bias_one_grad, gain_two_grad, bias_two_grad])
    first_qkv, first_out, first_in, first_down, first_norm = (
        lax.psum_scatter(grad_qkv, "batch", scatter_dimension=1, tiled=True),
        lax.psum_scatter(grad_out, "batch", scatter_dimension=0, tiled=True),
        lax.psum_scatter(grad_in, "batch", scatter_dimension=0, tiled=True),
        lax.psum_scatter(grad_down, "batch", scatter_dimension=1, tiled=True),
        lax.psum_scatter(grad_norm, "batch", scatter_dimension=1, tiled=True),
    )
    owned = (
        lax.psum_scatter(
            first_qkv.astype(jnp.bfloat16), "seq", scatter_dimension=2, tiled=True
        ).astype(jnp.float32),
        lax.psum_scatter(
            first_out.astype(jnp.bfloat16), "seq", scatter_dimension=1, tiled=True
        ).astype(jnp.float32),
        lax.psum_scatter(
            first_in.astype(jnp.bfloat16), "seq", scatter_dimension=1, tiled=True
        ).astype(jnp.float32),
        lax.psum_scatter(
            first_down.astype(jnp.bfloat16), "seq", scatter_dimension=0, tiled=True
        ).astype(jnp.float32),
        lax.psum_scatter(
            first_norm.astype(jnp.bfloat16), "seq", scatter_dimension=0, tiled=True
        ).astype(jnp.float32),
    )
    return (result[None], tokens_grad[None], owned[0], owned[1], owned[2], owned[3], owned[4])


MESH = pl.DeviceIdType.MESH
LOW = jnp.bfloat16
WIDE = jnp.float32
LOG2E = 1.4426950408889634
ROOT_HALF = 0.7071067811865476
PDF_SCALE = 0.3989422804014327
PAD = 16
OWN_STEP = {"zxy": (3, 4, 5, 6), "zyx": (4, 5, 4, 5), "plane": (2, 3, 4, 5)}
KIND = {"kv": "plane", "qo": "zxy", "w1a": "zxy", "w1b": "zyx", "w2a": "zyx", "w2b": "zxy"}
EARLY = 2
PLAN = (
    ("norm", "kv", ),
    (),
    (),
    (),
    (),
    ("qo", ),
    ("w1b", ),
    ("kv", ),
    ("w1a", ),
    ("w2a", "qo", ),
    ("w2b", "w1b", ),
    ("kv", "qo", ),
    ("w1a", "w1b", ),
    ("qo", ),
    ("w2a", ),
    ("ar1", ),
    ("w2b", ),
    ("ar1", ),
    ("w1a", "w2a", ),
    ("ar1", "w1a", "w1b", "w2b", ),
    ("w2b", ),
    ("w1b", ),
    (),
    ("w2a", ),
    (),
    (),
    ("w1a", ),
    ("w1a", ),
    (),
    ("g2a", "g2b", "g1a", "g1b", ),
    (),
    ("ar2", ),
    (),
    ("ar2", "g2a", "g2b", "g1a", "g1b", ),
    ("qog", ),
    ("qog", ),
    (),
    (),
    (),
    (),
    ("g2a", "g2b", "g1a", ),
    ("kg", "vg", ),
    ("g1b", ),
    (),
    ("g2b", "qog", ),
    ("kg", "vg", ),
    ("g2a", "g1a", "g1b", ),
    ("vg", "g2b", ),
    ("qog", ),
    ("ngs", ),
    ("kg", "vg", "ngs", ),
    ("ngs", ),
    ("kg", "g2a", "ngs", "g1a", ),
    ("vg", "g1b", "ngs", ),
)


def dot_over(a, b, ca, cb):
    return lax.dot_general(a, b, (((ca,), (cb,)), ((), ())), preferred_element_type=WIDE)


def nn(a, b):
    return dot_over(a, b, 1, 0)


def nt(a, b):
    return dot_over(a, b, 1, 1)


def turn(a):
    if a.dtype == LOW:
        return a.astype(WIDE).T.astype(LOW)
    return a.T


def flat(a):
    return a.reshape(-1, a.shape[-1])


def unit_norm(x):
    cen = x - jnp.mean(x, axis=-1, keepdims=True)
    inv = lax.rsqrt(jnp.mean(cen * cen, axis=-1, keepdims=True) + EPS)
    return cen * inv, inv


def norm_back(incoming, unit, inv, gain):
    e = incoming * gain
    mean_e = jnp.mean(e, axis=-1, keepdims=True)
    mean_eu = jnp.mean(e * unit, axis=-1, keepdims=True)
    return inv * (e - mean_e - unit * mean_eu)


def features(proj, u_low, scale, feat):
    wide = u_low.astype(WIDE)
    sq = jnp.sum(wide * wide, axis=0, keepdims=True)
    shift = (0.5 * scale * scale * LOG2E) * sq
    half_log = 0.5 * (feat.bit_length() - 1)
    return jnp.exp2((scale * LOG2E) * proj - (shift + half_log))


class Wires:
    def __init__(self, send_sems, recv_sems):
        self.send_sems, self.recv_sems, self.used, self.sent = send_sems, recv_sems, 0, []

    def send(self, src, dst, dev):
        c = pltpu.make_async_remote_copy(
            src_ref=src,
            dst_ref=dst,
            send_sem=self.send_sems.at[self.used],
            recv_sem=self.recv_sems.at[self.used],
            device_id=dev,
            device_id_type=MESH,
        )
        self.used += 1
        c.start()
        self.sent.append(c)
        return c

    def left(self, copies):
        for c in copies:
            c.wait_send()
            self.sent = [o for o in self.sent if o is not c]

    def drain(self):
        self.left(list(self.sent))


def arrived(copies):
    for c in copies:
        c.wait_recv()


def layer_kernel(
    nz,
    ns,
    tok_in,
    wqkv_in,
    wo_in,
    win_in,
    wdn_in,
    nrm_in,
    rf,
    ls,
    pos,
    cnt,
    mg,
    mixed_out,
    tgrad_out,
    gqkv,
    gop,
    gin,
    gdn,
    gnorm,
    tok,
    w0,
    w1,
    w2,
    nb,
    wkvt,
    wqt,
    wo,
    xnt,
    kvt,
    vs,
    kft,
    pm,
    posc,
    rft,
    sumf,
    loc,
    ar_a,
    ar_r1,
    ar_r2,
    ar_f,
    dsumt,
    qrt,
    qfr,
    num_r,
    den_r,
    dn_st,
    hot,
    hort,
    dmid_low,
    xnrt,
    dqt,
    dhd,
    dxqt,
    g0,
    g1,
    g2,
    ng_a,
    ng_r,
    mixed_v,
    tgrad_v,
    send_sems,
    recv_sems,
    out_sems,
    *scatter_refs,
):
    rows, width = tok.shape
    slots = mg.shape[0]
    heads, size, feat = rf.shape
    scale = size**-0.25
    bd = w0.shape[3]
    sw = wqkv_in.shape[2]
    tile = 256
    wide_tile = 512
    b = lax.axis_index("batch")
    s = lax.axis_index("seq")
    x = lax.rem(b, 2)
    z = b // 2
    c = lax.rem(s, 2)
    y = s // 2
    s_core = s + 1 - 2 * c
    s_y = s + 2 - 4 * y
    s_far = s_core + 2 - 4 * y
    to_core = (b, s_core)
    to_y = (b, s_y)
    to_x = (b + 1 - 2 * x, s)
    to_z = [(lax.rem(z + k, nz) * 2 + x, s) for k in range(1, nz)]
    to_diag = [(lax.rem(z + k, nz) * 2 + 1 - x, s) for k in range(1, nz)]
    to_plane = to_z + [to_x] + to_diag
    to_seq = [to_core, to_y, (b, s_far)]
    wires = Wires(send_sems, recv_sems)

    in_t = pltpu.make_async_copy(tok_in, tok, out_sems.at[2])
    in_t.start()
    barrier = pltpu.get_barrier_semaphore()
    partners = to_plane + to_seq
    for dev in partners:
        pl.semaphore_signal(barrier, inc=1, device_id=dev, device_id_type=MESH)

    w0[s, z, x, :, 0:sw] = wqkv_in[1]
    w0[s, z, x, :, sw : 2 * sw] = wqkv_in[2]
    w0[s, z, x, :, 2 * sw : 3 * sw] = wqkv_in[0]
    w0[s, z, x, :, 3 * sw : 4 * sw] = wo_in[...]
    w1[s, z, x] = win_in[...]
    w2[s, z, x] = wdn_in[...]
    place = (
        lax.broadcasted_iota(jnp.int32, (bd, 2 * bd), 1)
        == lax.broadcasted_iota(jnp.int32, (bd, 2 * bd), 0) + bd * x
    )
    nb[s, z, x] = nn(
        jnp.broadcast_to(nrm_in[...], (PAD, bd)), jnp.where(place, 1.0, 0.0).astype(LOW)
    ).astype(LOW)
    pl.semaphore_wait(barrier, len(partners))

    tasks, steps = {}, {}
    plan = list(PLAN)

    def go(name):
        steps[name] += 1
        next(tasks[name], None)

    def poll():
        for name in plan.pop(0) if plan else ():
            go(name)

    def need(name, step):
        while steps[name] < step:
            go(name)

    def gather_norm():
        at = nb.at[s, z, x]
        first = [wires.send(at, at, dev) for dev in to_plane]
        yield
        arrived(first)
        at = nb.at[s]
        second = [wires.send(at, at, dev) for dev in to_seq]
        yield
        arrived(second)
        yield

    def gather_plane(ref, lo, hi):
        at = ref.at[s, z, x, :, lo:hi]
        first = [wires.send(at, at, dev) for dev in to_plane]
        yield
        arrived(first)
        at = ref.at[s, :, :, :, lo:hi]
        near = [wires.send(at, at, to_core)]
        far = [wires.send(at, at, to_y)]
        yield
        arrived(near)
        yield
        arrived(far)
        at = ref.at[s_y, :, :, :, lo:hi]
        last = [wires.send(at, at, to_core)]
        yield
        arrived(last)
        yield

    def gather_zxy(ref, lo, hi):
        at = ref.at[s, z, x, :, lo:hi]
        now = [wires.send(at, at, dev) for dev in to_z]
        yield
        arrived(now)
        at = ref.at[s, :, x, :, lo:hi]
        now = [wires.send(at, at, to_x)]
        yield
        arrived(now)
        at = ref.at[s, :, :, :, lo:hi]
        near = [wires.send(at, at, to_core)]
        far = [wires.send(at, at, to_y)]
        yield
        arrived(near)
        yield
        arrived(far)
        at = ref.at[s_y, :, :, :, lo:hi]
        last = [wires.send(at, at, to_core)]
        yield
        arrived(last)
        yield

    def gather_zyx(ref, lo, hi):
        at = ref.at[s, z, x, :, lo:hi]
        now = [wires.send(at, at, dev) for dev in to_z]
        yield
        arrived(now)
        at = ref.at[s, :, x, :, lo:hi]
        now = [wires.send(at, at, to_y)]
        yield
        arrived(now)
        now = []
        for side in (s, s_y):
            at = ref.at[side, :, x, :, lo:hi]
            now.append(wires.send(at, at, to_x))
        yield
        arrived(now)
        now = []
        for side in (s, s_y):
            at = ref.at[side, :, :, :, lo:hi]
            now.append(wires.send(at, at, to_core))
        yield
        arrived(now)
        yield

    def reduce_seq(k):
        r1, r2, f = ar_r1.at[k], ar_r2.at[k], ar_f.at[k]
        now = [wires.send(ar_a.at[2 * v + 1 - c], r1.at[v], to_core) for v in range(2)]
        yield
        arrived(now)
        wires.left(now)
        for v in range(2):
            ar_a[2 * v + c] = ar_a[2 * v + c] + r1[v]
        now = [wires.send(ar_a.at[2 * v + c], r2.at[v], to_y) for v in range(2)]
        yield
        arrived(now)
        wires.left(now)
        for v in range(2):
            f[2 * v + c] = ar_a[2 * v + c] + r2[v]
        now = [wires.send(f.at[2 * v + c], f.at[2 * v + c], to_core) for v in range(2)]
        yield
        arrived(now)
        yield

    def scatter_start(g, lo, hi, rc):
        now = [
            wires.send(g.at[2 * v + 1 - c, :, :, :, lo:hi], rc.at[v], to_core) for v in range(2)
        ]
        yield
        arrived(now)
        for v in range(2):

            def add(j, carry):
                at = (2 * v + c, j, slice(None), slice(None), slice(lo, hi))
                g[at] = g[at] + rc[v, j]
                return carry

            lax.fori_loop(0, nz, add, 0)

    def scatter_end(g, lo, hi, rz):
        now = [
            wires.send(g.at[s, lax.rem(z + k, nz), x, :, lo:hi], rz.at[k - 1], to_z[k - 1])
            for k in range(1, nz)
        ]
        yield
        arrived(now)
        yield

    def scatter_yxz(g, lo, hi, rc, ra, rb, rz):
        yield from scatter_start(g, lo, hi, rc)
        now = [wires.send(g.at[2 * (1 - y) + c, :, :, :, lo:hi], ra, to_y)]
        yield
        arrived(now)

        def add(j, carry):
            g[s, j, :, :, lo:hi] = g[s, j, :, :, lo:hi] + ra[j]
            return carry

        lax.fori_loop(0, nz, add, 0)
        now = [wires.send(g.at[s, :, 1 - x, :, lo:hi], rb, to_x)]
        yield
        arrived(now)
        g[s, :, x, :, lo:hi] = g[s, :, x, :, lo:hi] + rb[...]
        yield from scatter_end(g, lo, hi, rz)

    def scatter_xyz(g, lo, hi, rc, ra, rb, rz):
        yield from scatter_start(g, lo, hi, rc)
        now = [
            wires.send(g.at[2 * v + c, :, 1 - x, :, lo:hi], rb.at[v], to_x) for v in range(2)
        ]
        yield
        arrived(now)
        for v in range(2):
            g[2 * v + c, :, x, :, lo:hi] = g[2 * v + c, :, x, :, lo:hi] + rb[v]
        now = [wires.send(g.at[2 * (1 - y) + c, :, x, :, lo:hi], ra, to_y)]
        yield
        arrived(now)
        g[s, :, x, :, lo:hi] = g[s, :, x, :, lo:hi] + ra[...]
        yield from scatter_end(g, lo, hi, rz)

    def scattered(name):
        g, lo, hi, rz = scattered_parts[name]
        total = g[s, z, x, :, lo:hi].astype(WIDE)
        for k in range(nz - 1):
            total = total + rz[k].astype(WIDE)
        return total

    def add_task(name, task):
        tasks[name], steps[name] = task, 0

    half = w1.shape[4] // 2
    gathers = {"plane": gather_plane, "zxy": gather_zxy, "zyx": gather_zyx}
    add_task("norm", gather_norm())
    add_task("kv", gathers[KIND["kv"]](w0, 0, 2 * sw))
    add_task("qo", gathers[KIND["qo"]](w0, 2 * sw, 4 * sw))
    for name, ref in (("w1", w1), ("w2", w2)):
        add_task(name + "a", gathers[KIND[name + "a"]](ref, 0, half))
        add_task(name + "b", gathers[KIND[name + "b"]](ref, half, 2 * half))
    add_task("ar1", reduce_seq(0))
    add_task("ar2", reduce_seq(1))
    scattered_parts = {}
    for n, (name, kind, g, lo, hi) in enumerate(
        scatter_parts(g0, g1, g2, sw, half)
    ):
        rc, ra, rb, rz = scatter_refs[4 * n : 4 * n + 4]
        make = scatter_yxz if kind == "yxz" else scatter_xyz
        add_task(name, make(g, lo, hi, rc, ra, rb, rz))
        scattered_parts[name] = (g, lo, hi, rz)

    def own_ready(name, j):
        need(name, OWN_STEP[KIND[name]][j])

    poll()

    seq_pos = s * rows
    long_from = ls[0, 0]
    long_to = long_from + ns * rows - SHORT
    blocks = [s, s_core, s_y, s_far]

    def shared_mask(position):
        at = position + seq_pos
        return jnp.where((at >= long_from) & (at < long_to), 1.0, 0.0)

    def tiles(lo, hi, step):
        def body(t, carry):
            step(t)
            return carry

        lax.fori_loop(lo, hi, body, 0)

    pos_row = pos[...]
    posc[...] = jnp.broadcast_to(pos_row.astype(WIDE), (128, slots)).T
    sh_r = shared_mask(pos_row)

    def select_tile(t):
        at = pl.multiple_of(t * tile, tile)
        for j in range(tile // 128):
            lane = lax.broadcasted_iota(jnp.int32, (slots, 128), 1) + (at + 128 * j)
            pm[:, pl.ds(at + 128 * j, 128)] = jnp.where(
                lane.astype(WIDE) == posc[...], 1.0, 0.0
            ).astype(LOW)
        lane = lax.broadcasted_iota(jnp.int32, (1, tile), 1) + at
        sh = shared_mask(lane)
        row = lax.broadcasted_iota(jnp.int32, (PAD, tile), 0)
        ones = jnp.where(row == 0, sh, jnp.where(row == 1, 1.0 - sh, 0.0)).astype(LOW)
        for h in range(heads):
            vs[h, 2 * size : 2 * size + PAD, pl.ds(at, tile)] = ones

    tiles(0, rows // tile, select_tile)
    poll()
    for h in range(heads):
        rft[h] = turn(rf[h])
    in_t.wait()
    toks_r = nn(pm[...], tok[...])
    poll()
    need("norm", 2)
    unit_r, _ = unit_norm(toks_r)
    poll()
    need("norm", 3)

    def norm_row(i):
        return jnp.concatenate(
            [
                (nb[i, j, 0, 0:1, :] + nb[i, j, 1, 0:1, :]).astype(WIDE)
                for j in range(nz)
            ],
            axis=1,
        )

    gain1, bias1, gain2, bias2 = [norm_row(i) for i in range(4)]
    xn_r = (unit_r * gain1 + bias1).astype(LOW)
    xnrt[...] = turn(xn_r)

    def norm_tile(t):
        at = pl.multiple_of(t * tile, tile)
        unit, _ = unit_norm(tok[pl.ds(at, tile), :].astype(WIDE))
        xnt[:, pl.ds(at, tile)] = turn((unit * gain1 + bias1).astype(LOW))

    for n in range(3):
        tiles(2 * n, 2 * n + 2, norm_tile)
        poll()

    def kv_tile(sd, t):
        at = pl.multiple_of(t * wide_tile, wide_tile)
        cols = pl.ds(at, wide_tile)
        r = nn(wkvt[sd], xnt[:, cols]).astype(LOW)
        kvt[sd, :, cols] = r
        lane = lax.broadcasted_iota(jnp.int32, (1, wide_tile), 1) + at
        sh = shared_mask(lane).astype(LOW)
        for i in range(2):
            h = 2 * sd + i
            k_h = r[size * i : size * (i + 1)]
            v_h = r[sw + size * i : sw + size * (i + 1)]
            kft[h, :, cols] = features(nn(rft[h], k_h), k_h, scale, feat).astype(LOW)
            vs[h, 0:size, cols] = v_h * sh
            vs[h, size : 2 * size, cols] = v_h * (1.0 - sh)

    def kv_sums(sd):
        for i in range(2):
            h = 2 * sd + i
            part = nt(vs[h], kft[h]).astype(LOW)
            ar_a[sd, i, 0:size, :] = part[0:size]
            ar_a[sd, i, size : size + PAD, :] = part[2 * size :]
            loc[h] = part[size:]

    for j, sd in enumerate(blocks):
        own_ready("kv", j)
        wkvt[sd] = turn(flat(w0[sd, :, :, :, 0 : 2 * sw]))
        tiles(0, rows // wide_tile, functools.partial(kv_tile, sd))
        poll()
        kv_sums(sd)
        poll()
    poll()

    keep = (g0, g1, g2)

    def q_block(sd):
        wqt[sd] = turn(flat(w0[sd, :, :, :, 2 * sw : 3 * sw]))
        for t, gt in enumerate(keep):
            cols = slice(t * wide_tile, (t + 1) * wide_tile)
            q = nn(wqt[sd], xnt[:, cols]).astype(LOW)
            for i in range(2):
                q_h = q[size * i : size * (i + 1)]
                qf = features(nn(rft[2 * sd + i], q_h), q_h, scale, feat).astype(LOW)
                gt[sd, 2 * i : 2 * i + 2] = qf.reshape((2,) + g0.shape[2:4] + (wide_tile,))
        q = nn(wqt[sd], xnrt[...]).astype(LOW)
        for i in range(2):
            q_h = q[size * i : size * (i + 1)]
            qrt[2 * sd + i] = q_h
            qfr[2 * sd + i] = features(nn(rft[2 * sd + i], q_h), q_h, scale, feat).astype(LOW)

    for j, sd in enumerate(blocks):
        own_ready("qo", j)
        q_block(sd)
        poll()
    need("ar1", 4)

    def tail_rows(k, h):
        first = lax.broadcasted_iota(jnp.int32, (PAD, feat), 0) == 0
        return jnp.where(
            first,
            ar_f[k, h // 2, h % 2, size : size + PAD, :].astype(WIDE),
            loc[h, size : size + PAD, :].astype(WIDE),
        ).astype(LOW)

    for h in range(heads):
        sumf[h, 0:size, :] = ar_f[0, h // 2, h % 2, 0:size, :]
        sumf[h, size : 2 * size, :] = loc[h, 0:size, :]
        sumf[h, 2 * size : 2 * size + PAD, :] = tail_rows(0, h)

    def split_ratio(nd, sh):
        pick = jnp.broadcast_to(sh, (size, sh.shape[1])) > 0.5
        num = jnp.where(pick, nd[0:size], nd[size : 2 * size])
        den = jnp.where(sh > 0.5, nd[2 * size : 2 * size + 1], nd[2 * size + 1 : 2 * size + 2])
        return num, den

    for h in range(heads):
        num, den = split_ratio(nn(sumf[h], qfr[h]), sh_r)
        num_r[h] = num
        den_r[h] = jnp.broadcast_to(den, (8, slots))
        hort[size * h : size * (h + 1), :] = (num * (1.0 / den)).astype(LOW)
    poll()

    for t, gt in enumerate(keep):
        cols = slice(t * wide_tile, (t + 1) * wide_tile)
        lane = lax.broadcasted_iota(jnp.int32, (1, wide_tile), 1) + t * wide_tile
        sh = shared_mask(lane)

        def attend(i, gt=gt, cols=cols, sh=sh):
            for jj in range(2):
                h = 2 * i + jj
                qf = gt[i, 2 * jj : 2 * jj + 2].reshape(feat, wide_tile)
                num, den = split_ratio(nn(sumf[h], qf), sh)
                hot[h, :, cols] = (num * (1.0 / den)).astype(LOW)

        tiles(0, ns, attend)
        poll()

    for i in range(ns):
        wo[:, sw * i : sw * (i + 1)] = flat(w0[i, :, :, :, 3 * sw : 4 * sw])
    middle_r = toks_r + nn(turn(hort[...]), wo[...])
    unit2, inv2 = unit_norm(middle_r)
    xn2_r = (unit2 * gain2 + bias2).astype(LOW)
    xn2_rt = turn(xn2_r)
    slot_id = lax.broadcasted_iota(jnp.int32, (slots, 1), 0)
    cot = mg[...].astype(WIDE) * jnp.where(slot_id < cnt[0, 0], 1.0, 0.0)
    cot_low = cot.astype(LOW)
    cot_t = turn(cot_low)
    poll()

    dn2 = jnp.zeros((slots, width), WIDE)
    for j, sd in enumerate(blocks):
        for name in ("w1a", "w1b", "w2a", "w2b"):
            own_ready(name, j)
        win = flat(w1[sd])
        upper = nn(xn2_r, win)
        cdf = 0.5 + 0.5 * lax.erf(upper * ROOT_HALF)
        act = (upper * cdf).astype(LOW)
        slope = cdf + upper * (PDF_SCALE * jnp.exp(-0.5 * upper * upper))
        du = (nn(cot_low, flat(w2[sd])) * slope).astype(LOW)
        g2[sd] = nn(cot_t, act).astype(LOW).reshape(g2.shape[1:])
        g1[sd] = nn(xn2_rt, du).astype(LOW).reshape(g1.shape[1:])
        dn2 = dn2 + nt(du, win)
        poll()
    poll()

    norm_g2 = jnp.sum(dn2 * unit2, axis=0, keepdims=True)
    norm_g3 = jnp.sum(dn2, axis=0, keepdims=True)
    d_att = (cot + norm_back(dn2, unit2, inv2, gain2)).astype(LOW)
    dmid_low[...] = d_att
    dhd[...] = nt(wo[...], d_att)
    for h in range(heads):
        dh = dhd[size * h : size * (h + 1), :]
        rden = 1.0 / den_r[h, 0:1, :]
        d_num = (dh * rden).astype(LOW)
        d_den = (-jnp.sum(dh * num_r[h], axis=0, keepdims=True) * (rden * rden)).astype(LOW)
        shl = sh_r.astype(LOW)
        dn_st[h, 0:size, :] = d_num * shl
        dn_st[h, size : 2 * size, :] = d_num * (1.0 - shl)
        row = lax.broadcasted_iota(jnp.int32, (PAD, slots), 0)
        dd = jnp.broadcast_to(d_den.astype(WIDE), (PAD, slots))
        dn_st[h, 2 * size : 2 * size + PAD, :] = jnp.where(
            row == 0, dd * sh_r, jnp.where(row == 1, dd * (1.0 - sh_r), 0.0)
        ).astype(LOW)
        part = nt(dn_st[h], qfr[h]).astype(LOW)
        ar_a[h // 2, h % 2, 0:size, :] = part[0:size]
        ar_a[h // 2, h % 2, size : size + PAD, :] = part[2 * size :]
        loc[h] = part[size:]
    poll()
    poll()

    for h in range(heads):
        d_qf = nn(turn(sumf[h]), dn_st[h])
        w = d_qf * qfr[h].astype(WIDE)
        ws = jnp.sum(w, axis=0, keepdims=True)
        q_h = qrt[h].astype(WIDE)
        dqt[size * h : size * (h + 1), :] = (
            scale * nn(rf[h], w.astype(LOW)) - (scale * scale) * q_h * ws
        ).astype(LOW)
    poll()
    for i in range(ns):
        part = nt(xnrt[...], dqt[sw * i : sw * (i + 1), :]).astype(LOW)
        g0[i, :, :, :, 2 * sw : 3 * sw] = part.reshape(g0.shape[1:4] + (sw,))
        part = nn(hort[...], d_att[:, sw * i : sw * (i + 1)]).astype(LOW)
        g0[i, :, :, :, 3 * sw : 4 * sw] = part.reshape(g0.shape[1:4] + (sw,))
    acc = jnp.zeros((width, slots), WIDE)
    for i in range(ns):
        acc = acc + nn(flat(w0[i, :, :, :, 2 * sw : 3 * sw]), dqt[sw * i : sw * (i + 1), :])
    dxqt[...] = acc.astype(LOW)
    poll()
    poll()

    def dense_tile(t):
        at = pl.multiple_of(t * tile, tile)
        cols = pl.ds(at, tile)
        ho = turn(flat(hot[:, :, cols]))
        mid = tok[cols, :].astype(WIDE) + nn(ho, wo[...])
        unit, _ = unit_norm(mid)
        xn2 = (unit * gain2 + bias2).astype(LOW)
        total = mid
        for i in range(ns):
            up = nn(xn2, flat(w1[i]))
            act = (up * (0.5 + 0.5 * lax.erf(up * ROOT_HALF))).astype(LOW)
            total = total + nt(act, flat(w2[i]))
        mixed_v[cols, :] = total.astype(LOW)

    for n in range(EARLY):
        tiles(n, n + 1, dense_tile)
        poll()
    need("ar2", 4)

    for h in range(heads):
        stack = jnp.concatenate(
            [ar_f[1, h // 2, h % 2, 0:size, :], loc[h, 0:size, :], tail_rows(1, h)], axis=0
        )
        ar_a[h // 2, h % 2, 0:size, :] = stack[0:size]
        dsumt[h] = turn(stack)
    poll()

    def key_tile(sd, t):
        at = pl.multiple_of(t * wide_tile, wide_tile)
        cols = pl.ds(at, wide_tile)
        lane = lax.broadcasted_iota(jnp.int32, (1, wide_tile), 1) + at
        sh = shared_mask(lane)
        pick = jnp.broadcast_to(sh, (size, wide_tile)) > 0.5
        for i in range(2):
            h = 2 * sd + i
            kf = kft[h, :, cols]
            w = nn(dsumt[h], vs[h, :, cols]) * kf.astype(WIDE)
            ws = jnp.sum(w, axis=0, keepdims=True)
            k_h = kvt[sd, size * i : size * (i + 1), cols].astype(WIDE)
            dk = scale * nn(rf[h], w.astype(LOW)) - (scale * scale) * k_h * ws
            dva = nn(ar_a[sd, i, 0:size, :], kf)
            dvb = nn(loc[h, 0:size, :], kf)
            kvt[sd, size * i : size * (i + 1), cols] = dk.astype(LOW)
            kvt[sd, sw + size * i : sw + size * (i + 1), cols] = jnp.where(pick, dva, dvb).astype(LOW)

    for sd in (s_core, s_far, s_y, s):
        tiles(0, rows // wide_tile, functools.partial(key_tile, sd))
        poll()
        part = nt(xnt[...], kvt[sd]).astype(LOW)
        g0[sd, :, :, :, 0 : 2 * sw] = part.reshape(g0.shape[1:4] + (2 * sw,))
        poll()

    ng_a[...] = jnp.zeros(ng_a.shape, WIDE)

    def token_tile(t):
        at = pl.multiple_of(t * tile, tile)
        cols = pl.ds(at, tile)
        dxt = nn(dxqt[...], pm[:, cols])
        for i in range(ns):
            dxt = dxt + nn(flat(w0[i, :, :, :, 0 : 2 * sw]), kvt[i, :, cols])
        dx = dxt.T
        unit, inv = unit_norm(tok[cols, :].astype(WIDE))
        tgrad_v[cols, :] = norm_back(dx, unit, inv, gain1) + nn(turn(pm[:, cols]), dmid_low[...])
        ng_a[0:1, :] += jnp.sum(dx * unit, axis=0, keepdims=True)
        ng_a[1:2, :] += jnp.sum(dx, axis=0, keepdims=True)

    for n in range(3):
        tiles(2 * n, 2 * n + 2, token_tile)
        poll()
    out_t = pltpu.make_async_copy(tgrad_v, tgrad_out, out_sems.at[0])
    out_t.start()
    ng_a[2:3, :] = norm_g2
    ng_a[3:4, :] = norm_g3

    def sum_norm():
        order = [([to_core], 0), ([to_y], 1), ([to_x], 2), (to_z, 3)]
        for devs, k in order:
            now = [wires.send(ng_a, ng_r.at[k + n], dev) for n, dev in enumerate(devs)]
            yield
            arrived(now)
            wires.left(now)
            for n in range(len(devs)):
                ng_a[...] += ng_r[k + n]
        yield

    add_task("ngs", sum_norm())
    poll()
    for n in range(EARLY, rows // tile):
        tiles(n, n + 1, dense_tile)
        poll()
    out_m = pltpu.make_async_copy(mixed_v, mixed_out, out_sems.at[1])
    out_m.start()

    need("qog", 5)
    for name in ("g2a", "g2b", "g1a", "g1b"):
        need(name, 5)
    gin[:, 0:half] = scattered("g1a")
    gin[:, half:] = scattered("g1b")
    gdn[:, 0:half] = scattered("g2a")
    gdn[:, half:] = scattered("g2b")
    qo = scattered("qog")
    gqkv[0] = qo[:, 0:sw]
    gop[...] = qo[:, sw : 2 * sw]
    for step in range(1, 6):
        need("kg", step)
        need("vg", step)
        need("ngs", step)
    gqkv[1] = scattered("kg")
    gqkv[2] = scattered("vg")
    total = ng_a[...]
    row = lax.broadcasted_iota(jnp.int32, total.shape, 0)
    mine = jnp.sum(jnp.where(row == s, total, 0.0), axis=0, keepdims=True)
    mine = jnp.broadcast_to(mine, total.shape)
    gnorm[...] = pltpu.roll(mine, lax.rem(width - bd * b, width), 1)[0:1, 0:bd]
    assert not plan
    wires.drain()
    out_t.wait()
    out_m.wait()


def scatter_parts(g0, g1, g2, sw, half):
    return (
        ("g1a", "yxz", g1, 0, half),
        ("g1b", "xyz", g1, half, 2 * half),
        ("g2a", "yxz", g2, 0, half),
        ("g2b", "xyz", g2, half, 2 * half),
        ("qog", "xyz", g0, 2 * sw, 4 * sw),
        ("kg", "yxz", g0, 0, sw),
        ("vg", "xyz", g0, sw, 2 * sw),
    )


def fits(mesh, args):
    tokens, qkv_weight, _, in_weight, _, _, rand_features = args[:7]
    nbat, ns = mesh.shape["batch"], mesh.shape["seq"]
    bd, sw = qkv_weight.shape[1], qkv_weight.shape[2]
    rows, width = tokens.shape[1], tokens.shape[2]
    heads, size, feat = rand_features.shape
    return (
        ns == 4
        and nbat == 8
        and tokens.shape[0] == 1
        and bd % 64 == 0
        and sw == 2 * size
        and in_weight.shape[1] == 4 * sw
        and heads == 2 * ns
        and rows == 3 * 512
        and feat == 256
    )


def fused_layer(
    nbat,
    ns,
    tokens,
    qkv_weight,
    out_proj,
    in_weight,
    out_weight,
    norm_params,
    rand_features,
    long_start,
    masked_pos,
    masked_count,
    masked_grad,
):
    nz = nbat // 2
    rows, width = tokens.shape[1], tokens.shape[2]
    slots = masked_grad.shape[1]
    heads, size, feat = rand_features.shape
    bd, sw = qkv_weight.shape[1], qkv_weight.shape[2]
    fw = in_weight.shape[1]
    stack = 2 * size + PAD
    low = lambda *shape: pltpu.VMEM(shape, LOW)
    wide = lambda *shape: pltpu.VMEM(shape, WIDE)
    vmem = pl.BlockSpec(memory_space=pltpu.VMEM)
    smem = pl.BlockSpec(memory_space=pltpu.SMEM)
    anywhere = pl.BlockSpec(memory_space=pl.ANY)
    tall = (nz, 2, bd)
    scratch = [
        low(rows, width),
        low(ns, *tall, 4 * sw),
        low(ns, *tall, fw),
        low(ns, *tall, fw),
        low(ns, nz, 2, PAD, 2 * bd),
        low(ns, 2 * sw, width),
        low(ns, sw, width),
        low(width, width),
        low(width, rows),
        low(ns, 2 * sw, rows),
        low(heads, stack, rows),
        low(heads, feat, rows),
        low(slots, rows),
        wide(slots, 128),
        low(heads, feat, size),
        low(heads, stack, feat),
        low(heads, size + PAD, feat),
        low(ns, 2, size + PAD, feat),
        low(2, 2, 2, size + PAD, feat),
        low(2, 2, 2, size + PAD, feat),
        low(2, ns, 2, size + PAD, feat),
        low(heads, feat, stack),
        low(heads, size, slots),
        low(heads, feat, slots),
        wide(heads, size, slots),
        wide(heads, 8, slots),
        low(heads, stack, slots),
        low(heads, size, rows),
        low(width, slots),
        low(slots, width),
        low(width, slots),
        low(width, slots),
        wide(width, slots),
        low(width, slots),
        low(ns, *tall, 4 * sw),
        low(ns, *tall, fw),
        low(ns, *tall, fw),
        wide(8, width),
        wide(2 + nz, 8, width),
        low(rows, width),
        wide(rows, width),
        pltpu.SemaphoreType.DMA((160,)),
        pltpu.SemaphoreType.DMA((160,)),
        pltpu.SemaphoreType.DMA((3,)),
    ]
    for _, kind, _, lo, hi in scatter_parts(None, None, None, sw, fw // 2):
        n = hi - lo
        scratch.append(low(2, *tall, n))
        if kind == "yxz":
            scratch += [low(*tall, n), low(nz, bd, n)]
        else:
            scratch += [low(nz, bd, n), low(2, nz, bd, n)]
        scratch.append(low(nz - 1, bd, n))
    f32 = lambda *shape: jax.ShapeDtypeStruct(shape, WIDE)
    outs = pl.pallas_call(
        functools.partial(layer_kernel, nz, ns),
        out_shape=(
            jax.ShapeDtypeStruct((rows, width), LOW),
            f32(rows, width),
            f32(3, bd, sw),
            f32(bd, sw),
            f32(bd, fw),
            f32(bd, fw),
            f32(1, bd),
        ),
        in_specs=[anywhere] + [vmem] * 6 + [smem, vmem, smem, vmem],
        out_specs=(anywhere, anywhere, vmem, vmem, vmem, vmem, vmem),
        scratch_shapes=scratch,
        compiler_params=pltpu.CompilerParams(
            collective_id=0, has_side_effects=True, vmem_limit_bytes=62 * 2**20
        ),
        name="layer",
    )(
        tokens.reshape(rows, width),
        qkv_weight,
        out_proj,
        in_weight,
        out_weight.T,
        norm_params,
        rand_features,
        long_start.reshape(1, 1),
        masked_pos,
        masked_count,
        masked_grad.reshape(slots, width),
    )
    return (outs[0][None], outs[1][None]) + outs[2:5] + (outs[5].T, outs[6])


def solution(mesh):
    def body(*args):
        if fits(mesh, args):
            return fused_layer(mesh.shape["batch"], mesh.shape["seq"], *args)
        return on_device(*args)

    placed = (
        P("batch", "seq", None),
        P(None, "batch", "seq"),
        P("batch", "seq"),
        P("batch", "seq"),
        P("seq", "batch"),
        P("seq", "batch"),
        P(),
        P("batch"),
        P("batch", "seq"),
        P("batch", "seq"),
        P("batch", "seq", None),
    )
    return jax.shard_map(
        body,
        mesh=mesh,
        in_specs=placed,
        out_specs=(
            P("batch", "seq", None),
            P("batch", "seq", None),
            P(None, "batch", "seq"),
            P("batch", "seq"),
            P("batch", "seq"),
            P("seq", "batch"),
            P("seq", "batch"),
        ),
        check_vma=False,
    )
```

```python
import functools

import jax
import jax.numpy as jnp
from jax import lax
from jax.experimental import pallas as pl
from jax.experimental.pallas import tpu as pltpu
from jax.sharding import PartitionSpec as P

SHORT = 1024


EPS = 1e-05


def layer_norm_parts(values, gain_row, shift_row):
    row_mean = jnp.mean(values, axis=-1, keepdims=True)
    centred = values - row_mean
    row_var = jnp.mean(centred * centred, axis=-1, keepdims=True)
    inverse = lax.rsqrt(row_var + EPS)
    unit_rows = centred * inverse
    return (unit_rows * gain_row + shift_row, unit_rows, inverse)


def layer_norm_back(incoming, unit_rows, inverse, gain_row):
    scaled = incoming * gain_row
    inner = (
        scaled
        - jnp.mean(scaled, axis=-1, keepdims=True)
        - unit_rows * jnp.mean(scaled * unit_rows, axis=-1, keepdims=True)
    )
    return (inner * inverse, jnp.sum(incoming * unit_rows, axis=0), jnp.sum(incoming, axis=0))


def exact_gelu(values):
    return jax.nn.gelu(values, approximate=False)


def positive_raw(values, feature_dirs):
    feat_scale = values.shape[-1] ** (-0.25)
    projected = feat_scale * jnp.einsum(
        "rhd,hdm->rhm", values, feature_dirs, preferred_element_type=jnp.float32
    )
    values_wide = values.astype(jnp.float32)
    sq_norm = jnp.sum(values_wide * values_wide, axis=-1, keepdims=True)
    return jnp.exp(projected - 0.5 * feat_scale * feat_scale * sq_norm) * feature_dirs.shape[
        -1
    ] ** (-0.5)


def positive_back(feat_grad, raw_feat, values, feature_dirs):
    feat_scale = values.shape[-1] ** (-0.25)
    exponent_grad = feat_grad * raw_feat
    direct = feat_scale * jnp.einsum(
        "rhm,hdm->rhd",
        exponent_grad.astype(jnp.bfloat16),
        feature_dirs,
        preferred_element_type=jnp.float32,
    )
    values_wide = values.astype(jnp.float32)
    norm_part = (
        feat_scale * feat_scale * values_wide * jnp.sum(exponent_grad, axis=-1, keepdims=True)
    )
    return (direct - norm_part).astype(jnp.bfloat16)


def place_two(first_sel, second_sel, first_val, second_val):
    shape_tail = (1,) * first_val.ndim
    return (
        first_sel.reshape((3,) + shape_tail) * first_val[None]
        + second_sel.reshape((3,) + shape_tail) * second_val[None]
    )


def pick_one(stacked, which):
    return lax.dynamic_index_in_dim(stacked, which, 0, keepdims=False)


def on_device(
    tokens,
    qkv_weight,
    out_proj,
    in_weight,
    out_weight,
    norm_params,
    rand_features,
    long_start,
    masked_pos,
    masked_count,
    masked_grad,
):
    low_type = jnp.bfloat16
    wider_number_type = jnp.float32
    part_qkv, part_out, part_in, part_down, part_norm = (
        lax.all_gather(qkv_weight, "seq", axis=2, tiled=True),
        lax.all_gather(out_proj, "seq", axis=1, tiled=True),
        lax.all_gather(in_weight, "seq", axis=1, tiled=True),
        lax.all_gather(out_weight, "seq", axis=0, tiled=True),
        lax.all_gather(norm_params, "seq", axis=0, tiled=True),
    )
    w_qkv, w_out, w_in, w_down, norm_low = (
        lax.all_gather(part_qkv, "batch", axis=1, tiled=True),
        lax.all_gather(part_out, "batch", axis=0, tiled=True),
        lax.all_gather(part_in, "batch", axis=0, tiled=True),
        lax.all_gather(part_down, "batch", axis=1, tiled=True),
        lax.all_gather(part_norm, "batch", axis=1, tiled=True),
    )
    norm_wide = norm_low.astype(wider_number_type)
    row_count = tokens.shape[1]
    model_width = tokens.shape[2]
    head_count = rand_features.shape[0]
    head_size = rand_features.shape[1]
    seq_index = lax.axis_index("seq")
    seq_last = lax.axis_size("seq") - 1
    position = seq_index * row_count + jnp.arange(row_count, dtype=jnp.int32)
    long_from = long_start[0]
    long_span = lax.axis_size("seq") * row_count - SHORT
    segment = (position >= long_from).astype(jnp.int32) + (
        position >= long_from + long_span
    ).astype(jnp.int32)
    seg_lower = jnp.where(seq_index == 0, 0, 1).astype(jnp.int32)
    seg_upper = jnp.where(seq_index == seq_last, 2, 1).astype(jnp.int32)
    member_upper = ((segment == seg_upper) & (seg_upper != seg_lower)).astype(wider_number_type)
    member_lower = 1.0 - member_upper
    sel_lower = (jnp.arange(3, dtype=jnp.int32) == seg_lower).astype(wider_number_type)
    sel_upper = (jnp.arange(3, dtype=jnp.int32) == seg_upper).astype(wider_number_type) * (
        seg_upper != seg_lower
    ).astype(wider_number_type)
    tokens_wide = tokens[0].astype(wider_number_type)
    normed_wide, unit_one, inverse_one = layer_norm_parts(tokens_wide, norm_wide[0], norm_wide[1])
    normed = normed_wide.astype(low_type)
    query = (
        jnp.dot(normed, w_qkv[0], preferred_element_type=wider_number_type)
        .astype(low_type)
        .reshape(row_count, head_count, head_size)
    )
    key_vecs = (
        jnp.dot(normed, w_qkv[1], preferred_element_type=wider_number_type)
        .astype(low_type)
        .reshape(row_count, head_count, head_size)
    )
    value_vectors = (
        jnp.dot(normed, w_qkv[2], preferred_element_type=wider_number_type)
        .astype(low_type)
        .reshape(row_count, head_count, head_size)
    )
    key_raw = positive_raw(key_vecs, rand_features)
    key_feature_map = key_raw.astype(low_type)
    query_feature_map = positive_raw(query, rand_features).astype(low_type)
    key_bottom_rows = key_feature_map * member_lower.astype(low_type)[:, None, None]
    key_top_rows = key_feature_map * member_upper.astype(low_type)[:, None, None]
    summary_lower = jnp.einsum(
        "jkn,jkp->knp", key_bottom_rows, value_vectors, preferred_element_type=wider_number_type
    )
    summary_upper = jnp.einsum(
        "jkn,jkp->knp", key_top_rows, value_vectors, preferred_element_type=wider_number_type
    )
    total_lower = jnp.einsum(
        "thm,t->hm",
        key_feature_map,
        member_lower.astype(low_type),
        preferred_element_type=wider_number_type,
    )
    total_upper = jnp.einsum(
        "thm,t->hm",
        key_feature_map,
        member_upper.astype(low_type),
        preferred_element_type=wider_number_type,
    )
    summary_part = place_two(sel_lower, sel_upper, summary_lower, summary_upper)
    total_part = place_two(sel_lower, sel_upper, total_lower, total_upper)
    state_summary, total = lax.psum((summary_part, total_part), "seq")
    summary_low = state_summary.astype(low_type)
    total_low = total.astype(low_type)
    sum_bottom_half = pick_one(summary_low, seg_lower)
    sum_top_half = pick_one(summary_low, seg_upper)
    tot_lo = pick_one(total_low, seg_lower)
    tot_hi = pick_one(total_low, seg_upper)
    numerator = member_lower[:, None, None] * jnp.einsum(
        "pox,oxa->poa", query_feature_map, sum_bottom_half, preferred_element_type=wider_number_type
    )
    numerator = numerator + member_upper[:, None, None] * jnp.einsum(
        "pox,oxa->poa", query_feature_map, sum_top_half, preferred_element_type=wider_number_type
    )
    denom = member_lower[:, None] * jnp.einsum(
        "thm,hm->th", query_feature_map, tot_lo, preferred_element_type=wider_number_type
    )
    denom = denom + member_upper[:, None] * jnp.einsum(
        "thm,hm->th", query_feature_map, tot_hi, preferred_element_type=wider_number_type
    )
    heads_out = (numerator / denom[:, :, None]).reshape(row_count, model_width).astype(low_type)
    middle = tokens_wide + jnp.dot(heads_out, w_out, preferred_element_type=wider_number_type)
    normed_two = layer_norm_parts(middle, norm_wide[2], norm_wide[3])[0].astype(low_type)
    upper = jnp.dot(normed_two, w_in, preferred_element_type=wider_number_type)
    activated = exact_gelu(upper).astype(low_type)
    result = (middle + jnp.dot(activated, w_down, preferred_element_type=wider_number_type)).astype(
        low_type
    )
    back_qkv, back_out, back_in, back_down = (w_qkv, w_out, w_in, w_down)
    picked = masked_pos[0]
    in_use = (jnp.arange(picked.shape[0], dtype=jnp.int32) < masked_count[0, 0]).astype(
        wider_number_type
    )
    cot_rows = masked_grad[0].astype(wider_number_type) * in_use[:, None]
    cot_low = cot_rows.astype(low_type)
    middle_rows = middle[picked]
    normed_rows_wide, unit_two, inverse_two = layer_norm_parts(
        middle_rows, norm_wide[2], norm_wide[3]
    )
    normed_rows = normed_rows_wide.astype(low_type)
    upper_rows = jnp.dot(normed_rows, back_in, preferred_element_type=wider_number_type)
    act_rows = exact_gelu(upper_rows).astype(low_type)
    act_grad = jnp.dot(cot_low, back_down.T, preferred_element_type=wider_number_type)
    upper_grad = jax.vjp(exact_gelu, upper_rows)[1](act_grad)[0].astype(low_type)
    grad_in = jnp.einsum(
        "rd,rf->df", normed_rows, upper_grad, preferred_element_type=wider_number_type
    )
    grad_down = jnp.einsum("rf,rd->fd", act_rows, cot_low, preferred_element_type=wider_number_type)
    normed_grad_two = jnp.dot(upper_grad, back_in.T, preferred_element_type=wider_number_type)
    middle_ln, gain_two_grad, bias_two_grad = layer_norm_back(
        normed_grad_two, unit_two, inverse_two, norm_wide[2]
    )
    middle_grad = cot_rows + middle_ln
    attn_grad = middle_grad.astype(low_type)
    grad_out = jnp.einsum(
        "rd,re->de", heads_out[picked], attn_grad, preferred_element_type=wider_number_type
    )
    heads_grad = jnp.dot(attn_grad, back_out.T, preferred_element_type=wider_number_type).reshape(
        -1, head_count, head_size
    )
    query_rows = query[picked]
    query_raw_rows = positive_raw(query_rows, rand_features)
    query_feat_rows = query_feature_map[picked]
    lower_rows = member_lower[picked]
    upper_rows_mask = member_upper[picked]
    numer_rows = numerator[picked]
    denom_rows = denom[picked]
    numerator_gradient = (heads_grad / denom_rows[:, :, None]).astype(low_type)
    denom_grad = (-jnp.sum(heads_grad * numer_rows, axis=-1) / (denom_rows * denom_rows)).astype(
        low_type
    )
    lower_rows_low = lower_rows.astype(low_type)
    upper_rows_low = upper_rows_mask.astype(low_type)
    sgrad_lower = jnp.einsum(
        "wpb,wpq->pbq",
        query_feat_rows,
        numerator_gradient * lower_rows_low[:, None, None],
        preferred_element_type=wider_number_type,
    )
    sgrad_upper = jnp.einsum(
        "wpb,wpq->pbq",
        query_feat_rows,
        numerator_gradient * upper_rows_low[:, None, None],
        preferred_element_type=wider_number_type,
    )
    tgrad_lower = jnp.einsum(
        "rhm,rh->hm",
        query_feat_rows,
        denom_grad * lower_rows_low[:, None],
        preferred_element_type=wider_number_type,
    )
    tgrad_upper = jnp.einsum(
        "rhm,rh->hm",
        query_feat_rows,
        denom_grad * upper_rows_low[:, None],
        preferred_element_type=wider_number_type,
    )
    summary_grad_part = place_two(sel_lower, sel_upper, sgrad_lower, sgrad_upper)
    total_grad_part = place_two(sel_lower, sel_upper, tgrad_lower, tgrad_upper)
    summary_grad, total_grad = (
        lax.psum(summary_grad_part.astype(jnp.bfloat16), "seq").astype(jnp.float32),
        lax.psum(total_grad_part.astype(jnp.bfloat16), "seq").astype(jnp.float32),
    )
    summary_grad_low = summary_grad.astype(low_type)
    segment_grad_bottom = pick_one(summary_grad_low, seg_lower)
    segment_grad_top = pick_one(summary_grad_low, seg_upper)
    tg_lo = pick_one(total_grad, seg_lower)
    tg_hi = pick_one(total_grad, seg_upper)
    denom_grad_wide = denom_grad.astype(wider_number_type)
    query_lower = (
        jnp.einsum(
            "sci,cni->scn",
            numerator_gradient,
            sum_bottom_half,
            preferred_element_type=wider_number_type,
        )
        + denom_grad_wide[:, :, None] * tot_lo.astype(wider_number_type)[None]
    )
    query_upper = (
        jnp.einsum(
            "sci,cni->scn",
            numerator_gradient,
            sum_top_half,
            preferred_element_type=wider_number_type,
        )
        + denom_grad_wide[:, :, None] * tot_hi.astype(wider_number_type)[None]
    )
    query_feat_grad = (
        lower_rows[:, None, None] * query_lower + upper_rows_mask[:, None, None] * query_upper
    )
    key_lower_grad = (
        jnp.einsum(
            "zqy,qiy->zqi",
            value_vectors,
            segment_grad_bottom,
            preferred_element_type=wider_number_type,
        )
        + tg_lo[None]
    )
    key_upper_grad = (
        jnp.einsum(
            "zqy,qiy->zqi",
            value_vectors,
            segment_grad_top,
            preferred_element_type=wider_number_type,
        )
        + tg_hi[None]
    )
    key_feat_grad = (
        member_lower[:, None, None] * key_lower_grad + member_upper[:, None, None] * key_upper_grad
    )
    value_grad = member_lower[:, None, None] * jnp.einsum(
        "pox,oxa->poa",
        key_feature_map,
        segment_grad_bottom,
        preferred_element_type=wider_number_type,
    )
    value_grad = value_grad + member_upper[:, None, None] * jnp.einsum(
        "pox,oxa->poa", key_feature_map, segment_grad_top, preferred_element_type=wider_number_type
    )
    query_grad = positive_back(query_feat_grad, query_raw_rows, query_rows, rand_features).reshape(
        -1, model_width
    )
    key_grad = positive_back(key_feat_grad, key_raw, key_vecs, rand_features).reshape(
        row_count, model_width
    )
    value_low = value_grad.astype(low_type).reshape(row_count, model_width)
    grad_query_w = jnp.einsum(
        "rd,re->de", normed[picked], query_grad, preferred_element_type=wider_number_type
    )
    grad_key_w = jnp.einsum("td,te->de", normed, key_grad, preferred_element_type=wider_number_type)
    grad_value_w = jnp.einsum(
        "td,te->de", normed, value_low, preferred_element_type=wider_number_type
    )
    query_back = jnp.dot(query_grad, back_qkv[0].T, preferred_element_type=wider_number_type)
    normed_grad_one = jnp.dot(
        key_grad, back_qkv[1].T, preferred_element_type=wider_number_type
    ) + jnp.dot(value_low, back_qkv[2].T, preferred_element_type=wider_number_type)
    normed_grad_one = normed_grad_one.at[picked].add(query_back)
    token_ln, gain_one_grad, bias_one_grad = layer_norm_back(
        normed_grad_one, unit_one, inverse_one, norm_wide[0]
    )
    tokens_grad = token_ln.at[picked].add(middle_grad)
    grad_qkv = jnp.stack([grad_query_w, grad_key_w, grad_value_w])
    grad_norm = jnp.stack([gain_one_grad, bias_one_grad, gain_two_grad, bias_two_grad])
    first_qkv, first_out, first_in, first_down, first_norm = (
        lax.psum_scatter(grad_qkv, "batch", scatter_dimension=1, tiled=True),
        lax.psum_scatter(grad_out, "batch", scatter_dimension=0, tiled=True),
        lax.psum_scatter(grad_in, "batch", scatter_dimension=0, tiled=True),
        lax.psum_scatter(grad_down, "batch", scatter_dimension=1, tiled=True),
        lax.psum_scatter(grad_norm, "batch", scatter_dimension=1, tiled=True),
    )
    owned = (
        lax.psum_scatter(
            first_qkv.astype(jnp.bfloat16), "seq", scatter_dimension=2, tiled=True
        ).astype(jnp.float32),
        lax.psum_scatter(
            first_out.astype(jnp.bfloat16), "seq", scatter_dimension=1, tiled=True
        ).astype(jnp.float32),
        lax.psum_scatter(
            first_in.astype(jnp.bfloat16), "seq", scatter_dimension=1, tiled=True
        ).astype(jnp.float32),
        lax.psum_scatter(
            first_down.astype(jnp.bfloat16), "seq", scatter_dimension=0, tiled=True
        ).astype(jnp.float32),
        lax.psum_scatter(
            first_norm.astype(jnp.bfloat16), "seq", scatter_dimension=0, tiled=True
        ).astype(jnp.float32),
    )
    return (result[None], tokens_grad[None], owned[0], owned[1], owned[2], owned[3], owned[4])


MESH = pl.DeviceIdType.MESH
LOW = jnp.bfloat16
WIDE = jnp.float32
LOG2E = 1.4426950408889634
ROOT_HALF = 0.7071067811865476
PDF_SCALE = 0.3989422804014327
PAD = 16


def own_step(order, j):
    n = len(order)
    return n + j if order[-1] == "y" else n + 1 + j % 2


def scatter_shapes(order, nz, bd, lanes):
    shapes = [(nz, 2, bd, lanes)] * 2
    sides, tall, pair = 2, (nz,), (2,)
    for ax in order:
        if ax == "z":
            tall = ()
            shapes += [pair + (bd, lanes)] * (sides * (nz - 1))
        elif ax == "x":
            pair = ()
            shapes += [tall + (bd, lanes)] * sides
        elif ax == "y":
            sides = 1
            shapes += [tall + pair + (bd, lanes)]
        else:
            sides, pair = 1, ()
            shapes += [tall + (bd, lanes)] * 3
    return shapes


KIND = {
    "kv": "zR",
    "qo": "xzy",
    "w1a": "zxy",
    "w1b": "yxz",
    "w2a": "zxy",
    "w2b": "zyx",
    "g2a": "zyx",
    "g2b": "yxz",
    "g1a": "xyz",
    "g1b": "zR",
    "qog": "xyz",
    "kg": "Rz",
    "vg": "Rz",
}
EARLY = 2
PLAN = (
    ("norm", "kv", ),
    ("qo", ),
    (),
    ("w1b", "w2b", "qo", "kv", ),
    (),
    ("w1a", "w1b", "w2b", ),
    (),
    ("qo", ),
    ("w2a", ),
    ("w1b", ),
    ("qo", "w1a", ),
    ("w2b", ),
    (),
    ("ar1a", "ar1b", ),
    (),
    ("ar1a", "ar1b", "w2a", ),
    ("w1a", ),
    (),
    ("w1a", "w2a", ),
    ("w2b", ),
    (),
    ("w1b", "w2a", ),
    (),
    ("w1a", "w2b", ),
    (),
    ("w1a", ),
    ("g2a", ),
    (),
    ("w2a", ),
    ("g2a", ),
    (),
    ("g1a", "g1b", ),
    ("ar2a", ),
    ("ar2b", ),
    ("g2b", "ar2a", "ar2b", "g1a", "g1b", ),
    ("qog", ),
    ("g2b", ),
    ("ar2a", "ar2b", "qog", ),
    ("ar2a", "ar2b", ),
    (),
    ("g1a", ),
    (),
    ("g2a", "g2b", ),
    (),
    (),
    ("qog", ),
    ("kg", "vg", "g1a", ),
    ("g2a", "g2b", ),
    ("kg", "vg", ),
    ("g2a", "qog", ),
    ("g1b", ),
    (),
    ("ngs", ),
    ("g1a", "ngs", ),
    ("kg", "vg", "g2b", "g1b", "ngs", "qog", ),
    ("ngs", ),
    ("ngs", ),
)


def dot_over(a, b, ca, cb):
    return lax.dot_general(a, b, (((ca,), (cb,)), ((), ())), preferred_element_type=WIDE)


def nn(a, b):
    return dot_over(a, b, 1, 0)


def nt(a, b):
    return dot_over(a, b, 1, 1)


def turn(a):
    if a.dtype == LOW:
        return a.astype(WIDE).T.astype(LOW)
    return a.T


def flat(a):
    return a.reshape(-1, a.shape[-1])


def unit_norm(x):
    cen = x - jnp.mean(x, axis=-1, keepdims=True)
    inv = lax.rsqrt(jnp.mean(cen * cen, axis=-1, keepdims=True) + EPS)
    return cen * inv, inv


def norm_back(incoming, unit, inv, gain):
    e = incoming * gain
    mean_e = jnp.mean(e, axis=-1, keepdims=True)
    mean_eu = jnp.mean(e * unit, axis=-1, keepdims=True)
    return inv * (e - mean_e - unit * mean_eu)


def features(proj, u_low, scale, feat):
    wide = u_low.astype(WIDE)
    sq = jnp.sum(wide * wide, axis=0, keepdims=True)
    shift = (0.5 * scale * scale * LOG2E) * sq
    half_log = 0.5 * (feat.bit_length() - 1)
    return jnp.exp2((scale * LOG2E) * proj - (shift + half_log))


class Wires:
    def __init__(self, send_sems, recv_sems):
        self.send_sems, self.recv_sems, self.used, self.sent = send_sems, recv_sems, 0, []

    def send(self, src, dst, dev):
        c = pltpu.make_async_remote_copy(
            src_ref=src,
            dst_ref=dst,
            send_sem=self.send_sems.at[self.used],
            recv_sem=self.recv_sems.at[self.used],
            device_id=dev,
            device_id_type=MESH,
        )
        self.used += 1
        c.start()
        self.sent.append(c)
        return c

    def left(self, copies):
        for c in copies:
            c.wait_send()
            self.sent = [o for o in self.sent if o is not c]

    def drain(self):
        self.left(list(self.sent))


def arrived(copies):
    for c in copies:
        c.wait_recv()


def layer_kernel(
    nz,
    ns,
    tok_in,
    wqkv_in,
    wo_in,
    win_in,
    wdn_in,
    nrm_in,
    rf_in,
    ls,
    pos,
    cnt,
    mg_in,
    mixed_out,
    tgrad_out,
    gqkv,
    gop,
    gin,
    gdn,
    gnorm,
    tok,
    rf,
    mg,
    w0,
    w1,
    w2,
    nb,
    wkvt,
    wqt,
    wo,
    xnt,
    kvt,
    vs,
    kft,
    pm,
    posc,
    rft,
    sumf,
    loc,
    ar_a,
    ar_r1,
    ar_r2,
    ar_f,
    dsumt,
    qrt,
    qfr,
    num_r,
    den_r,
    dn_st,
    hot,
    hort,
    dmid_low,
    xnrt,
    dqt,
    dhd,
    dxqt,
    g0,
    g1,
    g2,
    ng_a,
    ng_r,
    mixed_v,
    tgrad_v,
    send_sems,
    recv_sems,
    out_sems,
    *scatter_refs,
):
    rows, width = tok.shape
    slots = mg.shape[0]
    heads, size, feat = rf.shape
    scale = size**-0.25
    bd = w0.shape[3]
    sw = wqkv_in.shape[2]
    tile = 256
    wide_tile = 512
    b = lax.axis_index("batch")
    s = lax.axis_index("seq")
    x = lax.rem(b, 2)
    z = b // 2
    c = lax.rem(s, 2)
    y = s // 2
    s_core = s + 1 - 2 * c
    s_y = s + 2 - 4 * y
    s_far = s_core + 2 - 4 * y
    to_core = (b, s_core)
    to_y = (b, s_y)
    to_x = (b + 1 - 2 * x, s)
    to_z = [(lax.rem(z + k, nz) * 2 + x, s) for k in range(1, nz)]
    to_diag = [(lax.rem(z + k, nz) * 2 + 1 - x, s) for k in range(1, nz)]
    to_xy = (b + 1 - 2 * x, s_y)
    to_plane = to_z + [to_x] + to_diag
    to_seq = [to_core, to_y, (b, s_far)]
    wires = Wires(send_sems, recv_sems)

    shards = (
        (wqkv_in.at[1], w0.at[s, z, x, :, 0:sw]),
        (wqkv_in.at[2], w0.at[s, z, x, :, sw : 2 * sw]),
        (wqkv_in.at[0], w0.at[s, z, x, :, 2 * sw : 3 * sw]),
        (wo_in, w0.at[s, z, x, :, 3 * sw : 4 * sw]),
        (win_in, w1.at[s, z, x]),
        (wdn_in, w2.at[s, z, x]),
        (rf_in, rf),
        (tok_in, tok),
        (mg_in, mg),
    )
    loads = [pltpu.make_async_copy(a, o, out_sems.at[2 + n]) for n, (a, o) in enumerate(shards)]
    for load in loads:
        load.start()
    barrier = pltpu.get_barrier_semaphore()
    partners = to_plane + to_seq + [to_xy]
    for dev in partners:
        pl.semaphore_signal(barrier, inc=1, device_id=dev, device_id_type=MESH)

    place = (
        lax.broadcasted_iota(jnp.int32, (bd, 2 * bd), 1)
        == lax.broadcasted_iota(jnp.int32, (bd, 2 * bd), 0) + bd * x
    )
    nb[s, z, x] = nn(
        jnp.broadcast_to(nrm_in[...], (PAD, bd)), jnp.where(place, 1.0, 0.0).astype(LOW)
    ).astype(LOW)
    seq_pos = s * rows
    long_from = ls[0, 0]
    long_to = long_from + ns * rows - SHORT
    blocks = [s, s_core, s_y, s_far]

    def shared_mask(position):
        at = position + seq_pos
        return jnp.where((at >= long_from) & (at < long_to), 1.0, 0.0)

    def tiles(lo, hi, step):
        def body(t, carry):
            step(t)
            return carry

        lax.fori_loop(lo, hi, body, 0)

    pos_row = pos[...]
    posc[...] = jnp.broadcast_to(pos_row.astype(WIDE), (128, slots)).T
    sh_r = shared_mask(pos_row)

    def select_tile(t):
        at = pl.multiple_of(t * tile, tile)
        for j in range(tile // 128):
            lane = lax.broadcasted_iota(jnp.int32, (slots, 128), 1) + (at + 128 * j)
            pm[:, pl.ds(at + 128 * j, 128)] = jnp.where(
                lane.astype(WIDE) == posc[...], 1.0, 0.0
            ).astype(LOW)
        lane = lax.broadcasted_iota(jnp.int32, (1, tile), 1) + at
        sh = shared_mask(lane)
        row = lax.broadcasted_iota(jnp.int32, (PAD, tile), 0)
        ones = jnp.where(row == 0, sh, jnp.where(row == 1, 1.0 - sh, 0.0)).astype(LOW)
        for h in range(heads):
            vs[h, 2 * size : 2 * size + PAD, pl.ds(at, tile)] = ones

    tiles(0, rows // tile, select_tile)
    for load in loads[:7]:
        load.wait()
    for h in range(heads):
        rft[h] = turn(rf[h])
    pl.semaphore_wait(barrier, len(partners))

    tasks, steps = {}, {}
    plan = list(PLAN)

    def go(name):
        steps[name] += 1
        next(tasks[name], None)

    def poll():
        for name in plan.pop(0) if plan else ():
            go(name)

    def need(name, step):
        while steps[name] < step:
            go(name)

    def gather_norm():
        at = nb.at[s, z, x]
        first = [wires.send(at, at, dev) for dev in to_plane]
        yield
        arrived(first)
        at = nb.at[s]
        second = [wires.send(at, at, dev) for dev in to_seq]
        yield
        arrived(second)
        yield

    every = slice(None)

    def gather(ref, lo, hi, order):
        sides, zi, xi = [s], z, x
        early = order[-1] == "y"
        near, now = [], []
        for ax in order:
            if ax == "z":
                for side in sides:
                    at = ref.at[side, z, xi, :, lo:hi]
                    now += [wires.send(at, at, dev) for dev in to_z]
                zi = every
            elif ax == "x":
                for side in sides:
                    at = ref.at[side, zi, x, :, lo:hi]
                    now.append(wires.send(at, at, to_x))
                xi = every
            elif ax == "y":
                at = ref.at[s, zi, xi, :, lo:hi]
                now.append(wires.send(at, at, to_y))
                if early:
                    near = [wires.send(at, at, to_core)]
                sides = [s, s_y]
            else:
                at = ref.at[s, zi, x, :, lo:hi]
                now += [wires.send(at, at, dev) for dev in (to_x, to_y, to_xy)]
                xi, sides = every, [s, s_y]
            yield
            if near:
                arrived(near)
                yield
            arrived(now)
            now = []
        for side in [s_y] if early else [s, s_y]:
            at = ref.at[side, :, :, :, lo:hi]
            now.append(wires.send(at, at, to_core))
        yield
        arrived(now)
        yield

    def reduce_seq(k, v):
        r1, r2, f = ar_r1.at[k, v], ar_r2.at[k, v], ar_f.at[k]
        mine = 2 * v + c
        now = [wires.send(ar_a.at[2 * v + 1 - c], r1, to_core)]
        yield
        arrived(now)
        wires.left(now)
        ar_a[mine] = ar_a[mine] + r1[...]
        now = [wires.send(ar_a.at[mine], r2, to_y)]
        yield
        arrived(now)
        wires.left(now)
        f[mine] = ar_a[mine] + r2[...]
        now = [wires.send(f.at[mine], f.at[mine], to_core)]
        yield
        arrived(now)
        yield

    def add_into(g, side, zi, xi, lo, hi, got):
        if zi is every:

            def add(j, carry):
                at = (side, j, xi, every, slice(lo, hi))
                g[at] = g[at] + got[j]
                return carry

            lax.fori_loop(0, nz, add, 0)
        else:
            at = (side, zi, xi, every, slice(lo, hi))
            g[at] = g[at] + got[...]

    last_parts = {}

    def scatter(name, g, lo, hi, order, bufs):
        bufs = list(bufs)
        sides, zi, xi = [c, 2 + c], every, every
        now = [wires.send(g.at[2 * v + 1 - c, :, :, :, lo:hi], bufs[v], to_core) for v in range(2)]
        yield
        arrived(now)
        for v in range(2):
            add_into(g, sides[v], zi, xi, lo, hi, bufs[v])
        bufs = bufs[2:]
        for n, ax in enumerate(order):
            jobs = []
            if ax == "z":
                for side in sides:
                    for k in range(1, nz):
                        at = g.at[side, lax.rem(z + k, nz), xi, :, lo:hi]
                        jobs.append((at, to_z[k - 1], side))
                zi = z
            elif ax == "x":
                for side in sides:
                    jobs.append((g.at[side, zi, 1 - x, :, lo:hi], to_x, side))
                xi = x
            elif ax == "y":
                jobs.append((g.at[s_y, zi, xi, :, lo:hi], to_y, s))
                sides = [s]
            else:
                jobs.append((g.at[s, zi, 1 - x, :, lo:hi], to_x, s))
                jobs.append((g.at[s_y, zi, x, :, lo:hi], to_y, s))
                jobs.append((g.at[s_y, zi, 1 - x, :, lo:hi], to_xy, s))
                xi, sides = x, [s]
            got, bufs = bufs[: len(jobs)], bufs[len(jobs) :]
            now = [wires.send(at, buf, dev) for (at, dev, _), buf in zip(jobs, got)]
            yield
            arrived(now)
            if n < len(order) - 1:
                for (_, _, side), buf in zip(jobs, got):
                    add_into(g, side, zi, xi, lo, hi, buf)
            else:
                last_parts[name] = (g, lo, hi, got)
        yield

    def scattered(name):
        g, lo, hi, got = last_parts[name]
        total = g[s, z, x, :, lo:hi].astype(WIDE)
        for buf in got:
            total = total + buf[...].astype(WIDE)
        return total

    def add_task(name, task):
        tasks[name], steps[name] = task, 0

    half = w1.shape[4] // 2
    add_task("norm", gather_norm())
    add_task("kv", gather(w0, 0, 2 * sw, KIND["kv"]))
    add_task("qo", gather(w0, 2 * sw, 4 * sw, KIND["qo"]))
    for name, ref in (("w1", w1), ("w2", w2)):
        add_task(name + "a", gather(ref, 0, half, KIND[name + "a"]))
        add_task(name + "b", gather(ref, half, 2 * half, KIND[name + "b"]))
    for k in range(2):
        for v in range(2):
            add_task("ar%d%s" % (k + 1, "ab"[v]), reduce_seq(k, v))
    spare = list(scatter_refs)
    for name, g, lo, hi in scatter_parts(g0, g1, g2, sw, half):
        count = len(scatter_shapes(KIND[name], nz, bd, hi - lo))
        add_task(name, scatter(name, g, lo, hi, KIND[name], spare[:count]))
        spare = spare[count:]

    def own_ready(name, j):
        need(name, own_step(KIND[name], j))

    poll()

    loads[7].wait()
    toks_r = nn(pm[...], tok[...])
    poll()
    need("norm", 2)
    unit_r, _ = unit_norm(toks_r)
    poll()
    need("norm", 3)

    def norm_row(i):
        return jnp.concatenate(
            [
                (nb[i, j, 0, 0:1, :] + nb[i, j, 1, 0:1, :]).astype(WIDE)
                for j in range(nz)
            ],
            axis=1,
        )

    gain1, bias1, gain2, bias2 = [norm_row(i) for i in range(4)]
    xn_r = (unit_r * gain1 + bias1).astype(LOW)
    xnrt[...] = turn(xn_r)

    for n in range(2):
        cols = slice(n * rows // 2, (n + 1) * rows // 2)
        unit, _ = unit_norm(tok[cols, :].astype(WIDE))
        xnt[:, cols] = turn((unit * gain1 + bias1).astype(LOW))
        poll()

    sh_all = shared_mask(lax.broadcasted_iota(jnp.int32, (1, rows), 1))
    sh_low = sh_all.astype(LOW)

    def kv_features(sd):
        r = nn(wkvt[sd], xnt[...]).astype(LOW)
        kvt[sd] = r
        for i in range(2):
            h = 2 * sd + i
            k_h = r[size * i : size * (i + 1)]
            v_h = r[sw + size * i : sw + size * (i + 1)]
            kft[h] = features(nn(rft[h], k_h), k_h, scale, feat).astype(LOW)
            vs[h, 0:size, :] = v_h * sh_low
            vs[h, size : 2 * size, :] = v_h * (1.0 - sh_low)

    def kv_sums(sd):
        for i in range(2):
            h = 2 * sd + i
            part = nt(vs[h], kft[h]).astype(LOW)
            ar_a[sd, i, 0:size, :] = part[0:size]
            ar_a[sd, i, size : size + PAD, :] = part[2 * size :]
            loc[h] = part[size:]

    for j, sd in enumerate(blocks):
        own_ready("kv", j)
        wkvt[sd] = turn(flat(w0[sd, :, :, :, 0 : 2 * sw]))
        kv_features(sd)
        poll()
        kv_sums(sd)
        poll()
    poll()

    keep = (g0, g1, g2)

    def q_block(sd):
        wqt[sd] = turn(flat(w0[sd, :, :, :, 2 * sw : 3 * sw]))
        q = nn(wqt[sd], xnt[...]).astype(LOW)
        for i in range(2):
            q_h = q[size * i : size * (i + 1)]
            qf = features(nn(rft[2 * sd + i], q_h), q_h, scale, feat).astype(LOW)
            for t, gt in enumerate(keep):
                part = qf[:, t * wide_tile : (t + 1) * wide_tile]
                gt[sd, 2 * i : 2 * i + 2] = part.reshape((2,) + g0.shape[2:4] + (wide_tile,))
        q = nn(wqt[sd], xnrt[...]).astype(LOW)
        for i in range(2):
            q_h = q[size * i : size * (i + 1)]
            qrt[2 * sd + i] = q_h
            qfr[2 * sd + i] = features(nn(rft[2 * sd + i], q_h), q_h, scale, feat).astype(LOW)

    for j, sd in enumerate(blocks):
        own_ready("qo", j)
        q_block(sd)
        poll()
    for step in range(1, 5):
        need("ar1a", step)
        need("ar1b", step)

    def tail_rows(k, h):
        first = lax.broadcasted_iota(jnp.int32, (PAD, feat), 0) == 0
        return jnp.where(
            first,
            ar_f[k, h // 2, h % 2, size : size + PAD, :].astype(WIDE),
            loc[h, size : size + PAD, :].astype(WIDE),
        ).astype(LOW)

    for h in range(heads):
        sumf[h, 0:size, :] = ar_f[0, h // 2, h % 2, 0:size, :]
        sumf[h, size : 2 * size, :] = loc[h, 0:size, :]
        sumf[h, 2 * size : 2 * size + PAD, :] = tail_rows(0, h)

    def split_ratio(nd, sh):
        pick = jnp.broadcast_to(sh, (size, sh.shape[1])) > 0.5
        num = jnp.where(pick, nd[0:size], nd[size : 2 * size])
        den = jnp.where(sh > 0.5, nd[2 * size : 2 * size + 1], nd[2 * size + 1 : 2 * size + 2])
        return num, den

    for h in range(heads):
        num, den = split_ratio(nn(sumf[h], qfr[h]), sh_r)
        num_r[h] = num
        den_r[h] = jnp.broadcast_to(den, (8, slots))
        hort[size * h : size * (h + 1), :] = (num * (1.0 / den)).astype(LOW)
    poll()

    for t, gt in enumerate(keep):
        cols = slice(t * wide_tile, (t + 1) * wide_tile)
        for h in range(heads):
            i, jj = h // 2, h % 2
            qf = gt[i, 2 * jj : 2 * jj + 2].reshape(feat, wide_tile)
            num, den = split_ratio(nn(sumf[h], qf), sh_all[:, cols])
            hot[h, :, cols] = (num * (1.0 / den)).astype(LOW)
        poll()

    for i in range(ns):
        wo[:, sw * i : sw * (i + 1)] = flat(w0[i, :, :, :, 3 * sw : 4 * sw])
    middle_r = toks_r + nn(turn(hort[...]), wo[...])
    unit2, inv2 = unit_norm(middle_r)
    xn2_r = (unit2 * gain2 + bias2).astype(LOW)
    xn2_rt = turn(xn2_r)
    slot_id = lax.broadcasted_iota(jnp.int32, (slots, 1), 0)
    loads[8].wait()
    cot = mg[...].astype(WIDE) * jnp.where(slot_id < cnt[0, 0], 1.0, 0.0)
    cot_low = cot.astype(LOW)
    cot_t = turn(cot_low)
    poll()

    for j, sd in enumerate(blocks):
        for name in ("w1a", "w1b"):
            own_ready(name, j)
        upper = nn(xn2_r, flat(w1[sd]))
        cdf = 0.5 + 0.5 * lax.erf(upper * ROOT_HALF)
        act = (upper * cdf).astype(LOW)
        slope = cdf + upper * (PDF_SCALE * jnp.exp2((-0.5 * LOG2E) * (upper * upper)))
        tgrad_v[slots * j : slots * (j + 1), :] = slope
        g2[sd] = nn(cot_t, act).astype(LOW).reshape(g2.shape[1:])
        poll()
    dn2 = jnp.zeros((slots, width), WIDE)
    for j, sd in enumerate(blocks):
        for name in ("w2a", "w2b"):
            own_ready(name, j)
        slope = tgrad_v[slots * j : slots * (j + 1), :]
        du = (nn(cot_low, flat(w2[sd])) * slope).astype(LOW)
        g1[sd] = nn(xn2_rt, du).astype(LOW).reshape(g1.shape[1:])
        dn2 = dn2 + nt(du, flat(w1[sd]))
        poll()
    poll()

    norm_g2 = jnp.sum(dn2 * unit2, axis=0, keepdims=True)
    norm_g3 = jnp.sum(dn2, axis=0, keepdims=True)
    d_att = (cot + norm_back(dn2, unit2, inv2, gain2)).astype(LOW)
    dmid_low[...] = d_att
    dhd[...] = nt(wo[...], d_att)
    for h in range(heads):
        dh = dhd[size * h : size * (h + 1), :]
        rden = 1.0 / den_r[h, 0:1, :]
        d_num = (dh * rden).astype(LOW)
        d_den = (-jnp.sum(dh * num_r[h], axis=0, keepdims=True) * (rden * rden)).astype(LOW)
        shl = sh_r.astype(LOW)
        dn_st[h, 0:size, :] = d_num * shl
        dn_st[h, size : 2 * size, :] = d_num * (1.0 - shl)
        row = lax.broadcasted_iota(jnp.int32, (PAD, slots), 0)
        dd = jnp.broadcast_to(d_den.astype(WIDE), (PAD, slots))
        dn_st[h, 2 * size : 2 * size + PAD, :] = jnp.where(
            row == 0, dd * sh_r, jnp.where(row == 1, dd * (1.0 - sh_r), 0.0)
        ).astype(LOW)
        part = nt(dn_st[h], qfr[h]).astype(LOW)
        ar_a[h // 2, h % 2, 0:size, :] = part[0:size]
        ar_a[h // 2, h % 2, size : size + PAD, :] = part[2 * size :]
        loc[h] = part[size:]
        if h == heads // 2 - 1:
            poll()
    poll()

    for h in range(heads):
        d_qf = nn(turn(sumf[h]), dn_st[h])
        w = d_qf * qfr[h].astype(WIDE)
        ws = jnp.sum(w, axis=0, keepdims=True)
        q_h = qrt[h].astype(WIDE)
        dqt[size * h : size * (h + 1), :] = (
            scale * nn(rf[h], w.astype(LOW)) - (scale * scale) * q_h * ws
        ).astype(LOW)
    poll()
    grad_q = nt(xnrt[...], dqt[...]).astype(LOW)
    grad_o = nn(hort[...], dmid_low[...]).astype(LOW)
    for i in range(ns):
        for n, part in enumerate((grad_q, grad_o)):
            part = part[:, sw * i : sw * (i + 1)]
            g0[i, :, :, :, (2 + n) * sw : (3 + n) * sw] = part.reshape(g0.shape[1:4] + (sw,))
    poll()
    acc = jnp.zeros((width, slots), WIDE)
    for i in range(ns):
        acc = acc + nn(flat(w0[i, :, :, :, 2 * sw : 3 * sw]), dqt[sw * i : sw * (i + 1), :])
    dxqt[...] = acc.astype(LOW)
    poll()

    def dense_tile(t):
        cols = slice(t * wide_tile, (t + 1) * wide_tile)
        ho = turn(flat(hot[:, :, cols]))
        mid = tok[cols, :].astype(WIDE) + nn(ho, wo[...])
        unit, _ = unit_norm(mid)
        xn2 = (unit * gain2 + bias2).astype(LOW)
        total = mid
        for i in range(ns):
            up = nn(xn2, flat(w1[i]))
            act = (up * (0.5 + 0.5 * lax.erf(up * ROOT_HALF))).astype(LOW)
            total = total + nt(act, flat(w2[i]))
            if i == 1:
                yield
        mixed_v[cols, :] = total.astype(LOW)
        yield

    def dense_pieces():
        for t in range(rows // wide_tile):
            yield from dense_tile(t)

    dense = dense_pieces()

    def dense_some(count):
        for _ in range(count):
            next(dense)
            poll()

    dense_some(EARLY)
    def key_sums(v):
        for h in range(4 * v, 4 * v + 4):
            stack = jnp.concatenate(
                [ar_f[1, h // 2, h % 2, 0:size, :], loc[h, 0:size, :], tail_rows(1, h)], axis=0
            )
            ar_a[h // 2, h % 2, 0:size, :] = stack[0:size]
            dsumt[h] = turn(stack)

    def key_block(sd):
        for i in range(2):
            h = 2 * sd + i
            w = nn(dsumt[h], vs[h]) * kft[h].astype(WIDE)
            ws = jnp.sum(w, axis=0, keepdims=True)
            k_h = kvt[sd, size * i : size * (i + 1), :].astype(WIDE)
            dk = scale * nn(rf[h], w.astype(LOW)) - (scale * scale) * k_h * ws
            both = nn(jnp.concatenate([ar_a[sd, i, 0:size, :], loc[h, 0:size, :]], axis=0), kft[h])
            pick = jnp.broadcast_to(sh_all, (size, rows)) > 0.5
            kvt[sd, size * i : size * (i + 1), :] = dk.astype(LOW)
            kvt[sd, sw + size * i : sw + size * (i + 1), :] = jnp.where(
                pick, both[0:size], both[size:]
            ).astype(LOW)

    for v in range(2):
        need("ar2" + "ab"[v], 4)
        key_sums(v)
        poll()
        for sd in (2 * v + 1 - c, 2 * v + c):
            key_block(sd)
            poll()
            part = nt(xnt[...], kvt[sd]).astype(LOW)
            g0[sd, :, :, :, 0 : 2 * sw] = part.reshape(g0.shape[1:4] + (2 * sw,))
            poll()

    ng_a[...] = jnp.zeros(ng_a.shape, WIDE)

    def token_tile(t):
        cols = slice(t * wide_tile, (t + 1) * wide_tile)
        dxt = nn(dxqt[...], pm[:, cols])
        for i in range(ns):
            dxt = dxt + nn(flat(w0[i, :, :, :, 0 : 2 * sw]), kvt[i, :, cols])
        dx = dxt.T
        unit, inv = unit_norm(tok[cols, :].astype(WIDE))
        tgrad_v[cols, :] = norm_back(dx, unit, inv, gain1) + nn(turn(pm[:, cols]), dmid_low[...])
        ng_a[0:1, :] += jnp.sum(dx * unit, axis=0, keepdims=True)
        ng_a[1:2, :] += jnp.sum(dx, axis=0, keepdims=True)

    for n in range(rows // wide_tile):
        token_tile(n)
        poll()
    out_t = pltpu.make_async_copy(tgrad_v, tgrad_out, out_sems.at[0])
    out_t.start()
    ng_a[2:3, :] = norm_g2
    ng_a[3:4, :] = norm_g3

    def sum_norm():
        order = [([to_core], 0), ([to_y], 1), ([to_x], 2), (to_z, 3)]
        for devs, k in order:
            now = [wires.send(ng_a, ng_r.at[k + n], dev) for n, dev in enumerate(devs)]
            yield
            arrived(now)
            wires.left(now)
            for n in range(len(devs)):
                ng_a[...] += ng_r[k + n]
        yield

    add_task("ngs", sum_norm())
    poll()
    dense_some(2 * (rows // wide_tile) - EARLY)
    out_m = pltpu.make_async_copy(mixed_v, mixed_out, out_sems.at[1])
    out_m.start()

    for step in range(1, 6):
        for name in ("g2a", "g2b", "g1a", "g1b", "qog"):
            need(name, step)
    gin[:, 0:half] = scattered("g1a")
    gin[:, half:] = scattered("g1b")
    gdn[:, 0:half] = scattered("g2a")
    gdn[:, half:] = scattered("g2b")
    qo = scattered("qog")
    gqkv[0] = qo[:, 0:sw]
    gop[...] = qo[:, sw : 2 * sw]
    for step in range(1, 6):
        need("kg", step)
        need("vg", step)
        need("ngs", step)
    gqkv[1] = scattered("kg")
    gqkv[2] = scattered("vg")
    total = ng_a[...]
    row = lax.broadcasted_iota(jnp.int32, total.shape, 0)
    mine = jnp.sum(jnp.where(row == s, total, 0.0), axis=0, keepdims=True)
    mine = jnp.broadcast_to(mine, total.shape)
    gnorm[...] = pltpu.roll(mine, lax.rem(width - bd * b, width), 1)[0:1, 0:bd]
    assert not plan
    wires.drain()
    out_t.wait()
    out_m.wait()


def scatter_parts(g0, g1, g2, sw, half):
    return (
        ("g1a", g1, 0, half),
        ("g1b", g1, half, 2 * half),
        ("g2a", g2, 0, half),
        ("g2b", g2, half, 2 * half),
        ("qog", g0, 2 * sw, 4 * sw),
        ("kg", g0, 0, sw),
        ("vg", g0, sw, 2 * sw),
    )


def fits(mesh, args):
    tokens, qkv_weight, _, in_weight, _, _, rand_features = args[:7]
    nbat, ns = mesh.shape["batch"], mesh.shape["seq"]
    bd, sw = qkv_weight.shape[1], qkv_weight.shape[2]
    rows, width = tokens.shape[1], tokens.shape[2]
    heads, size, feat = rand_features.shape
    return (
        ns == 4
        and nbat == 8
        and tokens.shape[0] == 1
        and bd % 64 == 0
        and sw == 2 * size
        and in_weight.shape[1] == 4 * sw
        and heads == 2 * ns
        and rows == 3 * 512
        and args[10].shape[1] * ns == rows
        and in_weight.shape[1] == width
        and feat == 256
    )


def fused_layer(
    nbat,
    ns,
    tokens,
    qkv_weight,
    out_proj,
    in_weight,
    out_weight,
    norm_params,
    rand_features,
    long_start,
    masked_pos,
    masked_count,
    masked_grad,
):
    nz = nbat // 2
    rows, width = tokens.shape[1], tokens.shape[2]
    slots = masked_grad.shape[1]
    heads, size, feat = rand_features.shape
    bd, sw = qkv_weight.shape[1], qkv_weight.shape[2]
    fw = in_weight.shape[1]
    stack = 2 * size + PAD
    low = lambda *shape: pltpu.VMEM(shape, LOW)
    wide = lambda *shape: pltpu.VMEM(shape, WIDE)
    vmem = pl.BlockSpec(memory_space=pltpu.VMEM)
    smem = pl.BlockSpec(memory_space=pltpu.SMEM)
    anywhere = pl.BlockSpec(memory_space=pl.ANY)
    tall = (nz, 2, bd)
    scratch = [
        low(rows, width),
        low(heads, size, feat),
        low(slots, width),
        low(ns, *tall, 4 * sw),
        low(ns, *tall, fw),
        low(ns, *tall, fw),
        low(ns, nz, 2, PAD, 2 * bd),
        low(ns, 2 * sw, width),
        low(ns, sw, width),
        low(width, width),
        low(width, rows),
        low(ns, 2 * sw, rows),
        low(heads, stack, rows),
        low(heads, feat, rows),
        low(slots, rows),
        wide(slots, 128),
        low(heads, feat, size),
        low(heads, stack, feat),
        low(heads, size + PAD, feat),
        low(ns, 2, size + PAD, feat),
        low(2, 2, 2, size + PAD, feat),
        low(2, 2, 2, size + PAD, feat),
        low(2, ns, 2, size + PAD, feat),
        low(heads, feat, stack),
        low(heads, size, slots),
        low(heads, feat, slots),
        wide(heads, size, slots),
        wide(heads, 8, slots),
        low(heads, stack, slots),
        low(heads, size, rows),
        low(width, slots),
        low(slots, width),
        low(width, slots),
        low(width, slots),
        wide(width, slots),
        low(width, slots),
        low(ns, *tall, 4 * sw),
        low(ns, *tall, fw),
        low(ns, *tall, fw),
        wide(8, width),
        wide(2 + nz, 8, width),
        low(rows, width),
        wide(rows, width),
        pltpu.SemaphoreType.DMA((224,)),
        pltpu.SemaphoreType.DMA((224,)),
        pltpu.SemaphoreType.DMA((11,)),
    ]
    for name, _, lo, hi in scatter_parts(None, None, None, sw, fw // 2):
        scratch += [low(*shape) for shape in scatter_shapes(KIND[name], nz, bd, hi - lo)]
    f32 = lambda *shape: jax.ShapeDtypeStruct(shape, WIDE)
    outs = pl.pallas_call(
        functools.partial(layer_kernel, nz, ns),
        out_shape=(
            jax.ShapeDtypeStruct((rows, width), LOW),
            f32(rows, width),
            f32(3, bd, sw),
            f32(bd, sw),
            f32(bd, fw),
            f32(bd, fw),
            f32(1, bd),
        ),
        in_specs=[anywhere] * 5 + [vmem, anywhere, smem, vmem, smem, anywhere],
        out_specs=(anywhere, anywhere, vmem, vmem, vmem, vmem, vmem),
        scratch_shapes=scratch,
        compiler_params=pltpu.CompilerParams(
            collective_id=0, has_side_effects=True, vmem_limit_bytes=62 * 2**20
        ),
        name="layer",
    )(
        tokens.reshape(rows, width),
        qkv_weight,
        out_proj,
        in_weight,
        out_weight.T,
        norm_params,
        rand_features,
        long_start.reshape(1, 1),
        masked_pos,
        masked_count,
        masked_grad.reshape(slots, width),
    )
    return (outs[0][None], outs[1][None]) + outs[2:5] + (outs[5].T, outs[6])


def solution(mesh):
    def body(*args):
        if fits(mesh, args):
            return fused_layer(mesh.shape["batch"], mesh.shape["seq"], *args)
        return on_device(*args)

    placed = (
        P("batch", "seq", None),
        P(None, "batch", "seq"),
        P("batch", "seq"),
        P("batch", "seq"),
        P("seq", "batch"),
        P("seq", "batch"),
        P(),
        P("batch"),
        P("batch", "seq"),
        P("batch", "seq"),
        P("batch", "seq", None),
    )
    return jax.shard_map(
        body,
        mesh=mesh,
        in_specs=placed,
        out_specs=(
            P("batch", "seq", None),
            P("batch", "seq", None),
            P(None, "batch", "seq"),
            P("batch", "seq"),
            P("batch", "seq"),
            P("seq", "batch"),
            P("seq", "batch"),
        ),
        check_vma=False,
    )
```

```python
import functools

import jax
import jax.numpy as jnp
from jax import lax
from jax.experimental import pallas as pl
from jax.experimental.pallas import tpu as pltpu
from jax.sharding import PartitionSpec as P

SHORT = 1024


EPS = 1e-05


def layer_norm_parts(values, gain_row, shift_row):
    row_mean = jnp.mean(values, axis=-1, keepdims=True)
    centred = values - row_mean
    row_var = jnp.mean(centred * centred, axis=-1, keepdims=True)
    inverse = lax.rsqrt(row_var + EPS)
    unit_rows = centred * inverse
    return (unit_rows * gain_row + shift_row, unit_rows, inverse)


def layer_norm_back(incoming, unit_rows, inverse, gain_row):
    scaled = incoming * gain_row
    inner = (
        scaled
        - jnp.mean(scaled, axis=-1, keepdims=True)
        - unit_rows * jnp.mean(scaled * unit_rows, axis=-1, keepdims=True)
    )
    return (inner * inverse, jnp.sum(incoming * unit_rows, axis=0), jnp.sum(incoming, axis=0))


def exact_gelu(values):
    return jax.nn.gelu(values, approximate=False)


def positive_raw(values, feature_dirs):
    feat_scale = values.shape[-1] ** (-0.25)
    projected = feat_scale * jnp.einsum(
        "rhd,hdm->rhm", values, feature_dirs, preferred_element_type=jnp.float32
    )
    values_wide = values.astype(jnp.float32)
    sq_norm = jnp.sum(values_wide * values_wide, axis=-1, keepdims=True)
    return jnp.exp(projected - 0.5 * feat_scale * feat_scale * sq_norm) * feature_dirs.shape[
        -1
    ] ** (-0.5)


def positive_back(feat_grad, raw_feat, values, feature_dirs):
    feat_scale = values.shape[-1] ** (-0.25)
    exponent_grad = feat_grad * raw_feat
    direct = feat_scale * jnp.einsum(
        "rhm,hdm->rhd",
        exponent_grad.astype(jnp.bfloat16),
        feature_dirs,
        preferred_element_type=jnp.float32,
    )
    values_wide = values.astype(jnp.float32)
    norm_part = (
        feat_scale * feat_scale * values_wide * jnp.sum(exponent_grad, axis=-1, keepdims=True)
    )
    return (direct - norm_part).astype(jnp.bfloat16)


def place_two(first_sel, second_sel, first_val, second_val):
    shape_tail = (1,) * first_val.ndim
    return (
        first_sel.reshape((3,) + shape_tail) * first_val[None]
        + second_sel.reshape((3,) + shape_tail) * second_val[None]
    )


def pick_one(stacked, which):
    return lax.dynamic_index_in_dim(stacked, which, 0, keepdims=False)


def on_device(
    tokens,
    qkv_weight,
    out_proj,
    in_weight,
    out_weight,
    norm_params,
    rand_features,
    long_start,
    masked_pos,
    masked_count,
    masked_grad,
):
    low_type = jnp.bfloat16
    wider_number_type = jnp.float32
    part_qkv, part_out, part_in, part_down, part_norm = (
        lax.all_gather(qkv_weight, "seq", axis=2, tiled=True),
        lax.all_gather(out_proj, "seq", axis=1, tiled=True),
        lax.all_gather(in_weight, "seq", axis=1, tiled=True),
        lax.all_gather(out_weight, "seq", axis=0, tiled=True),
        lax.all_gather(norm_params, "seq", axis=0, tiled=True),
    )
    w_qkv, w_out, w_in, w_down, norm_low = (
        lax.all_gather(part_qkv, "batch", axis=1, tiled=True),
        lax.all_gather(part_out, "batch", axis=0, tiled=True),
        lax.all_gather(part_in, "batch", axis=0, tiled=True),
        lax.all_gather(part_down, "batch", axis=1, tiled=True),
        lax.all_gather(part_norm, "batch", axis=1, tiled=True),
    )
    norm_wide = norm_low.astype(wider_number_type)
    row_count = tokens.shape[1]
    model_width = tokens.shape[2]
    head_count = rand_features.shape[0]
    head_size = rand_features.shape[1]
    seq_index = lax.axis_index("seq")
    seq_last = lax.axis_size("seq") - 1
    position = seq_index * row_count + jnp.arange(row_count, dtype=jnp.int32)
    long_from = long_start[0]
    long_span = lax.axis_size("seq") * row_count - SHORT
    segment = (position >= long_from).astype(jnp.int32) + (
        position >= long_from + long_span
    ).astype(jnp.int32)
    seg_lower = jnp.where(seq_index == 0, 0, 1).astype(jnp.int32)
    seg_upper = jnp.where(seq_index == seq_last, 2, 1).astype(jnp.int32)
    member_upper = ((segment == seg_upper) & (seg_upper != seg_lower)).astype(wider_number_type)
    member_lower = 1.0 - member_upper
    sel_lower = (jnp.arange(3, dtype=jnp.int32) == seg_lower).astype(wider_number_type)
    sel_upper = (jnp.arange(3, dtype=jnp.int32) == seg_upper).astype(wider_number_type) * (
        seg_upper != seg_lower
    ).astype(wider_number_type)
    tokens_wide = tokens[0].astype(wider_number_type)
    normed_wide, unit_one, inverse_one = layer_norm_parts(tokens_wide, norm_wide[0], norm_wide[1])
    normed = normed_wide.astype(low_type)
    query = (
        jnp.dot(normed, w_qkv[0], preferred_element_type=wider_number_type)
        .astype(low_type)
        .reshape(row_count, head_count, head_size)
    )
    key_vecs = (
        jnp.dot(normed, w_qkv[1], preferred_element_type=wider_number_type)
        .astype(low_type)
        .reshape(row_count, head_count, head_size)
    )
    value_vectors = (
        jnp.dot(normed, w_qkv[2], preferred_element_type=wider_number_type)
        .astype(low_type)
        .reshape(row_count, head_count, head_size)
    )
    key_raw = positive_raw(key_vecs, rand_features)
    key_feature_map = key_raw.astype(low_type)
    query_feature_map = positive_raw(query, rand_features).astype(low_type)
    key_bottom_rows = key_feature_map * member_lower.astype(low_type)[:, None, None]
    key_top_rows = key_feature_map * member_upper.astype(low_type)[:, None, None]
    summary_lower = jnp.einsum(
        "jkn,jkp->knp", key_bottom_rows, value_vectors, preferred_element_type=wider_number_type
    )
    summary_upper = jnp.einsum(
        "jkn,jkp->knp", key_top_rows, value_vectors, preferred_element_type=wider_number_type
    )
    total_lower = jnp.einsum(
        "thm,t->hm",
        key_feature_map,
        member_lower.astype(low_type),
        preferred_element_type=wider_number_type,
    )
    total_upper = jnp.einsum(
        "thm,t->hm",
        key_feature_map,
        member_upper.astype(low_type),
        preferred_element_type=wider_number_type,
    )
    summary_part = place_two(sel_lower, sel_upper, summary_lower, summary_upper)
    total_part = place_two(sel_lower, sel_upper, total_lower, total_upper)
    state_summary, total = lax.psum((summary_part, total_part), "seq")
    summary_low = state_summary.astype(low_type)
    total_low = total.astype(low_type)
    sum_bottom_half = pick_one(summary_low, seg_lower)
    sum_top_half = pick_one(summary_low, seg_upper)
    tot_lo = pick_one(total_low, seg_lower)
    tot_hi = pick_one(total_low, seg_upper)
    numerator = member_lower[:, None, None] * jnp.einsum(
        "pox,oxa->poa", query_feature_map, sum_bottom_half, preferred_element_type=wider_number_type
    )
    numerator = numerator + member_upper[:, None, None] * jnp.einsum(
        "pox,oxa->poa", query_feature_map, sum_top_half, preferred_element_type=wider_number_type
    )
    denom = member_lower[:, None] * jnp.einsum(
        "thm,hm->th", query_feature_map, tot_lo, preferred_element_type=wider_number_type
    )
    denom = denom + member_upper[:, None] * jnp.einsum(
        "thm,hm->th", query_feature_map, tot_hi, preferred_element_type=wider_number_type
    )
    heads_out = (numerator / denom[:, :, None]).reshape(row_count, model_width).astype(low_type)
    middle = tokens_wide + jnp.dot(heads_out, w_out, preferred_element_type=wider_number_type)
    normed_two = layer_norm_parts(middle, norm_wide[2], norm_wide[3])[0].astype(low_type)
    upper = jnp.dot(normed_two, w_in, preferred_element_type=wider_number_type)
    activated = exact_gelu(upper).astype(low_type)
    result = (middle + jnp.dot(activated, w_down, preferred_element_type=wider_number_type)).astype(
        low_type
    )
    back_qkv, back_out, back_in, back_down = (w_qkv, w_out, w_in, w_down)
    picked = masked_pos[0]
    in_use = (jnp.arange(picked.shape[0], dtype=jnp.int32) < masked_count[0, 0]).astype(
        wider_number_type
    )
    cot_rows = masked_grad[0].astype(wider_number_type) * in_use[:, None]
    cot_low = cot_rows.astype(low_type)
    middle_rows = middle[picked]
    normed_rows_wide, unit_two, inverse_two = layer_norm_parts(
        middle_rows, norm_wide[2], norm_wide[3]
    )
    normed_rows = normed_rows_wide.astype(low_type)
    upper_rows = jnp.dot(normed_rows, back_in, preferred_element_type=wider_number_type)
    act_rows = exact_gelu(upper_rows).astype(low_type)
    act_grad = jnp.dot(cot_low, back_down.T, preferred_element_type=wider_number_type)
    upper_grad = jax.vjp(exact_gelu, upper_rows)[1](act_grad)[0].astype(low_type)
    grad_in = jnp.einsum(
        "rd,rf->df", normed_rows, upper_grad, preferred_element_type=wider_number_type
    )
    grad_down = jnp.einsum("rf,rd->fd", act_rows, cot_low, preferred_element_type=wider_number_type)
    normed_grad_two = jnp.dot(upper_grad, back_in.T, preferred_element_type=wider_number_type)
    middle_ln, gain_two_grad, bias_two_grad = layer_norm_back(
        normed_grad_two, unit_two, inverse_two, norm_wide[2]
    )
    middle_grad = cot_rows + middle_ln
    attn_grad = middle_grad.astype(low_type)
    grad_out = jnp.einsum(
        "rd,re->de", heads_out[picked], attn_grad, preferred_element_type=wider_number_type
    )
    heads_grad = jnp.dot(attn_grad, back_out.T, preferred_element_type=wider_number_type).reshape(
        -1, head_count, head_size
    )
    query_rows = query[picked]
    query_raw_rows = positive_raw(query_rows, rand_features)
    query_feat_rows = query_feature_map[picked]
    lower_rows = member_lower[picked]
    upper_rows_mask = member_upper[picked]
    numer_rows = numerator[picked]
    denom_rows = denom[picked]
    numerator_gradient = (heads_grad / denom_rows[:, :, None]).astype(low_type)
    denom_grad = (-jnp.sum(heads_grad * numer_rows, axis=-1) / (denom_rows * denom_rows)).astype(
        low_type
    )
    lower_rows_low = lower_rows.astype(low_type)
    upper_rows_low = upper_rows_mask.astype(low_type)
    sgrad_lower = jnp.einsum(
        "wpb,wpq->pbq",
        query_feat_rows,
        numerator_gradient * lower_rows_low[:, None, None],
        preferred_element_type=wider_number_type,
    )
    sgrad_upper = jnp.einsum(
        "wpb,wpq->pbq",
        query_feat_rows,
        numerator_gradient * upper_rows_low[:, None, None],
        preferred_element_type=wider_number_type,
    )
    tgrad_lower = jnp.einsum(
        "rhm,rh->hm",
        query_feat_rows,
        denom_grad * lower_rows_low[:, None],
        preferred_element_type=wider_number_type,
    )
    tgrad_upper = jnp.einsum(
        "rhm,rh->hm",
        query_feat_rows,
        denom_grad * upper_rows_low[:, None],
        preferred_element_type=wider_number_type,
    )
    summary_grad_part = place_two(sel_lower, sel_upper, sgrad_lower, sgrad_upper)
    total_grad_part = place_two(sel_lower, sel_upper, tgrad_lower, tgrad_upper)
    summary_grad, total_grad = (
        lax.psum(summary_grad_part.astype(jnp.bfloat16), "seq").astype(jnp.float32),
        lax.psum(total_grad_part.astype(jnp.bfloat16), "seq").astype(jnp.float32),
    )
    summary_grad_low = summary_grad.astype(low_type)
    segment_grad_bottom = pick_one(summary_grad_low, seg_lower)
    segment_grad_top = pick_one(summary_grad_low, seg_upper)
    tg_lo = pick_one(total_grad, seg_lower)
    tg_hi = pick_one(total_grad, seg_upper)
    denom_grad_wide = denom_grad.astype(wider_number_type)
    query_lower = (
        jnp.einsum(
            "sci,cni->scn",
            numerator_gradient,
            sum_bottom_half,
            preferred_element_type=wider_number_type,
        )
        + denom_grad_wide[:, :, None] * tot_lo.astype(wider_number_type)[None]
    )
    query_upper = (
        jnp.einsum(
            "sci,cni->scn",
            numerator_gradient,
            sum_top_half,
            preferred_element_type=wider_number_type,
        )
        + denom_grad_wide[:, :, None] * tot_hi.astype(wider_number_type)[None]
    )
    query_feat_grad = (
        lower_rows[:, None, None] * query_lower + upper_rows_mask[:, None, None] * query_upper
    )
    key_lower_grad = (
        jnp.einsum(
            "zqy,qiy->zqi",
            value_vectors,
            segment_grad_bottom,
            preferred_element_type=wider_number_type,
        )
        + tg_lo[None]
    )
    key_upper_grad = (
        jnp.einsum(
            "zqy,qiy->zqi",
            value_vectors,
            segment_grad_top,
            preferred_element_type=wider_number_type,
        )
        + tg_hi[None]
    )
    key_feat_grad = (
        member_lower[:, None, None] * key_lower_grad + member_upper[:, None, None] * key_upper_grad
    )
    value_grad = member_lower[:, None, None] * jnp.einsum(
        "pox,oxa->poa",
        key_feature_map,
        segment_grad_bottom,
        preferred_element_type=wider_number_type,
    )
    value_grad = value_grad + member_upper[:, None, None] * jnp.einsum(
        "pox,oxa->poa", key_feature_map, segment_grad_top, preferred_element_type=wider_number_type
    )
    query_grad = positive_back(query_feat_grad, query_raw_rows, query_rows, rand_features).reshape(
        -1, model_width
    )
    key_grad = positive_back(key_feat_grad, key_raw, key_vecs, rand_features).reshape(
        row_count, model_width
    )
    value_low = value_grad.astype(low_type).reshape(row_count, model_width)
    grad_query_w = jnp.einsum(
        "rd,re->de", normed[picked], query_grad, preferred_element_type=wider_number_type
    )
    grad_key_w = jnp.einsum("td,te->de", normed, key_grad, preferred_element_type=wider_number_type)
    grad_value_w = jnp.einsum(
        "td,te->de", normed, value_low, preferred_element_type=wider_number_type
    )
    query_back = jnp.dot(query_grad, back_qkv[0].T, preferred_element_type=wider_number_type)
    normed_grad_one = jnp.dot(
        key_grad, back_qkv[1].T, preferred_element_type=wider_number_type
    ) + jnp.dot(value_low, back_qkv[2].T, preferred_element_type=wider_number_type)
    normed_grad_one = normed_grad_one.at[picked].add(query_back)
    token_ln, gain_one_grad, bias_one_grad = layer_norm_back(
        normed_grad_one, unit_one, inverse_one, norm_wide[0]
    )
    tokens_grad = token_ln.at[picked].add(middle_grad)
    grad_qkv = jnp.stack([grad_query_w, grad_key_w, grad_value_w])
    grad_norm = jnp.stack([gain_one_grad, bias_one_grad, gain_two_grad, bias_two_grad])
    first_qkv, first_out, first_in, first_down, first_norm = (
        lax.psum_scatter(grad_qkv, "batch", scatter_dimension=1, tiled=True),
        lax.psum_scatter(grad_out, "batch", scatter_dimension=0, tiled=True),
        lax.psum_scatter(grad_in, "batch", scatter_dimension=0, tiled=True),
        lax.psum_scatter(grad_down, "batch", scatter_dimension=1, tiled=True),
        lax.psum_scatter(grad_norm, "batch", scatter_dimension=1, tiled=True),
    )
    owned = (
        lax.psum_scatter(
            first_qkv.astype(jnp.bfloat16), "seq", scatter_dimension=2, tiled=True
        ).astype(jnp.float32),
        lax.psum_scatter(
            first_out.astype(jnp.bfloat16), "seq", scatter_dimension=1, tiled=True
        ).astype(jnp.float32),
        lax.psum_scatter(
            first_in.astype(jnp.bfloat16), "seq", scatter_dimension=1, tiled=True
        ).astype(jnp.float32),
        lax.psum_scatter(
            first_down.astype(jnp.bfloat16), "seq", scatter_dimension=0, tiled=True
        ).astype(jnp.float32),
        lax.psum_scatter(
            first_norm.astype(jnp.bfloat16), "seq", scatter_dimension=0, tiled=True
        ).astype(jnp.float32),
    )
    return (result[None], tokens_grad[None], owned[0], owned[1], owned[2], owned[3], owned[4])


MESH = pl.DeviceIdType.MESH
LOW = jnp.bfloat16
WIDE = jnp.float32
LOG2E = 1.4426950408889634
ROOT_HALF = 0.7071067811865476
PDF_SCALE = 0.3989422804014327
PAD = 16


def scatter_shapes(order, nz, bd, lanes):
    shapes = [(nz, 2, bd, lanes)] * 2
    sides, tall, pair = 2, (nz,), (2,)
    for ax in order:
        if ax == "z":
            tall = ()
            shapes += [pair + (bd, lanes)] * (sides * (nz - 1))
        elif ax == "x":
            pair = ()
            shapes += [tall + (bd, lanes)] * sides
        elif ax == "y":
            sides = 1
            shapes += [tall + pair + (bd, lanes)]
        else:
            sides, pair = 1, ()
            shapes += [tall + (bd, lanes)] * 3
    return shapes


KIND = {
    "kv": "zR",
    "qo": "Rz",
    "w1a": "zR",
    "w1b": "zR",
    "w2a": "zxy",
    "w2b": "xyz",
    "g2a": "xzy",
    "g2b": "zR",
    "g1a": "xzy",
    "g1b": "yxz",
    "qog": "Rz",
    "kg": "xyz",
    "vg": "yxz",
}
EARLY = 0
PLAN = (
    (("norm", 0), ("kv", 0), ),
    (("qo", 0), ("norm", 1), ),
    (("w1a", 0), ("norm", 2), ),
    (("qo", 1), ),
    (),
    (("kv", 1), ("kv", 2), ),
    (("w2b", 0), ("w1a", 1), ),
    (),
    (("w1b", 0), ("kv", 3), ),
    (),
    (),
    (),
    (("w2b", 1), ),
    (),
    (),
    (),
    (),
    (("w2a", 0), ("ar1a", 0), ("ar1b", 0), ),
    (("qo", 2), ),
    (("ar1a", 1), ("ar1b", 1), ("w1a", 2), ("w1b", 1), ("w2b", 2), ),
    (("qo", 3), ),
    (("w2a", 1), ),
    (),
    (("w1a", 3), ),
    (),
    (),
    (("ar1a", 2), ("ar1b", 2), ("ar1a", 3), ("ar1b", 3), ),
    (("w2a", 2), ),
    (),
    (("w1b", 2), ),
    (("w2a", 3), ),
    (),
    (),
    (),
    (("w1b", 3), ),
    (("w2b", 3), ),
    (),
    (),
    (),
    (),
    (),
    (("w2a", 4), ("w2b", 4), ),
    (),
    (),
    (("g2b", 0), ),
    (("g2a", 0), ("w2a", 5), ),
    (),
    (),
    (("g1a", 0), ("g1b", 0), ),
    (("ar2a", 0), ("g2b", 1), ("g2a", 1), ),
    (("ar2b", 0), ("ar2a", 1), ),
    (("ar2b", 1), ("g1a", 1), ("g1b", 1), ("ar2a", 2), ),
    (("qog", 0), ),
    (("ar2a", 3), ),
    (),
    (),
    (("ar2b", 2), ("g2a", 2), ("qog", 1), ),
    (),
    (),
    (),
    (("ar2b", 3), ),
    (),
    (),
    (),
    (),
    (("kg", 0), ("vg", 0), ),
    (),
    (),
    (("g2b", 2), ("g1a", 2), ("g1b", 2), ),
    (("kg", 1), ("vg", 1), ),
    (("g2a", 3), ),
    (),
    (("qog", 2), ("g2a", 4), ("g2b", 3), ),
    (("ngs", 0), ),
    (("vg", 2), ("g1a", 3), ("ngs", 1), ),
    (("kg", 2), ("g1b", 3), ("ngs", 2), ("g1a", 4), ),
    (("vg", 3), ("qog", 3), ("ngs", 3), ),
    (("kg", 3), ("ngs", 4), ),
    (("g1b", 4), ),
    (("kg", 4), ("vg", 4), ),
    (),
    (),
)


def dot_over(a, b, ca, cb):
    return lax.dot_general(a, b, (((ca,), (cb,)), ((), ())), preferred_element_type=WIDE)


def nn(a, b):
    return dot_over(a, b, 1, 0)


def nt(a, b):
    return dot_over(a, b, 1, 1)


def turn(a):
    if a.dtype == LOW:
        return a.astype(WIDE).T.astype(LOW)
    return a.T


def flat(a):
    return a.reshape(-1, a.shape[-1])


def unit_norm(x):
    cen = x - jnp.mean(x, axis=-1, keepdims=True)
    inv = lax.rsqrt(jnp.mean(cen * cen, axis=-1, keepdims=True) + EPS)
    return cen * inv, inv


def norm_back(incoming, unit, inv, gain):
    e = incoming * gain
    mean_e = jnp.mean(e, axis=-1, keepdims=True)
    mean_eu = jnp.mean(e * unit, axis=-1, keepdims=True)
    return inv * (e - mean_e - unit * mean_eu)


def features(proj, u_low, scale, feat):
    wide = u_low.astype(WIDE)
    sq = jnp.sum(wide * wide, axis=0, keepdims=True)
    shift = (0.5 * scale * scale * LOG2E) * sq
    half_log = 0.5 * (feat.bit_length() - 1)
    return jnp.exp2((scale * LOG2E) * proj - (shift + half_log))


class Wires:
    def __init__(self, send_sems, recv_sems):
        self.send_sems, self.recv_sems, self.used = send_sems, recv_sems, 0
        self.sent, self.now = [], []

    def send(self, src, dst, dev):
        copy = pltpu.make_async_remote_copy(
            src_ref=src,
            dst_ref=dst,
            send_sem=self.send_sems.at[self.used],
            recv_sem=self.recv_sems.at[self.used],
            device_id=dev,
            device_id_type=MESH,
        )
        self.used += 1
        self.now.append(copy.start)
        self.sent.append(copy)
        return copy

    def arrived(self, copies):
        self.now += [copy.wait_recv for copy in copies]

    def left(self, copies):
        self.now += [copy.wait_send for copy in copies]
        self.sent = [o for o in self.sent if all(o is not copy for copy in copies)]

    def steps(self, task):
        kept = []
        self.now = []
        for _ in task:
            kept.append(self.now)
            self.now = []
        return kept

    def drain(self):
        for copy in self.sent:
            copy.wait_send()


def layer_kernel(
    nz,
    ns,
    tok_in,
    wqkv_in,
    wo_in,
    win_in,
    wdn_in,
    nrm_in,
    rf_in,
    ls,
    pos,
    cnt,
    mg_in,
    mixed_out,
    tgrad_out,
    gqkv,
    gop,
    gin,
    gdn,
    gnorm,
    tok,
    rf,
    mg,
    w0,
    w1,
    w2,
    nb,
    wkvt,
    wqt,
    wo,
    xnt,
    kvt,
    vs,
    kft,
    pm,
    posc,
    rft,
    sumf,
    loc,
    ar_a,
    ar_r1,
    ar_r2,
    ar_f,
    dsumt,
    qrt,
    qfr,
    num_r,
    den_r,
    dn_st,
    hot,
    hort,
    dmid_low,
    xnrt,
    dqt,
    dhd,
    dxqt,
    g0,
    g1,
    g2,
    ng_a,
    ng_r,
    mixed_v,
    tgrad_v,
    send_sems,
    recv_sems,
    out_sems,
    *scatter_refs,
):
    rows, width = tok.shape
    slots = mg.shape[0]
    heads, size, feat = rf.shape
    scale = size**-0.25
    bd = w0.shape[3]
    sw = wqkv_in.shape[2]
    tile = 256
    wide_tile = 512
    b = lax.axis_index("batch")
    s = lax.axis_index("seq")
    x = lax.rem(b, 2)
    z = b // 2
    c = lax.rem(s, 2)
    y = s // 2
    s_core = s + 1 - 2 * c
    s_y = s + 2 - 4 * y
    s_far = s_core + 2 - 4 * y
    own_col, mate_col = [c, 2 + c], [1 - c, 3 - c]
    x_other = 1 - x
    z_next = [lax.rem(z + k, nz) for k in range(1, nz)]
    to_core = (b, s_core)
    to_y = (b, s_y)
    to_x = (b + 1 - 2 * x, s)
    to_z = [(at * 2 + x, s) for at in z_next]
    to_diag = [(at * 2 + x_other, s) for at in z_next]
    to_xy = (b + 1 - 2 * x, s_y)
    to_plane = to_z + [to_x] + to_diag
    to_seq = [to_core, to_y, (b, s_far)]
    wires = Wires(send_sems, recv_sems)

    shards = (
        (wqkv_in.at[1], w0.at[s, z, x, :, 0:sw]),
        (wqkv_in.at[2], w0.at[s, z, x, :, sw : 2 * sw]),
        (wqkv_in.at[0], w0.at[s, z, x, :, 2 * sw : 3 * sw]),
        (wo_in, w0.at[s, z, x, :, 3 * sw : 4 * sw]),
        (win_in, w1.at[s, z, x]),
        (wdn_in, w2.at[s, z, x]),
        (rf_in, rf),
        (tok_in, tok),
        (mg_in, mg),
    )
    loads = [pltpu.make_async_copy(a, o, out_sems.at[2 + n]) for n, (a, o) in enumerate(shards)]
    for load in loads:
        load.start()
    barrier = pltpu.get_barrier_semaphore()
    partners = to_plane + to_seq + [to_xy]
    for dev in partners:
        pl.semaphore_signal(barrier, inc=1, device_id=dev, device_id_type=MESH)

    place = (
        lax.broadcasted_iota(jnp.int32, (bd, 2 * bd), 1)
        == lax.broadcasted_iota(jnp.int32, (bd, 2 * bd), 0) + bd * x
    )
    nb[s, z, x] = nn(
        jnp.broadcast_to(nrm_in[...], (PAD, bd)), jnp.where(place, 1.0, 0.0).astype(LOW)
    ).astype(LOW)
    seq_pos = s * rows
    long_from = ls[0, 0]
    long_to = long_from + ns * rows - SHORT

    def shared_mask(position):
        at = position + seq_pos
        return jnp.where((at >= long_from) & (at < long_to), 1.0, 0.0)

    def tiles(lo, hi, step):
        def body(t, carry):
            step(t)
            return carry

        lax.fori_loop(lo, hi, body, 0)

    pos_row = pos[...]
    posc[...] = jnp.broadcast_to(pos_row.astype(WIDE), (128, slots)).T
    sh_r = shared_mask(pos_row)

    def select_tile(t):
        at = pl.multiple_of(t * tile, tile)
        for j in range(tile // 128):
            lane = lax.broadcasted_iota(jnp.int32, (slots, 128), 1) + (at + 128 * j)
            pm[:, pl.ds(at + 128 * j, 128)] = jnp.where(
                lane.astype(WIDE) == posc[...], 1.0, 0.0
            ).astype(LOW)
        lane = lax.broadcasted_iota(jnp.int32, (1, tile), 1) + at
        sh = shared_mask(lane)
        row = lax.broadcasted_iota(jnp.int32, (PAD, tile), 0)
        ones = jnp.where(row == 0, sh, jnp.where(row == 1, 1.0 - sh, 0.0)).astype(LOW)
        for h in range(heads):
            vs[h, 2 * size : 2 * size + PAD, pl.ds(at, tile)] = ones

    tiles(0, rows // tile, select_tile)
    for load in loads[:7]:
        load.wait()
    for h in range(heads):
        rft[h] = turn(rf[h])
    pl.semaphore_wait(barrier, len(partners))

    tasks = {}
    plan = list(PLAN)

    def take(names):
        for name, n in names:
            for act in tasks[name][n]:
                act()

    def poll():
        take(plan.pop(0))

    def rounds(count, points):
        taken = [[plan.pop(0) for _ in range(points)] for _ in range(count)]

        def at_point(j, n):
            for k in range(count):
                if taken[k][n]:
                    pl.when(j == k)(functools.partial(take, taken[k][n]))

        return at_point

    def loop(count, body):
        def step(j, carry):
            body(j)
            return carry

        lax.fori_loop(0, count, step, 0)

    def gather_norm():
        at = nb.at[s, z, x]
        first = [wires.send(at, at, dev) for dev in to_plane]
        yield
        wires.arrived(first)
        at = nb.at[s]
        second = [wires.send(at, at, dev) for dev in to_seq]
        yield
        wires.arrived(second)
        yield

    every = slice(None)

    def gather(ref, lo, hi, order):
        sides, zi, xi = [s], z, x
        early = order[-1] == "y"
        near, now = [], []
        for ax in order:
            if ax == "z":
                for side in sides:
                    at = ref.at[side, z, xi, :, lo:hi]
                    now += [wires.send(at, at, dev) for dev in to_z]
                zi = every
            elif ax == "x":
                for side in sides:
                    at = ref.at[side, zi, x, :, lo:hi]
                    now.append(wires.send(at, at, to_x))
                xi = every
            elif ax == "y":
                at = ref.at[s, zi, xi, :, lo:hi]
                now.append(wires.send(at, at, to_y))
                if early:
                    near = [wires.send(at, at, to_core)]
                sides = [s, s_y]
            else:
                at = ref.at[s, zi, x, :, lo:hi]
                now += [wires.send(at, at, dev) for dev in (to_x, to_y, to_xy)]
                xi, sides = every, [s, s_y]
            yield
            if near:
                wires.arrived(near)
                yield
            wires.arrived(now)
            now = []
        for side in [s_y] if early else [s, s_y]:
            at = ref.at[side, :, :, :, lo:hi]
            now.append(wires.send(at, at, to_core))
        yield
        wires.arrived(now)
        yield

    def add_seq(out, n, one, other):
        out[n] = one[n] + other[...]

    def reduce_seq(k, v):
        r1, r2, f = ar_r1.at[k, v], ar_r2.at[k, v], ar_f.at[k]
        mine = own_col[v]
        now = [wires.send(ar_a.at[mate_col[v]], r1, to_core)]
        yield
        wires.arrived(now)
        wires.left(now)
        wires.now.append(functools.partial(add_seq, ar_a, mine, ar_a, r1))
        now = [wires.send(ar_a.at[mine], r2, to_y)]
        yield
        wires.arrived(now)
        wires.left(now)
        wires.now.append(functools.partial(add_seq, f, mine, ar_a, r2))
        now = [wires.send(f.at[mine], f.at[mine], to_core)]
        yield
        wires.arrived(now)
        yield

    def add_into(g, side, zi, xi, lo, hi, got):
        if zi is every:

            def add(j, carry):
                at = (side, j, xi, every, slice(lo, hi))
                g[at] = g[at] + got[j]
                return carry

            lax.fori_loop(0, nz, add, 0)
        else:
            at = (side, zi, xi, every, slice(lo, hi))
            g[at] = g[at] + got[...]

    last_parts = {}

    def scatter(name, g, lo, hi, order, bufs):
        bufs = list(bufs)
        sides, zi, xi = own_col, every, every
        now = [wires.send(g.at[mate_col[v], :, :, :, lo:hi], bufs[v], to_core) for v in range(2)]
        yield
        wires.arrived(now)
        for v in range(2):
            wires.now.append(functools.partial(add_into, g, sides[v], zi, xi, lo, hi, bufs[v]))
        bufs = bufs[2:]
        for n, ax in enumerate(order):
            jobs = []
            if ax == "z":
                for side in sides:
                    for k in range(1, nz):
                        at = g.at[side, z_next[k - 1], xi, :, lo:hi]
                        jobs.append((at, to_z[k - 1], side))
                zi = z
            elif ax == "x":
                for side in sides:
                    jobs.append((g.at[side, zi, x_other, :, lo:hi], to_x, side))
                xi = x
            elif ax == "y":
                jobs.append((g.at[s_y, zi, xi, :, lo:hi], to_y, s))
                sides = [s]
            else:
                jobs.append((g.at[s, zi, x_other, :, lo:hi], to_x, s))
                jobs.append((g.at[s_y, zi, x, :, lo:hi], to_y, s))
                jobs.append((g.at[s_y, zi, x_other, :, lo:hi], to_xy, s))
                xi, sides = x, [s]
            got, bufs = bufs[: len(jobs)], bufs[len(jobs) :]
            now = [wires.send(at, buf, dev) for (at, dev, _), buf in zip(jobs, got)]
            yield
            wires.arrived(now)
            if n < len(order) - 1:
                for (_, _, side), buf in zip(jobs, got):
                    wires.now.append(functools.partial(add_into, g, side, zi, xi, lo, hi, buf))
            else:
                last_parts[name] = (g, lo, hi, got)
        yield

    def scattered(name):
        g, lo, hi, got = last_parts[name]
        total = g[s, z, x, :, lo:hi].astype(WIDE)
        for buf in got:
            total = total + buf[...].astype(WIDE)
        return total

    def add_task(name, task):
        tasks[name] = wires.steps(task)

    half = w1.shape[4] // 2
    add_task("norm", gather_norm())
    add_task("kv", gather(w0, 0, 2 * sw, KIND["kv"]))
    add_task("qo", gather(w0, 2 * sw, 4 * sw, KIND["qo"]))
    for name, ref in (("w1", w1), ("w2", w2)):
        add_task(name + "a", gather(ref, 0, half, KIND[name + "a"]))
        add_task(name + "b", gather(ref, half, 2 * half, KIND[name + "b"]))
    for k in range(2):
        for v in range(2):
            add_task("ar%d%s" % (k + 1, "ab"[v]), reduce_seq(k, v))
    def add_norm(ks):
        for k in ks:
            ng_a[...] += ng_r[k]

    def sum_norm():
        order = [([to_core], 0), ([to_y], 1), ([to_x], 2), (to_z, 3)]
        for devs, k in order:
            now = [wires.send(ng_a, ng_r.at[k + n], dev) for n, dev in enumerate(devs)]
            yield
            wires.arrived(now)
            wires.left(now)
            wires.now.append(functools.partial(add_norm, range(k, k + len(devs))))
        yield

    add_task("ngs", sum_norm())
    spare = list(scatter_refs)
    for name, g, lo, hi in scatter_parts(g0, g1, g2, sw, half):
        count = len(scatter_shapes(KIND[name], nz, bd, hi - lo))
        add_task(name, scatter(name, g, lo, hi, KIND[name], spare[:count]))
        spare = spare[count:]

    poll()

    loads[7].wait()
    toks_r = nn(pm[...], tok[...])
    poll()
    unit_r, _ = unit_norm(toks_r)
    poll()

    def norm_row(i):
        return jnp.concatenate(
            [
                (nb[i, j, 0, 0:1, :] + nb[i, j, 1, 0:1, :]).astype(WIDE)
                for j in range(nz)
            ],
            axis=1,
        )

    gain1, bias1, gain2, bias2 = [norm_row(i) for i in range(4)]
    xn_r = (unit_r * gain1 + bias1).astype(LOW)
    xnrt[...] = turn(xn_r)

    for n in range(2):
        cols = slice(n * rows // 2, (n + 1) * rows // 2)
        unit, _ = unit_norm(tok[cols, :].astype(WIDE))
        xnt[:, cols] = turn((unit * gain1 + bias1).astype(LOW))
        poll()

    sh_all = shared_mask(lax.broadcasted_iota(jnp.int32, (1, rows), 1))
    sh_low = sh_all.astype(LOW)

    def kv_features(sd):
        r = nn(wkvt[sd], xnt[...]).astype(LOW)
        kvt[sd] = r
        for i in range(2):
            h = 2 * sd + i
            k_h = r[size * i : size * (i + 1)]
            v_h = r[sw + size * i : sw + size * (i + 1)]
            kft[h] = features(nn(rft[h], k_h), k_h, scale, feat).astype(LOW)
            vs[h, 0:size, :] = v_h * sh_low
            vs[h, size : 2 * size, :] = v_h * (1.0 - sh_low)

    def kv_sums(sd):
        for i in range(2):
            h = 2 * sd + i
            part = nt(vs[h], kft[h]).astype(LOW)
            ar_a[sd, i, 0:size, :] = part[0:size]
            ar_a[sd, i, size : size + PAD, :] = part[2 * size :]
            loc[h] = part[size:]

    def block_at(j):
        return 2 * lax.rem(y + j // 2, 2) + lax.rem(c + j, 2)

    at_point = rounds(ns, 3)

    def kv_block(j, at_point=at_point):
        sd = block_at(j)
        at_point(j, 0)
        wkvt[sd] = turn(flat(w0[sd, :, :, :, 0 : 2 * sw]))
        kv_features(sd)
        at_point(j, 1)
        kv_sums(sd)
        at_point(j, 2)

    loop(ns, kv_block)
    poll()

    keep = (g0, g1, g2)

    def q_block(sd):
        wqt[sd] = turn(flat(w0[sd, :, :, :, 2 * sw : 3 * sw]))
        q = nn(wqt[sd], xnt[...]).astype(LOW)
        for i in range(2):
            q_h = q[size * i : size * (i + 1)]
            qf = features(nn(rft[2 * sd + i], q_h), q_h, scale, feat).astype(LOW)
            for t, gt in enumerate(keep):
                part = qf[:, t * wide_tile : (t + 1) * wide_tile]
                gt[sd, 2 * i : 2 * i + 2] = part.reshape((2,) + g0.shape[2:4] + (wide_tile,))
        q = nn(wqt[sd], xnrt[...]).astype(LOW)
        for i in range(2):
            q_h = q[size * i : size * (i + 1)]
            qrt[2 * sd + i] = q_h
            qfr[2 * sd + i] = features(nn(rft[2 * sd + i], q_h), q_h, scale, feat).astype(LOW)

    at_point = rounds(ns, 2)

    def q_round(j, at_point=at_point):
        at_point(j, 0)
        q_block(block_at(j))
        at_point(j, 1)

    loop(ns, q_round)
    poll()
    def tail_rows(k, blk, n, h):
        first = lax.broadcasted_iota(jnp.int32, (PAD, feat), 0) == 0
        return jnp.where(
            first,
            ar_f[k, blk, n, size : size + PAD, :].astype(WIDE),
            loc[h, size : size + PAD, :].astype(WIDE),
        ).astype(LOW)

    for h in range(heads):
        sumf[h, 0:size, :] = ar_f[0, h // 2, h % 2, 0:size, :]
        sumf[h, size : 2 * size, :] = loc[h, 0:size, :]
        sumf[h, 2 * size : 2 * size + PAD, :] = tail_rows(0, h // 2, h % 2, h)

    def split_ratio(nd, sh):
        pick = jnp.broadcast_to(sh, (size, sh.shape[1])) > 0.5
        num = jnp.where(pick, nd[0:size], nd[size : 2 * size])
        den = jnp.where(sh > 0.5, nd[2 * size : 2 * size + 1], nd[2 * size + 1 : 2 * size + 2])
        return num, den

    for h in range(heads):
        num, den = split_ratio(nn(sumf[h], qfr[h]), sh_r)
        num_r[h] = num
        den_r[h] = jnp.broadcast_to(den, (8, slots))
        hort[size * h : size * (h + 1), :] = (num * (1.0 / den)).astype(LOW)
    poll()

    for t, gt in enumerate(keep):
        cols = slice(t * wide_tile, (t + 1) * wide_tile)
        for h in range(heads):
            i, jj = h // 2, h % 2
            qf = gt[i, 2 * jj : 2 * jj + 2].reshape(feat, wide_tile)
            num, den = split_ratio(nn(sumf[h], qf), sh_all[:, cols])
            hot[h, :, cols] = (num * (1.0 / den)).astype(LOW)
        poll()

    for i in range(ns):
        wo[:, sw * i : sw * (i + 1)] = flat(w0[i, :, :, :, 3 * sw : 4 * sw])
    middle_r = toks_r + nn(turn(hort[...]), wo[...])
    unit2, inv2 = unit_norm(middle_r)
    xn2_r = (unit2 * gain2 + bias2).astype(LOW)
    xn2_rt = turn(xn2_r)
    slot_id = lax.broadcasted_iota(jnp.int32, (slots, 1), 0)
    loads[8].wait()
    cot = mg[...].astype(WIDE) * jnp.where(slot_id < cnt[0, 0], 1.0, 0.0)
    cot_low = cot.astype(LOW)
    cot_t = turn(cot_low)
    poll()

    at_point = rounds(ns, 2)

    def forward(j, at_point=at_point):
        sd = block_at(j)
        at_point(j, 0)
        upper = nn(xn2_r, flat(w1[sd]))
        cdf = 0.5 + 0.5 * lax.erf(upper * ROOT_HALF)
        act = (upper * cdf).astype(LOW)
        slope = cdf + upper * (PDF_SCALE * jnp.exp2((-0.5 * LOG2E) * (upper * upper)))
        tgrad_v[pl.ds(pl.multiple_of(j * slots, slots), slots), :] = slope
        g2[sd] = nn(cot_t, act).astype(LOW).reshape(g2.shape[1:])
        at_point(j, 1)

    loop(ns, forward)
    at_point = rounds(ns, 2)
    dhd[...] = jnp.zeros(dhd.shape, WIDE)

    def backward(j, at_point=at_point):
        sd = block_at(j)
        at_point(j, 0)
        du = (nn(cot_low, flat(w2[sd])) * tgrad_v[pl.ds(pl.multiple_of(j * slots, slots), slots), :]).astype(LOW)
        g1[sd] = nn(xn2_rt, du).astype(LOW).reshape(g1.shape[1:])
        dhd[...] += nt(flat(w1[sd]), du)
        at_point(j, 1)

    loop(ns, backward)
    dn2 = dhd[...].T
    poll()

    norm_g2 = jnp.sum(dn2 * unit2, axis=0, keepdims=True)
    norm_g3 = jnp.sum(dn2, axis=0, keepdims=True)
    d_att = (cot + norm_back(dn2, unit2, inv2, gain2)).astype(LOW)
    dmid_low[...] = d_att
    dhd[...] = nt(wo[...], d_att)
    for h in range(heads):
        dh = dhd[size * h : size * (h + 1), :]
        rden = 1.0 / den_r[h, 0:1, :]
        d_num = (dh * rden).astype(LOW)
        d_den = (-jnp.sum(dh * num_r[h], axis=0, keepdims=True) * (rden * rden)).astype(LOW)
        shl = sh_r.astype(LOW)
        dn_st[h, 0:size, :] = d_num * shl
        dn_st[h, size : 2 * size, :] = d_num * (1.0 - shl)
        row = lax.broadcasted_iota(jnp.int32, (PAD, slots), 0)
        dd = jnp.broadcast_to(d_den.astype(WIDE), (PAD, slots))
        dn_st[h, 2 * size : 2 * size + PAD, :] = jnp.where(
            row == 0, dd * sh_r, jnp.where(row == 1, dd * (1.0 - sh_r), 0.0)
        ).astype(LOW)
        part = nt(dn_st[h], qfr[h]).astype(LOW)
        ar_a[h // 2, h % 2, 0:size, :] = part[0:size]
        ar_a[h // 2, h % 2, size : size + PAD, :] = part[2 * size :]
        loc[h] = part[size:]
        if h == heads // 2 - 1:
            poll()
    poll()

    for h in range(heads):
        d_qf = nn(turn(sumf[h]), dn_st[h])
        w = d_qf * qfr[h].astype(WIDE)
        ws = jnp.sum(w, axis=0, keepdims=True)
        q_h = qrt[h].astype(WIDE)
        dqt[size * h : size * (h + 1), :] = (
            scale * nn(rf[h], w.astype(LOW)) - (scale * scale) * q_h * ws
        ).astype(LOW)
    poll()
    grad_q = nt(xnrt[...], dqt[...]).astype(LOW)
    grad_o = nn(hort[...], dmid_low[...]).astype(LOW)
    for i in range(ns):
        for n, part in enumerate((grad_q, grad_o)):
            part = part[:, sw * i : sw * (i + 1)]
            g0[i, :, :, :, (2 + n) * sw : (3 + n) * sw] = part.reshape(g0.shape[1:4] + (sw,))
    poll()
    acc = jnp.zeros((width, slots), WIDE)
    for i in range(ns):
        acc = acc + nn(flat(w0[i, :, :, :, 2 * sw : 3 * sw]), dqt[sw * i : sw * (i + 1), :])
    dxqt[...] = acc.astype(LOW)
    poll()

    def dense_tile(t):
        cols = slice(t * wide_tile, (t + 1) * wide_tile)
        ho = turn(flat(hot[:, :, cols]))
        mid = tok[cols, :].astype(WIDE) + nn(ho, wo[...])
        unit, _ = unit_norm(mid)
        xn2 = (unit * gain2 + bias2).astype(LOW)
        total = mid
        for i in range(ns):
            up = nn(xn2, flat(w1[i]))
            act = (up * (0.5 + 0.5 * lax.erf(up * ROOT_HALF))).astype(LOW)
            total = total + nt(act, flat(w2[i]))
            if i == 1:
                yield
        mixed_v[cols, :] = total.astype(LOW)
        yield

    def dense_pieces():
        for t in range(rows // wide_tile):
            yield from dense_tile(t)

    dense = dense_pieces()

    def dense_some(count):
        for _ in range(count):
            next(dense)
            poll()

    dense_some(EARLY)
    def key_sums(v):
        for n in range(4):
            h, blk = 4 * v + n, 2 * v + n // 2
            stack = jnp.concatenate(
                [ar_f[1, blk, n % 2, 0:size, :], loc[h, 0:size, :], tail_rows(1, blk, n % 2, h)],
                axis=0,
            )
            ar_a[blk, n % 2, 0:size, :] = stack[0:size]
            dsumt[h] = turn(stack)

    def key_block(sd):
        for i in range(2):
            h = 2 * sd + i
            w = nn(dsumt[h], vs[h]) * kft[h].astype(WIDE)
            ws = jnp.sum(w, axis=0, keepdims=True)
            k_h = kvt[sd, size * i : size * (i + 1), :].astype(WIDE)
            dk = scale * nn(rf[h], w.astype(LOW)) - (scale * scale) * k_h * ws
            both = nn(jnp.concatenate([ar_a[sd, i, 0:size, :], loc[h, 0:size, :]], axis=0), kft[h])
            pick = jnp.broadcast_to(sh_all, (size, rows)) > 0.5
            kvt[sd, size * i : size * (i + 1), :] = dk.astype(LOW)
            kvt[sd, sw + size * i : sw + size * (i + 1), :] = jnp.where(
                pick, both[0:size], both[size:]
            ).astype(LOW)

    at_point = rounds(ns, 4)

    def key_round(j, at_point=at_point):
        at_point(j, 0)
        pl.when(lax.rem(j, 2) == 0)(functools.partial(key_sums, j // 2))
        at_point(j, 1)
        sd = 2 * (j // 2) + lax.rem(j + 1 + c, 2)
        key_block(sd)
        at_point(j, 2)
        part = nt(xnt[...], kvt[sd]).astype(LOW)
        g0[sd, :, :, :, 0 : 2 * sw] = part.reshape(g0.shape[1:4] + (2 * sw,))
        at_point(j, 3)

    loop(ns, key_round)

    ng_a[...] = jnp.zeros(ng_a.shape, WIDE)

    def token_tile(t):
        cols = slice(t * wide_tile, (t + 1) * wide_tile)
        dxt = nn(dxqt[...], pm[:, cols])
        for i in range(ns):
            dxt = dxt + nn(flat(w0[i, :, :, :, 0 : 2 * sw]), kvt[i, :, cols])
        dx = dxt.T
        unit, inv = unit_norm(tok[cols, :].astype(WIDE))
        tgrad_v[cols, :] = norm_back(dx, unit, inv, gain1) + nn(turn(pm[:, cols]), dmid_low[...])
        ng_a[0:1, :] += jnp.sum(dx * unit, axis=0, keepdims=True)
        ng_a[1:2, :] += jnp.sum(dx, axis=0, keepdims=True)

    for n in range(rows // wide_tile):
        token_tile(n)
        poll()
    out_t = pltpu.make_async_copy(tgrad_v, tgrad_out, out_sems.at[0])
    out_t.start()
    ng_a[2:3, :] = norm_g2
    ng_a[3:4, :] = norm_g3

    poll()
    dense_some(2 * (rows // wide_tile) - EARLY)
    out_m = pltpu.make_async_copy(mixed_v, mixed_out, out_sems.at[1])
    out_m.start()

    poll()
    gin[:, 0:half] = scattered("g1a")
    gin[:, half:] = scattered("g1b")
    gdn[:, 0:half] = scattered("g2a")
    gdn[:, half:] = scattered("g2b")
    qo = scattered("qog")
    gqkv[0] = qo[:, 0:sw]
    gop[...] = qo[:, sw : 2 * sw]
    poll()
    gqkv[1] = scattered("kg")
    gqkv[2] = scattered("vg")
    total = ng_a[...]
    row = lax.broadcasted_iota(jnp.int32, total.shape, 0)
    mine = jnp.sum(jnp.where(row == s, total, 0.0), axis=0, keepdims=True)
    mine = jnp.broadcast_to(mine, total.shape)
    gnorm[...] = pltpu.roll(mine, lax.rem(width - bd * b, width), 1)[0:1, 0:bd]
    assert not plan
    wires.drain()
    out_t.wait()
    out_m.wait()


def scatter_parts(g0, g1, g2, sw, half):
    return (
        ("g1a", g1, 0, half),
        ("g1b", g1, half, 2 * half),
        ("g2a", g2, 0, half),
        ("g2b", g2, half, 2 * half),
        ("qog", g0, 2 * sw, 4 * sw),
        ("kg", g0, 0, sw),
        ("vg", g0, sw, 2 * sw),
    )


def fits(mesh, args):
    tokens, qkv_weight, _, in_weight, _, _, rand_features = args[:7]
    nbat, ns = mesh.shape["batch"], mesh.shape["seq"]
    bd, sw = qkv_weight.shape[1], qkv_weight.shape[2]
    rows, width = tokens.shape[1], tokens.shape[2]
    heads, size, feat = rand_features.shape
    return (
        ns == 4
        and nbat == 8
        and tokens.shape[0] == 1
        and bd % 64 == 0
        and sw == 2 * size
        and in_weight.shape[1] == 4 * sw
        and heads == 2 * ns
        and rows == 3 * 512
        and args[10].shape[1] * ns == rows
        and in_weight.shape[1] == width
        and feat == 256
    )


def fused_layer(
    nbat,
    ns,
    tokens,
    qkv_weight,
    out_proj,
    in_weight,
    out_weight,
    norm_params,
    rand_features,
    long_start,
    masked_pos,
    masked_count,
    masked_grad,
):
    nz = nbat // 2
    rows, width = tokens.shape[1], tokens.shape[2]
    slots = masked_grad.shape[1]
    heads, size, feat = rand_features.shape
    bd, sw = qkv_weight.shape[1], qkv_weight.shape[2]
    fw = in_weight.shape[1]
    stack = 2 * size + PAD
    low = lambda *shape: pltpu.VMEM(shape, LOW)
    wide = lambda *shape: pltpu.VMEM(shape, WIDE)
    vmem = pl.BlockSpec(memory_space=pltpu.VMEM)
    smem = pl.BlockSpec(memory_space=pltpu.SMEM)
    anywhere = pl.BlockSpec(memory_space=pl.ANY)
    tall = (nz, 2, bd)
    scratch = [
        low(rows, width),
        low(heads, size, feat),
        low(slots, width),
        low(ns, *tall, 4 * sw),
        low(ns, *tall, fw),
        low(ns, *tall, fw),
        low(ns, nz, 2, PAD, 2 * bd),
        low(ns, 2 * sw, width),
        low(ns, sw, width),
        low(width, width),
        low(width, rows),
        low(ns, 2 * sw, rows),
        low(heads, stack, rows),
        low(heads, feat, rows),
        low(slots, rows),
        wide(slots, 128),
        low(heads, feat, size),
        low(heads, stack, feat),
        low(heads, size + PAD, feat),
        low(ns, 2, size + PAD, feat),
        low(2, 2, 2, size + PAD, feat),
        low(2, 2, 2, size + PAD, feat),
        low(2, ns, 2, size + PAD, feat),
        low(heads, feat, stack),
        low(heads, size, slots),
        low(heads, feat, slots),
        wide(heads, size, slots),
        wide(heads, 8, slots),
        low(heads, stack, slots),
        low(heads, size, rows),
        low(width, slots),
        low(slots, width),
        low(width, slots),
        low(width, slots),
        wide(width, slots),
        low(width, slots),
        low(ns, *tall, 4 * sw),
        low(ns, *tall, fw),
        low(ns, *tall, fw),
        wide(8, width),
        wide(2 + nz, 8, width),
        low(rows, width),
        wide(rows, width),
        pltpu.SemaphoreType.DMA((224,)),
        pltpu.SemaphoreType.DMA((224,)),
        pltpu.SemaphoreType.DMA((11,)),
    ]
    for name, _, lo, hi in scatter_parts(None, None, None, sw, fw // 2):
        scratch += [low(*shape) for shape in scatter_shapes(KIND[name], nz, bd, hi - lo)]
    f32 = lambda *shape: jax.ShapeDtypeStruct(shape, WIDE)
    outs = pl.pallas_call(
        functools.partial(layer_kernel, nz, ns),
        out_shape=(
            jax.ShapeDtypeStruct((rows, width), LOW),
            f32(rows, width),
            f32(3, bd, sw),
            f32(bd, sw),
            f32(bd, fw),
            f32(bd, fw),
            f32(1, bd),
        ),
        in_specs=[anywhere] * 5 + [vmem, anywhere, smem, vmem, smem, anywhere],
        out_specs=(anywhere, anywhere, vmem, vmem, vmem, vmem, vmem),
        scratch_shapes=scratch,
        compiler_params=pltpu.CompilerParams(
            collective_id=0, has_side_effects=True, vmem_limit_bytes=62 * 2**20
        ),
        name="layer",
    )(
        tokens.reshape(rows, width),
        qkv_weight,
        out_proj,
        in_weight,
        out_weight.T,
        norm_params,
        rand_features,
        long_start.reshape(1, 1),
        masked_pos,
        masked_count,
        masked_grad.reshape(slots, width),
    )
    outs = hand_over(outs)
    return (outs[0][None], outs[1][None]) + outs[2:5] + (outs[5].T, outs[6])


def hand_over(arrays):
    parts = 4

    def kernel(*refs):
        for a, o in zip(refs[: len(arrays)], refs[len(arrays) :]):
            o[...] = a[...]

    def spec(a):
        tail = a.shape[1:]
        if a.shape[0] % (parts * 32) == 0:
            return pl.BlockSpec((a.shape[0] // parts,) + tail, lambda i: (i,) + (0,) * len(tail))
        return pl.BlockSpec(a.shape, lambda i: (0,) * (1 + len(tail)))

    return pl.pallas_call(
        kernel,
        grid=(parts,),
        out_shape=tuple(jax.ShapeDtypeStruct(a.shape, a.dtype) for a in arrays),
        in_specs=[spec(a) for a in arrays],
        out_specs=tuple(spec(a) for a in arrays),
        name="hand_over",
    )(*arrays)


def solution(mesh):
    def body(*args):
        if fits(mesh, args):
            return fused_layer(mesh.shape["batch"], mesh.shape["seq"], *args)
        return on_device(*args)

    placed = (
        P("batch", "seq", None),
        P(None, "batch", "seq"),
        P("batch", "seq"),
        P("batch", "seq"),
        P("seq", "batch"),
        P("seq", "batch"),
        P(),
        P("batch"),
        P("batch", "seq"),
        P("batch", "seq"),
        P("batch", "seq", None),
    )
    return jax.shard_map(
        body,
        mesh=mesh,
        in_specs=placed,
        out_specs=(
            P("batch", "seq", None),
            P("batch", "seq", None),
            P(None, "batch", "seq"),
            P("batch", "seq"),
            P("batch", "seq"),
            P("seq", "batch"),
            P("seq", "batch"),
        ),
        check_vma=False,
    )
```
